256 devices in a mesh: tm: 32 (over z, y), chan: 8 (over x, core).
Axes of the slice: x: 4, y: 4, z: 8, core: 2. Of those that a mesh axis runs over, the one named last changes fastest.
Arguments:
- observed_real: float32 [4096, 4096], P(('tm', 'chan')), may hold values from -6 to 6
- observed_imag: float32 [4096, 4096], P(('tm', 'chan')), may hold values from -6 to 6
- weights: float32 [4096, 4096], P(('tm', 'chan')), may hold values from 0.15 to 162
- taps: float32 [16, 8192], replicated, may hold values from -0.5 to 2
Outputs:
- solution: float32 [4096, 8192], P('tm', 'chan')
- residual: float32 [4096, 8192], P('tm', 'chan')
The draws below stay inside these ranges and needn't reach their ends.
All inputs are finite; a program needn't handle non-finite values.
Results may differ from the reference program's by a relative error of at most 0.00019.
Values sent between devices are 32-bit elements; how exact they have to be, the bound alone decides.
No kernel may reach another device: no remote copies, remote signals or barrier semaphores. Data moves between devices by JAX's collectives and lax.ppermute only.
A program may use at most 64 MiB of HBM per device.

```python
import math
import jax
import jax.numpy as jnp

CH = 4096
TAPS = 16
ITERS = 2
FRAMES = 4096


def draw_taps(key, part):
    key = jax.random.fold_in(key, 7)
    frame_len = 2 * CH
    spots = jnp.arange(TAPS * frame_len, dtype=jnp.float32).reshape(TAPS, frame_len)
    centred = (spots + 0.5 - 0.5 * TAPS * frame_len) / frame_len
    window = 0.5 - 0.5 * jnp.cos(2.0 * math.pi * (spots + 0.5) / (TAPS * frame_len))
    factor = jnp.exp(jax.random.uniform(key, (TAPS, frame_len), jnp.float32, -0.69, 0.69))
    return jnp.sinc(centred) * window * factor


def draw_weights(key, part):
    key = jax.random.fold_in(key, 13)
    cell_key, chan_key, frame_key = jax.random.split(key, 3)
    position = jnp.arange(FRAMES, dtype=jnp.float32)[:, None] / (FRAMES - 1)
    chan_scale = jnp.exp(jax.random.uniform(chan_key, (1, CH), jnp.float32, math.log(0.3), math.log(3.0)))
    frame_scale = jnp.exp(jax.random.uniform(frame_key, (FRAMES, 1), jnp.float32, 0.0, math.log(3.0)))
    cells = jnp.exp(jax.random.uniform(cell_key, (FRAMES, CH), jnp.float32, math.log(0.5), math.log(2.0)))
    rising = 1.0 + 2.0 * position
    return cells * chan_scale * frame_scale * rising


def level_of(key, dims, cuts, smallest, high):
    def one(axis_at, parts):
        draws = jax.random.uniform(jax.random.fold_in(jax.random.fold_in(key, 6), axis_at), (parts,), jnp.float32, smallest / len(cuts), high / len(cuts))
        return jnp.repeat(jnp.exp(draws), dims[axis_at] // parts).reshape((-1,) + (1,) * (len(dims) - axis_at - 1))

    factor_of = one(*cuts[0])
    for cut in cuts[1:]:
        factor_of = factor_of * one(*cut)
    return factor_of


def bell_draw(stream_key, dims, deviation, most, cuts=(), kind=jnp.bfloat16):
    drawn = jax.random.normal(stream_key, dims, jnp.float32) * deviation
    if len(cuts) > 0:
        drawn = level_of(stream_key, dims, cuts, -0.22, 0.18) * drawn
    return jnp.clip(drawn, min=-most, max=most).astype(kind)


def setup_inputs(seed: int = 0) -> dict:
    keys = jax.random.split(jax.random.key(seed), 5)
    observed_real = bell_draw(keys[0], (FRAMES, CH), 1.0, 6.0, ((0, 256),), jnp.float32)
    observed_imag = bell_draw(keys[1], (FRAMES, CH), 1.0, 6.0, ((0, 256),), jnp.float32)
    weights = draw_weights(jax.random.fold_in(keys[4], 71), 0)
    taps = draw_taps(jax.random.fold_in(keys[4], 71), 0)
    return {"observed_real": observed_real, "observed_imag": observed_imag, "weights": weights, "taps": taps}


RIDGE = 0.25

def pfb_filter(volts, taps):
    reach = taps.shape[0] - 1
    count = volts.shape[0]
    padded = jnp.concatenate([jnp.zeros((reach, volts.shape[1]), volts.dtype), volts], 0)
    total = jnp.zeros_like(volts)
    for tap in range(reach + 1):
        total = total + taps[tap] * padded[reach - tap:reach - tap + count]
    return total

def forward(volts, taps):
    spectrum = jnp.fft.rfft(pfb_filter(volts, taps), axis=1)[:, :CH]
    scale = 1.0 / math.sqrt(CH)
    return (jnp.real(spectrum) * scale, jnp.imag(spectrum) * scale)

def reference(observed_real, observed_imag, weights, taps):
    zeros = jnp.zeros((observed_real.shape[0], 2 * CH), taps.dtype)
    _, pullback = jax.vjp(lambda volts: forward(volts, taps), zeros)

    def operator(volts):
        real_part, imag_part = forward(volts, taps)
        return pullback((weights * real_part, weights * imag_part))[0] + RIDGE * volts
    right_side = pullback((weights * observed_real, weights * observed_imag))[0]
    solution = jnp.zeros_like(right_side)
    residual = right_side
    direction = right_side
    norm_now = jnp.sum(residual * residual)
    for step in range(ITERS):
        image = operator(direction)
        alpha = norm_now / jnp.sum(direction * image)
        solution = solution + alpha * direction
        residual = residual - alpha * image
        norm_next = jnp.sum(residual * residual)
        direction = residual + norm_next / norm_now * direction
        norm_now = norm_next
    return (solution, residual)
```

```python
import functools
import math

import jax
import jax.numpy as jnp
import numpy as np
from jax import lax
from jax.experimental import pallas as pl
from jax.experimental.pallas import tpu as pltpu
from jax.sharding import PartitionSpec as P

RIDGE = 0.25
ROWS = 64
LANES = 128
CHUNK = 4
F32 = jnp.float32
BF16 = jnp.bfloat16
AXES = ("tm", "chan")
VMEM_BYTES = 40 * 1024 * 1024


def params():
    return pltpu.CompilerParams(vmem_limit_bytes=VMEM_BYTES)


def halves(table):
    high = table.astype(np.float32).astype(jnp.bfloat16)
    low = (table - high.astype(np.float64)).astype(np.float32).astype(jnp.bfloat16)
    return high, low


def dft_tables():
    n1 = np.arange(ROWS)
    n2 = np.arange(LANES)
    k1 = np.arange(ROWS)
    k2 = (2 * np.arange(32)[None, :] + np.arange(2)[:, None]).reshape(-1)
    first = 2.0 * np.pi * (n1[:, None] * k1[None, :] % ROWS) / ROWS
    back_rows = np.concatenate([np.cos(first), -np.sin(first)], 1)
    second = 2.0 * np.pi * (k2[:, None] * n2[None, :] % LANES) / LANES
    scale = 1.0 / math.sqrt(ROWS * ROWS)
    cos = (np.cos(second) * scale).reshape(2, 32, LANES)
    sin = (np.sin(second) * scale).reshape(2, 32, LANES)
    from_real = np.concatenate([cos, sin], 2)
    from_imag = np.concatenate([-sin, cos], 2)
    back_lanes = np.stack([from_real, from_imag], 1).reshape(LANES, 2 * LANES)
    rows_high, rows_low = halves(back_rows)
    lanes_high, lanes_low = halves(back_lanes)
    twist = 2.0 * np.pi * k1[:, None] * n2[None, :] / (ROWS * LANES)
    return (
        np.concatenate([rows_high.T, rows_high.T, rows_low.T], 1),
        np.concatenate([lanes_high.T, lanes_high.T, lanes_low.T], 0),
        np.concatenate([lanes_high, lanes_high, lanes_low], 0),
        np.concatenate([rows_high, rows_high, rows_low], 1),
        np.stack([np.cos(twist), np.sin(twist)]).astype(np.float32),
    )


def split(value):
    high = value.astype(BF16)
    low = (value - high.astype(F32)).astype(BF16)
    return high, low


def dot(left, right):
    return jnp.dot(left, right, preferred_element_type=F32)


def forward_chunk(frames, ahead_rows, ahead_lanes, cos, sin):
    high, low = split(jnp.concatenate(frames, 1))
    mixed = dot(ahead_rows, jnp.concatenate([high, low, high], 0))
    turned = []
    for f in range(len(frames)):
        real = mixed[:ROWS, f * LANES : (f + 1) * LANES]
        imag = mixed[ROWS:, f * LANES : (f + 1) * LANES]
        turned.append(jnp.concatenate([real * cos + imag * sin, imag * cos - real * sin], 1))
    high, low = split(jnp.concatenate(turned, 0))
    return dot(jnp.concatenate([high, low, high], 1), ahead_lanes)


def backward_chunk(spectra, back_lanes, back_rows, cos, sin):
    high, low = split(spectra)
    mixed = dot(jnp.concatenate([high, low, high], 1), back_lanes)
    turned = []
    for f in range(spectra.shape[0] // ROWS):
        real = mixed[f * ROWS : (f + 1) * ROWS, :LANES]
        imag = mixed[f * ROWS : (f + 1) * ROWS, LANES:]
        turned.append(jnp.concatenate([real * cos - imag * sin, real * sin + imag * cos], 0))
    high, low = split(jnp.concatenate(turned, 1))
    return dot(back_rows, jnp.concatenate([high, low, high], 0))


def turn_pair(block):
    flipped = block.T
    low_half = flipped[:ROWS]
    high_half = flipped[ROWS:]
    left = lax.broadcasted_iota(jnp.int32, (ROWS, LANES), 1) < ROWS
    return (
        jnp.where(left, low_half, pltpu.roll(high_half, ROWS, 1)),
        jnp.where(left, pltpu.roll(low_half, ROWS, 1), high_half),
    )


def seed_kernel(real_ref, imag_ref, weights_ref, back_lanes_ref, back_rows_ref, twist_ref, out_ref, held):
    count = real_ref.shape[0]
    for j in range(32):
        columns = slice(j * LANES, (j + 1) * LANES)
        weights = weights_ref[:, columns]
        held[pl.ds(j, count, stride=ROWS), :] = weights * real_ref[:, columns]
        held[pl.ds(32 + j, count, stride=ROWS), :] = weights * imag_ref[:, columns]
    cos = twist_ref[0]
    sin = twist_ref[1]
    for start in range(0, count, CHUNK):
        spectra = []
        for f in range(start, start + CHUNK, 2):
            spectra += turn_pair(held[f * ROWS : (f + 2) * ROWS, :])
        frames = backward_chunk(
            jnp.concatenate(spectra, 0), back_lanes_ref[...], back_rows_ref[...], cos, sin
        )
        for f in range(CHUNK):
            out_ref[start + f] = frames[:, f * LANES : (f + 1) * LANES]


def arrange_kernel(weights_ref, taps_ref, weights_out, taps_out, held):
    count = weights_ref.shape[0]
    for j in range(32):
        weights = weights_ref[:, j * LANES : (j + 1) * LANES]
        held[pl.ds(j, count, stride=ROWS), :] = weights
        held[pl.ds(32 + j, count, stride=ROWS), :] = weights
    for f in range(0, count, 2):
        first, second = turn_pair(held[f * ROWS : (f + 2) * ROWS, :])
        weights_out[f] = first
        weights_out[f + 1] = second
    for n1 in range(ROWS):
        taps_out[pl.ds(n1, taps_ref.shape[0], stride=ROWS), :] = taps_ref[
            :, n1 * LANES : (n1 + 1) * LANES
        ]


def weighted_sum(taps, values):
    total = taps[0] * values[0]
    for tap, value in zip(taps[1:], values[1:]):
        total = total + tap * value
    return total


def back_filter(rows, taps, before_ref, here_ref, after_ref, keep):
    reach = len(taps) - 1
    count = here_ref.shape[0]
    frames = [before_ref[t, rows, :] for t in range(count - reach, count)]
    frames += [here_ref[t, rows, :] for t in range(count)]
    frames += [after_ref[t, rows, :] for t in range(reach)]
    result = []
    for at in range(reach + count):
        total = weighted_sum(taps, frames[at : at + reach + 1])
        result.append(total * keep if at < reach else total)
    return result


def ahead_filter(taps, frames):
    reach = len(taps) - 1
    return [
        weighted_sum(taps, [frames[at + reach - tap] for tap in range(reach + 1)])
        for at in range(len(frames) - reach)
    ]


def first_kernel(
    keep_ref, before_ref, here_ref, after_ref, taps_ref, weights_ref,
    ahead_rows_ref, ahead_lanes_ref, back_lanes_ref, back_rows_ref, twist_ref,
    out_ref, side_ref, filtered,
):
    count = here_ref.shape[0]
    keep = keep_ref[0]

    @pl.loop(0, ROWS // 8)
    def _(group):
        rows = pl.ds(pl.multiple_of(group * 8, 8), 8)
        taps = [taps_ref[p, rows, :] for p in range(taps_ref.shape[0])]
        side = back_filter(rows, taps, before_ref, here_ref, after_ref, keep)
        for at, value in enumerate(side):
            side_ref[at, rows, :] = value
        for at, value in enumerate(ahead_filter(taps, side)):
            filtered[at, rows, :] = value

    cos = twist_ref[0]
    sin = twist_ref[1]
    for start in range(0, count, CHUNK):
        spectra = forward_chunk(
            [filtered[start + f] for f in range(CHUNK)], ahead_rows_ref[...], ahead_lanes_ref[...], cos, sin
        )
        weights = weights_ref[start : start + CHUNK].reshape(CHUNK * ROWS, LANES)
        frames = backward_chunk(spectra * weights, back_lanes_ref[...], back_rows_ref[...], cos, sin)
        for f in range(CHUNK):
            out_ref[start + f] = frames[:, f * LANES : (f + 1) * LANES]


def second_kernel(
    keep_ref, before_ref, here_ref, after_ref, side_ref, taps_ref, weights_ref,
    ahead_rows_ref, ahead_lanes_ref, back_lanes_ref, back_rows_ref, twist_ref,
    out_ref, filtered, sums,
):
    count = here_ref.shape[0]
    keep = keep_ref[0]
    reach = taps_ref.shape[0] - 1
    sums[...] = jnp.zeros_like(sums)

    @pl.loop(0, ROWS // 8)
    def _(group):
        rows = pl.ds(pl.multiple_of(group * 8, 8), 8)
        taps = [taps_ref[p, rows, :] for p in range(reach + 1)]
        image = back_filter(rows, taps, before_ref, here_ref, after_ref, keep)
        side = [side_ref[at, rows, :] for at in range(reach + count)]
        image = [value + RIDGE * base for value, base in zip(image, side)]
        for at, value in enumerate(ahead_filter(taps, image)):
            filtered[at, rows, :] = value
        zero = sums[0]
        first, second, third = zero, sums[1], sums[2]
        for at in range(count):
            base = side[reach + at]
            value = image[reach + at]
            out_ref[group, at] = base
            out_ref[group, count + at] = value
            first = first + base * base
            second = second + base * value
            third = third + value * value
        sums[0] = first
        sums[1] = second
        sums[2] = third

    cos = twist_ref[0]
    sin = twist_ref[1]
    power = jnp.zeros((8, LANES), F32)
    for start in range(0, count, CHUNK):
        spectra = forward_chunk(
            [filtered[start + f] for f in range(CHUNK)], ahead_rows_ref[...], ahead_lanes_ref[...], cos, sin
        )
        weights = weights_ref[start : start + CHUNK].reshape(CHUNK * ROWS, LANES)
        weighted = spectra * weights
        power = power + jnp.sum((weighted * spectra).reshape(CHUNK * ROWS // 8, 8, LANES), 0)
        frames = backward_chunk(weighted, back_lanes_ref[...], back_rows_ref[...], cos, sin)
        for f in range(CHUNK):
            for group in range(ROWS // 8):
                out_ref[group, 2 * count + start + f] = frames[
                    group * 8 : (group + 1) * 8, f * LANES : (f + 1) * LANES
                ]
    totals = [jnp.sum(value, 0, keepdims=True) for value in (sums[0], sums[1], sums[2], power)]
    totals.append(jnp.zeros((4, LANES), F32))
    totals = jnp.concatenate(totals, 0)
    for group in range(ROWS // 8):
        out_ref[group, 3 * count] = totals


def last_kernel(place_ref, moved_ref, after_ref, sums_ref, taps_ref, solution_ref, residual_ref, kept, left):
    parts, slots = moved_ref.shape[:2]
    count = (slots - 1) // 3
    reach = taps_ref.shape[0] - 1
    rows = pl.ds(pl.multiple_of(place_ref[0] * 8, 8), 8)
    sums = sums_ref[0]
    for at in range(1, sums_ref.shape[0]):
        sums = sums + sums_ref[at]
    sums = jnp.sum(sums, 1, keepdims=True)
    norm, curve, square, power = (sums[at : at + 1] for at in range(4))
    cube = power + RIDGE * square
    step = norm / curve
    next_norm = step * step * square - norm
    grown = step * square / curve
    next_step = next_norm / (step * (step * cube - grown * square))
    to_base = step + next_step * grown
    to_image = -(next_step * step)
    image_rate = -(step + next_step * grown)
    cube_rate = next_step * step
    to_base, to_image, image_rate, cube_rate = (
        jnp.broadcast_to(value, (8, LANES)) for value in (to_base, to_image, image_rate, cube_rate)
    )
    taps = [taps_ref[p, rows, :] for p in range(reach + 1)]

    def finish(part, tail):
        frames = [moved_ref[part, 2 * count + t] for t in range(count)] + tail
        for at in range(count):
            base = moved_ref[part, at]
            image = moved_ref[part, count + at]
            again = weighted_sum(taps, frames[at : at + reach + 1]) + RIDGE * image
            here = pl.ds(pl.multiple_of((part * count + at) * 8, 8), 8)
            kept[here, :] = to_base * base + to_image * image
            left[here, :] = base + image_rate * image + cube_rate * again

    @pl.loop(0, parts - 1)
    def _(part):
        finish(part, [moved_ref[part + 1, 2 * count + t] for t in range(reach)])

    finish(parts - 1, [after_ref[t] for t in range(reach)])

    for block in range(parts * count // 8):
        for n1 in range(8):
            places = pl.ds(block * 64 + n1, 8, stride=8)
            columns = slice(n1 * LANES, (n1 + 1) * LANES)
            solution_ref[block * 8 : (block + 1) * 8, columns] = kept[places, :]
            residual_ref[block * 8 : (block + 1) * 8, columns] = left[places, :]


def shape(*dims):
    return jax.ShapeDtypeStruct(dims, F32)


def vmem(number):
    return [pl.BlockSpec(memory_space=pltpu.VMEM)] * number


SMEM = pl.BlockSpec(memory_space=pltpu.SMEM)


def local(observed_real, observed_imag, weights, taps):
    ahead_rows, ahead_lanes, back_lanes, back_rows, twist = dft_tables()
    count = weights.shape[0]
    reach = taps.shape[0] - 1
    parts = lax.axis_size("chan")
    devices = lax.axis_size("tm") * parts
    blocks = shape(count, ROWS, LANES)
    position = lax.axis_index(AXES)
    keep = (position > 0).astype(F32).reshape(1)
    place = lax.axis_index("chan").astype(jnp.int32).reshape(1)
    tables = (ahead_rows, ahead_lanes, back_lanes, back_rows, twist)

    def neighbours(block):
        later = [(i, i + 1) for i in range(devices - 1)]
        earlier = [(i + 1, i) for i in range(devices - 1)]
        return lax.ppermute(block, AXES, later), lax.ppermute(block, AXES, earlier)

    seeds = pl.pallas_call(
        seed_kernel,
        out_shape=blocks,
        in_specs=vmem(6),
        out_specs=vmem(1)[0],
        scratch_shapes=[pltpu.VMEM((count * ROWS, LANES), F32)],
        compiler_params=params(),
        name="seed",
    )(observed_real, observed_imag, weights, back_lanes, back_rows, twist)
    before, after = neighbours(seeds)
    weights, taps = pl.pallas_call(
        arrange_kernel,
        out_shape=(blocks, shape((reach + 1) * ROWS, LANES)),
        in_specs=vmem(2),
        out_specs=tuple(vmem(2)),
        scratch_shapes=[pltpu.VMEM((count * ROWS, LANES), F32)],
        compiler_params=params(),
        cost_estimate=pl.CostEstimate(flops=10**7, bytes_accessed=2 * 10**6, transcendentals=0),
        name="arrange",
    )(weights, taps)
    taps = taps.reshape(reach + 1, ROWS, LANES)

    images, side = pl.pallas_call(
        first_kernel,
        out_shape=(blocks, shape(reach + count, ROWS, LANES)),
        in_specs=[SMEM] + vmem(10),
        out_specs=tuple(vmem(2)),
        scratch_shapes=[pltpu.VMEM((count, ROWS, LANES), F32)],
        compiler_params=params(),
        name="first",
    )(keep, before, seeds, after, taps, weights, *tables)
    before, after = neighbours(images)

    outgoing = pl.pallas_call(
        second_kernel,
        out_shape=shape(parts, 3 * count + 1, 8, LANES),
        in_specs=[SMEM] + vmem(11),
        out_specs=vmem(1)[0],
        scratch_shapes=[
            pltpu.VMEM((count, ROWS, LANES), F32),
            pltpu.VMEM((3, 8, LANES), F32),
        ],
        compiler_params=params(),
        name="second",
    )(keep, before, images, after, side, taps, weights, *tables)

    moved = lax.all_to_all(outgoing, "chan", split_axis=0, concat_axis=0, tiled=True)
    groups = lax.axis_size("tm")
    after = lax.ppermute(
        moved[0, 2 * count : 3 * count], "tm", [(i + 1, i) for i in range(groups - 1)]
    )
    sums = jnp.sum(moved[:, 3 * count], 0)
    sums = lax.all_to_all(
        jnp.broadcast_to(sums, (groups, 8, LANES)), "tm", split_axis=0, concat_axis=0, tiled=True
    )
    return pl.pallas_call(
        last_kernel,
        out_shape=(shape(parts * count, 8 * LANES), shape(parts * count, 8 * LANES)),
        in_specs=[SMEM] + vmem(4),
        out_specs=tuple(vmem(2)),
        scratch_shapes=[
            pltpu.VMEM((parts * count * 8, LANES), F32),
            pltpu.VMEM((parts * count * 8, LANES), F32),
        ],
        compiler_params=params(),
        name="last",
    )(place, moved, after, sums, taps)


def solution(mesh):
    placed = (P(AXES, None), P(AXES, None), P(AXES, None), P())
    return jax.shard_map(
        local,
        mesh=mesh,
        in_specs=placed,
        out_specs=(P("tm", "chan"), P("tm", "chan")),
        check_vma=False,
    )
```

```python
import functools
import math

import jax
import jax.numpy as jnp
import numpy as np
from jax import lax
from jax.experimental import pallas as pl
from jax.experimental.pallas import tpu as pltpu
from jax.sharding import PartitionSpec as P

RIDGE = 0.25
ROWS = 64
LANES = 128
CHUNK = 4
F32 = jnp.float32
BF16 = jnp.bfloat16
AXES = ("tm", "chan")
VMEM_BYTES = 40 * 1024 * 1024


def params(limit=VMEM_BYTES):
    return pltpu.CompilerParams(vmem_limit_bytes=limit)


def halves(table):
    high = table.astype(np.float32).astype(jnp.bfloat16)
    low = (table - high.astype(np.float64)).astype(np.float32).astype(jnp.bfloat16)
    return high, low


def dft_tables():
    n1 = np.arange(ROWS)
    n2 = np.arange(LANES)
    k1 = np.arange(ROWS)
    k2 = (2 * np.arange(32)[None, :] + np.arange(2)[:, None]).reshape(-1)
    first = 2.0 * np.pi * (n1[:, None] * k1[None, :] % ROWS) / ROWS
    back_rows = np.concatenate([np.cos(first), -np.sin(first)], 1)
    second = 2.0 * np.pi * (k2[:, None] * n2[None, :] % LANES) / LANES
    scale = 1.0 / math.sqrt(ROWS * ROWS)
    cos = (np.cos(second) * scale).reshape(2, 32, LANES)
    sin = (np.sin(second) * scale).reshape(2, 32, LANES)
    from_real = np.concatenate([cos, sin], 2)
    from_imag = np.concatenate([-sin, cos], 2)
    back_lanes = np.stack([from_real, from_imag], 1).reshape(LANES, 2 * LANES)
    rows_high, rows_low = halves(back_rows)
    lanes_high, lanes_low = halves(back_lanes)
    twist = 2.0 * np.pi * k1[:, None] * n2[None, :] / (ROWS * LANES)
    return (
        np.concatenate([rows_high.T, rows_high.T, rows_low.T], 1),
        np.concatenate([lanes_high.T, lanes_high.T, lanes_low.T], 0),
        np.concatenate([lanes_high, lanes_high, lanes_low], 0),
        np.concatenate([rows_high, rows_high, rows_low], 1),
        np.stack([np.cos(twist), np.sin(twist)]).astype(np.float32),
    )


def split(value):
    high = value.astype(BF16)
    low = (value - high.astype(F32)).astype(BF16)
    return high, low


def dot(left, right):
    return jnp.dot(left, right, preferred_element_type=F32)


def forward_chunk(frames, ahead_rows, ahead_lanes, cos, sin):
    high, low = split(jnp.concatenate(frames, 1))
    mixed = dot(ahead_rows, jnp.concatenate([high, low, high], 0))
    turned = []
    for f in range(len(frames)):
        real = mixed[:ROWS, f * LANES : (f + 1) * LANES]
        imag = mixed[ROWS:, f * LANES : (f + 1) * LANES]
        turned.append(jnp.concatenate([real * cos + imag * sin, imag * cos - real * sin], 1))
    high, low = split(jnp.concatenate(turned, 0))
    return dot(jnp.concatenate([high, low, high], 1), ahead_lanes)


def backward_chunk(spectra, back_lanes, back_rows, cos, sin):
    high, low = split(spectra)
    mixed = dot(jnp.concatenate([high, low, high], 1), back_lanes)
    turned = []
    for f in range(spectra.shape[0] // ROWS):
        real = mixed[f * ROWS : (f + 1) * ROWS, :LANES]
        imag = mixed[f * ROWS : (f + 1) * ROWS, LANES:]
        turned.append(jnp.concatenate([real * cos - imag * sin, real * sin + imag * cos], 0))
    high, low = split(jnp.concatenate(turned, 1))
    return dot(back_rows, jnp.concatenate([high, low, high], 0))


def turn_pair(block):
    flipped = block.T
    low_half = flipped[:ROWS]
    high_half = flipped[ROWS:]
    left = lax.broadcasted_iota(jnp.int32, (ROWS, LANES), 1) < ROWS
    return (
        jnp.where(left, low_half, pltpu.roll(high_half, ROWS, 1)),
        jnp.where(left, pltpu.roll(low_half, ROWS, 1), high_half),
    )


def seed_kernel(*refs):
    sources, out_ref, places, held, semaphore = refs[:6], refs[6], refs[7:13], refs[13], refs[14]
    copies = [
        pltpu.make_async_copy(source, place, semaphore.at[at])
        for at, (source, place) in enumerate(zip(sources, places))
    ]
    for copy in copies:
        copy.start()
    real_ref, imag_ref, weights_ref, back_lanes_ref, back_rows_ref, twist_ref = places
    count = real_ref.shape[0]
    for copy in copies:
        copy.wait()
    for j in range(32):
        columns = slice(j * LANES, (j + 1) * LANES)
        weights = weights_ref[:, columns]
        held[pl.ds(j, count, stride=ROWS), :] = weights * real_ref[:, columns]
        held[pl.ds(32 + j, count, stride=ROWS), :] = weights * imag_ref[:, columns]
    cos = twist_ref[0]
    sin = twist_ref[1]
    for start in range(0, count, CHUNK):
        spectra = []
        for f in range(start, start + CHUNK, 2):
            spectra += turn_pair(held[f * ROWS : (f + 2) * ROWS, :])
        frames = backward_chunk(
            jnp.concatenate(spectra, 0), back_lanes_ref[...], back_rows_ref[...], cos, sin
        )
        for f in range(CHUNK):
            out_ref[start + f] = frames[:, f * LANES : (f + 1) * LANES]


def arrange_kernel(weights_ref, taps_ref, weights_out, taps_out, held):
    count = weights_ref.shape[0]
    for j in range(32):
        weights = weights_ref[:, j * LANES : (j + 1) * LANES]
        held[pl.ds(j, count, stride=ROWS), :] = weights
        held[pl.ds(32 + j, count, stride=ROWS), :] = weights
    for f in range(0, count, 2):
        first, second = turn_pair(held[f * ROWS : (f + 2) * ROWS, :])
        weights_out[f] = first
        weights_out[f + 1] = second
    for n1 in range(ROWS):
        taps_out[pl.ds(n1, taps_ref.shape[0], stride=ROWS), :] = taps_ref[
            :, n1 * LANES : (n1 + 1) * LANES
        ]


def weighted_sum(taps, values):
    total = taps[0] * values[0]
    for tap, value in zip(taps[1:], values[1:]):
        total = total + tap * value
    return total


def back_filter(rows, taps, before_ref, here_ref, after_ref, keep):
    reach = len(taps) - 1
    count = here_ref.shape[0]
    frames = [before_ref[t, rows, :] for t in range(count - reach, count)]
    frames += [here_ref[t, rows, :] for t in range(count)]
    frames += [after_ref[t, rows, :] * keep[1] for t in range(reach)]
    result = []
    for at in range(reach + count):
        total = weighted_sum(taps, frames[at : at + reach + 1])
        result.append(total * keep[0] if at < reach else total)
    return result


def ahead_filter(taps, frames):
    reach = len(taps) - 1
    return [
        weighted_sum(taps, [frames[at + reach - tap] for tap in range(reach + 1)])
        for at in range(len(frames) - reach)
    ]


def first_kernel(
    keep_ref, before_ref, here_ref, after_ref, taps_ref, weights_ref,
    ahead_rows_ref, ahead_lanes_ref, back_lanes_ref, back_rows_ref, twist_ref,
    out_ref, side_ref, filtered,
):
    count = here_ref.shape[0]
    keep = (keep_ref[0], keep_ref[1])

    @pl.loop(0, ROWS // 8)
    def _(group):
        rows = pl.ds(pl.multiple_of(group * 8, 8), 8)
        taps = [taps_ref[p, rows, :] for p in range(taps_ref.shape[0])]
        side = back_filter(rows, taps, before_ref, here_ref, after_ref, keep)
        for at, value in enumerate(side):
            side_ref[at, rows, :] = value
        for at, value in enumerate(ahead_filter(taps, side)):
            filtered[at, rows, :] = value

    cos = twist_ref[0]
    sin = twist_ref[1]
    for start in range(0, count, CHUNK):
        spectra = forward_chunk(
            [filtered[start + f] for f in range(CHUNK)], ahead_rows_ref[...], ahead_lanes_ref[...], cos, sin
        )
        weights = weights_ref[start : start + CHUNK].reshape(CHUNK * ROWS, LANES)
        frames = backward_chunk(spectra * weights, back_lanes_ref[...], back_rows_ref[...], cos, sin)
        for f in range(CHUNK):
            out_ref[start + f] = frames[:, f * LANES : (f + 1) * LANES]


def quarters():
    return lax.broadcasted_iota(jnp.int32, (8, LANES), 1) // 32


def pack(values):
    packed = jnp.zeros((8, LANES), F32)
    for at, value in enumerate(values):
        value = value + pltpu.roll(value, 64, 1)
        value = value + pltpu.roll(value, 32, 1)
        packed = jnp.where(quarters() == at, value, packed)
    return packed


def second_kernel(
    keep_ref, before_ref, here_ref, after_ref, side_ref, taps_ref, weights_ref,
    ahead_rows_ref, ahead_lanes_ref, back_lanes_ref, back_rows_ref, twist_ref,
    out_ref, filtered, sums,
):
    count = here_ref.shape[0]
    keep = (keep_ref[0], keep_ref[1])
    reach = taps_ref.shape[0] - 1
    sums[...] = jnp.zeros_like(sums)

    @pl.loop(0, ROWS // 8)
    def _(group):
        rows = pl.ds(pl.multiple_of(group * 8, 8), 8)
        taps = [taps_ref[p, rows, :] for p in range(reach + 1)]
        image = back_filter(rows, taps, before_ref, here_ref, after_ref, keep)
        side = [side_ref[at, rows, :] for at in range(reach + count)]
        image = [value + RIDGE * base for value, base in zip(image, side)]
        for at, value in enumerate(ahead_filter(taps, image)):
            filtered[at, rows, :] = value
        first, second, third = sums[0], sums[1], sums[2]
        for at in range(count):
            base = side[reach + at]
            value = image[reach + at]
            out_ref[group, at] = base
            out_ref[group, count + at] = value
            first = first + base * base
            second = second + base * value
            third = third + value * value
        sums[0] = first
        sums[1] = second
        sums[2] = third

    cos = twist_ref[0]
    sin = twist_ref[1]
    power = jnp.zeros((8, LANES), F32)
    for start in range(0, count, CHUNK):
        spectra = forward_chunk(
            [filtered[start + f] for f in range(CHUNK)], ahead_rows_ref[...], ahead_lanes_ref[...], cos, sin
        )
        weights = weights_ref[start : start + CHUNK].reshape(CHUNK * ROWS, LANES)
        weighted = spectra * weights
        power = power + jnp.sum((weighted * spectra).reshape(CHUNK * ROWS // 8, 8, LANES), 0)
        frames = backward_chunk(weighted, back_lanes_ref[...], back_rows_ref[...], cos, sin)
        for f in range(CHUNK):
            for group in range(ROWS // 8):
                out_ref[group, 2 * count + start + f] = frames[
                    group * 8 : (group + 1) * 8, f * LANES : (f + 1) * LANES
                ]
    totals = pack([sums[0], sums[1], sums[2], power])
    for group in range(ROWS // 8):
        out_ref[group, 3 * count] = totals


def last_kernel(
    place_ref, keep_ref, moved_ref, after_ref, sums_ref, taps_ref,
    solution_ref, residual_ref, kept, left,
):
    parts = moved_ref.shape[0]
    count = (moved_ref.shape[1] - 1) // 3
    reach = taps_ref.shape[0] - 1
    rows = pl.ds(pl.multiple_of(place_ref[0] * 8, 8), 8)
    sums = sums_ref[0:8]
    for at in range(8, sums_ref.shape[0], 8):
        sums = sums + sums_ref[at : at + 8]
    norm, curve, square, power = (
        jnp.sum(jnp.sum(jnp.where(quarters() == at, sums, 0.0), 1, keepdims=True), 0, keepdims=True)
        for at in range(4)
    )
    cube = power + RIDGE * square
    step = norm / curve
    next_norm = step * step * square - norm
    grown = step * square / curve
    next_step = next_norm / (step * (step * cube - grown * square))
    to_base = step + next_step * grown
    to_image = -(next_step * step)
    image_rate = -(step + next_step * grown)
    cube_rate = next_step * step
    to_base, to_image, image_rate, cube_rate = (
        jnp.broadcast_to(value, (8, LANES)) for value in (to_base, to_image, image_rate, cube_rate)
    )
    taps = [taps_ref[p, rows, :] for p in range(reach + 1)]

    def finish(part, tail):
        frames = [moved_ref[part, 2 * count + t] for t in range(count)] + tail
        for at in range(count):
            base = moved_ref[part, at]
            image = moved_ref[part, count + at]
            again = weighted_sum(taps, frames[at : at + reach + 1]) + RIDGE * image
            here = pl.ds(pl.multiple_of((part * count + at) * 8, 8), 8)
            kept[here, :] = to_base * base + to_image * image
            left[here, :] = base + image_rate * image + cube_rate * again

    @pl.loop(0, parts - 1)
    def _(part):
        finish(part, [moved_ref[part + 1, 2 * count + t] for t in range(reach)])

    finish(parts - 1, [after_ref[t] * keep_ref[0] for t in range(reach)])

    for block in range(parts * count // 8):
        for n1 in range(8):
            places = pl.ds(block * 64 + n1, 8, stride=8)
            columns = slice(n1 * LANES, (n1 + 1) * LANES)
            solution_ref[block * 8 : (block + 1) * 8, columns] = kept[places, :]
            residual_ref[block * 8 : (block + 1) * 8, columns] = left[places, :]


def shape(*dims):
    return jax.ShapeDtypeStruct(dims, F32)


def vmem(number):
    return [pl.BlockSpec(memory_space=pltpu.VMEM)] * number


SMEM = pl.BlockSpec(memory_space=pltpu.SMEM)


def local(observed_real, observed_imag, weights, taps):
    ahead_rows, ahead_lanes, back_lanes, back_rows, twist = dft_tables()
    count = weights.shape[0]
    reach = taps.shape[0] - 1
    parts = lax.axis_size("chan")
    devices = lax.axis_size("tm") * parts
    blocks = shape(count, ROWS, LANES)
    groups = lax.axis_size("tm")
    position = lax.axis_index(AXES)
    keep = jnp.stack([position > 0, position < devices - 1]).astype(F32)
    place = lax.axis_index("chan").astype(jnp.int32).reshape(1)
    keep_group = (lax.axis_index("tm") < groups - 1).astype(F32).reshape(1)
    tables = (ahead_rows, ahead_lanes, back_lanes, back_rows, twist)

    def neighbours(block):
        later = [(i, (i + 1) % devices) for i in range(devices)]
        earlier = [((i + 1) % devices, i) for i in range(devices)]
        return lax.ppermute(block, AXES, later), lax.ppermute(block, AXES, earlier)

    def exchange(value, axis):
        return lax.all_to_all(value, axis, split_axis=0, concat_axis=0, tiled=True)

    seed_inputs = (observed_real, observed_imag, weights, back_lanes, back_rows, twist)
    seeds = pl.pallas_call(
        seed_kernel,
        out_shape=blocks,
        in_specs=[pl.BlockSpec(memory_space=pltpu.HBM)] * 6,
        out_specs=vmem(1)[0],
        scratch_shapes=[pltpu.VMEM(value.shape, value.dtype) for value in seed_inputs]
        + [pltpu.VMEM((count * ROWS, LANES), F32), pltpu.SemaphoreType.DMA((6,))],
        compiler_params=params(62 * 1024 * 1024),
        name="seed",
    )(*seed_inputs)
    before, after = neighbours(seeds)
    weights, taps = pl.pallas_call(
        arrange_kernel,
        out_shape=(blocks, shape((reach + 1) * ROWS, LANES)),
        in_specs=vmem(2),
        out_specs=tuple(vmem(2)),
        scratch_shapes=[pltpu.VMEM((count * ROWS, LANES), F32)],
        compiler_params=params(),
        cost_estimate=pl.CostEstimate(flops=10**7, bytes_accessed=2 * 10**6, transcendentals=0),
        name="arrange",
    )(weights, taps)
    taps = taps.reshape(reach + 1, ROWS, LANES)

    images, side = pl.pallas_call(
        first_kernel,
        out_shape=(blocks, shape(reach + count, ROWS, LANES)),
        in_specs=[SMEM] + vmem(10),
        out_specs=tuple(vmem(2)),
        scratch_shapes=[pltpu.VMEM((count, ROWS, LANES), F32)],
        compiler_params=params(),
        name="first",
    )(keep, before, seeds, after, taps, weights, *tables)
    before, after = neighbours(images)

    outgoing = pl.pallas_call(
        second_kernel,
        out_shape=shape(parts, 3 * count + 1, 8, LANES),
        in_specs=[SMEM] + vmem(11),
        out_specs=vmem(1)[0],
        scratch_shapes=[
            pltpu.VMEM((count, ROWS, LANES), F32),
            pltpu.VMEM((3, 8, LANES), F32),
        ],
        compiler_params=params(),
        name="second",
    )(keep, before, images, after, side, taps, weights, *tables)

    moved = exchange(outgoing, "chan")
    after = lax.ppermute(
        moved[0, 2 * count : 3 * count], "tm", [((i + 1) % groups, i) for i in range(groups)]
    )
    sums = jnp.sum(moved[:, 3 * count], (0, 1))
    sums = exchange(jnp.broadcast_to(sums, (groups, LANES)), "tm")
    return pl.pallas_call(
        last_kernel,
        out_shape=(shape(parts * count, 8 * LANES), shape(parts * count, 8 * LANES)),
        in_specs=[SMEM, SMEM] + vmem(4),
        out_specs=tuple(vmem(2)),
        scratch_shapes=[
            pltpu.VMEM((parts * count * 8, LANES), F32),
            pltpu.VMEM((parts * count * 8, LANES), F32),
        ],
        compiler_params=params(),
        name="last",
    )(place, keep_group, moved, after, sums, taps)


def solution(mesh):
    placed = (P(AXES, None), P(AXES, None), P(AXES, None), P())
    return jax.shard_map(
        local,
        mesh=mesh,
        in_specs=placed,
        out_specs=(P("tm", "chan"), P("tm", "chan")),
        check_vma=False,
    )
```

```python
import functools
import math

import jax
import jax.numpy as jnp
import numpy as np
from jax import lax
from jax.experimental import pallas as pl
from jax.experimental.pallas import tpu as pltpu
from jax.sharding import PartitionSpec as P

RIDGE = 0.25
ROWS = 64
LANES = 128
CHUNK = 4
F32 = jnp.float32
BF16 = jnp.bfloat16
AXES = ("tm", "chan")
VMEM_BYTES = 40 * 1024 * 1024


def params(limit=VMEM_BYTES):
    return pltpu.CompilerParams(vmem_limit_bytes=limit)


def halves(table):
    high = table.astype(np.float32).astype(jnp.bfloat16)
    low = (table - high.astype(np.float64)).astype(np.float32).astype(jnp.bfloat16)
    return high, low


def dft_tables():
    n1 = np.arange(ROWS)
    n2 = np.arange(LANES)
    k1 = np.arange(ROWS)
    k2 = (2 * np.arange(32)[None, :] + np.arange(2)[:, None]).reshape(-1)
    first = 2.0 * np.pi * (n1[:, None] * k1[None, :] % ROWS) / ROWS
    back_rows = np.concatenate([np.cos(first), -np.sin(first)], 1)
    second = 2.0 * np.pi * (k2[:, None] * n2[None, :] % LANES) / LANES
    scale = 1.0 / math.sqrt(ROWS * ROWS)
    cos = (np.cos(second) * scale).reshape(2, 32, LANES)
    sin = (np.sin(second) * scale).reshape(2, 32, LANES)
    from_real = np.concatenate([cos, sin], 2)
    from_imag = np.concatenate([-sin, cos], 2)
    back_lanes = np.stack([from_real, from_imag], 1).reshape(LANES, 2 * LANES)
    rows_high, rows_low = halves(back_rows)
    lanes_high, lanes_low = halves(back_lanes)
    twist = 2.0 * np.pi * k1[:, None] * n2[None, :] / (ROWS * LANES)
    return (
        np.concatenate([rows_high.T, rows_high.T, rows_low.T], 1),
        np.concatenate([lanes_high.T, lanes_high.T, lanes_low.T], 0),
        np.concatenate([lanes_high, lanes_high, lanes_low], 0),
        np.concatenate([rows_high, rows_high, rows_low], 1),
        np.stack([np.cos(twist), np.sin(twist)]).astype(np.float32),
    )


def split(value):
    high = value.astype(BF16)
    low = (value - high.astype(F32)).astype(BF16)
    return high, low


def dot(left, right):
    return jnp.dot(left, right, preferred_element_type=F32)


def forward_chunk(frames, ahead_rows, ahead_lanes, cos, sin):
    high, low = split(jnp.concatenate(frames, 1))
    mixed = dot(ahead_rows, jnp.concatenate([high, low, high], 0))
    turned = []
    for f in range(len(frames)):
        real = mixed[:ROWS, f * LANES : (f + 1) * LANES]
        imag = mixed[ROWS:, f * LANES : (f + 1) * LANES]
        turned.append(jnp.concatenate([real * cos + imag * sin, imag * cos - real * sin], 1))
    high, low = split(jnp.concatenate(turned, 0))
    return dot(jnp.concatenate([high, low, high], 1), ahead_lanes)


def backward_chunk(spectra, back_lanes, back_rows, cos, sin):
    high, low = split(spectra)
    mixed = dot(jnp.concatenate([high, low, high], 1), back_lanes)
    turned = []
    for f in range(spectra.shape[0] // ROWS):
        real = mixed[f * ROWS : (f + 1) * ROWS, :LANES]
        imag = mixed[f * ROWS : (f + 1) * ROWS, LANES:]
        turned.append(jnp.concatenate([real * cos - imag * sin, real * sin + imag * cos], 0))
    high, low = split(jnp.concatenate(turned, 1))
    return dot(back_rows, jnp.concatenate([high, low, high], 0))


def turn_pair(block):
    flipped = block.T
    low_half = flipped[:ROWS]
    high_half = flipped[ROWS:]
    left = lax.broadcasted_iota(jnp.int32, (ROWS, LANES), 1) < ROWS
    return (
        jnp.where(left, low_half, pltpu.roll(high_half, ROWS, 1)),
        jnp.where(left, pltpu.roll(low_half, ROWS, 1), high_half),
    )


def seed_kernel(*refs):
    sources, out_ref, places, held, semaphore = refs[:6], refs[6], refs[7:13], refs[13], refs[14]
    copies = [
        pltpu.make_async_copy(source, place, semaphore.at[at])
        for at, (source, place) in enumerate(zip(sources, places))
    ]
    for copy in copies:
        copy.start()
    real_ref, imag_ref, weights_ref, back_lanes_ref, back_rows_ref, twist_ref = places
    count = real_ref.shape[0]
    for copy in copies:
        copy.wait()
    for j in range(32):
        columns = slice(j * LANES, (j + 1) * LANES)
        weights = weights_ref[:, columns]
        held[pl.ds(j, count, stride=ROWS), :] = weights * real_ref[:, columns]
        held[pl.ds(32 + j, count, stride=ROWS), :] = weights * imag_ref[:, columns]
    cos = twist_ref[0]
    sin = twist_ref[1]
    for start in range(0, count, CHUNK):
        spectra = []
        for f in range(start, start + CHUNK, 2):
            spectra += turn_pair(held[f * ROWS : (f + 2) * ROWS, :])
        frames = backward_chunk(
            jnp.concatenate(spectra, 0), back_lanes_ref[...], back_rows_ref[...], cos, sin
        )
        for f in range(CHUNK):
            out_ref[start + f] = frames[:, f * LANES : (f + 1) * LANES]


def arrange_kernel(weights_ref, taps_ref, weights_out, taps_out, held):
    count = weights_ref.shape[0]
    for j in range(32):
        weights = weights_ref[:, j * LANES : (j + 1) * LANES]
        held[pl.ds(j, count, stride=ROWS), :] = weights
        held[pl.ds(32 + j, count, stride=ROWS), :] = weights
    for f in range(0, count, 2):
        first, second = turn_pair(held[f * ROWS : (f + 2) * ROWS, :])
        weights_out[f] = first
        weights_out[f + 1] = second
    for n1 in range(ROWS):
        taps_out[pl.ds(n1, taps_ref.shape[0], stride=ROWS), :] = taps_ref[
            :, n1 * LANES : (n1 + 1) * LANES
        ]


def weighted_sum(taps, values):
    total = taps[0] * values[0]
    for tap, value in zip(taps[1:], values[1:]):
        total = total + tap * value
    return total


def back_filter(rows, taps, inside_ref, here_ref, across_ref, keep):
    reach = len(taps) - 1
    count = here_ref.shape[0]
    odd = jnp.full((8, LANES), keep[2]) > 0.5
    frames = [
        jnp.where(odd, inside_ref[t, rows, :], across_ref[t, rows, :]) for t in range(count - reach, count)
    ]
    frames += [here_ref[t, rows, :] for t in range(count)]
    frames += [
        jnp.where(odd, across_ref[t, rows, :], inside_ref[t, rows, :]) * keep[1] for t in range(reach)
    ]
    result = []
    for at in range(reach + count):
        total = weighted_sum(taps, frames[at : at + reach + 1])
        result.append(total * keep[0] if at < reach else total)
    return result


def ahead_filter(taps, frames):
    reach = len(taps) - 1
    return [
        weighted_sum(taps, [frames[at + reach - tap] for tap in range(reach + 1)])
        for at in range(len(frames) - reach)
    ]


def first_kernel(
    keep_ref, inside_ref, here_ref, across_ref, taps_ref, weights_ref,
    ahead_rows_ref, ahead_lanes_ref, back_lanes_ref, back_rows_ref, twist_ref,
    out_ref, side_ref, filtered,
):
    count = here_ref.shape[0]
    keep = (keep_ref[0], keep_ref[1], keep_ref[2])

    @pl.loop(0, ROWS // 8)
    def _(group):
        rows = pl.ds(pl.multiple_of(group * 8, 8), 8)
        taps = [taps_ref[p, rows, :] for p in range(taps_ref.shape[0])]
        side = back_filter(rows, taps, inside_ref, here_ref, across_ref, keep)
        for at, value in enumerate(side):
            side_ref[at, rows, :] = value
        for at, value in enumerate(ahead_filter(taps, side)):
            filtered[at, rows, :] = value

    cos = twist_ref[0]
    sin = twist_ref[1]
    for start in range(0, count, CHUNK):
        spectra = forward_chunk(
            [filtered[start + f] for f in range(CHUNK)], ahead_rows_ref[...], ahead_lanes_ref[...], cos, sin
        )
        weights = weights_ref[start : start + CHUNK].reshape(CHUNK * ROWS, LANES)
        frames = backward_chunk(spectra * weights, back_lanes_ref[...], back_rows_ref[...], cos, sin)
        for f in range(CHUNK):
            out_ref[start + f] = frames[:, f * LANES : (f + 1) * LANES]


def quarters():
    return lax.broadcasted_iota(jnp.int32, (8, LANES), 1) // 32


def pack(values):
    packed = jnp.zeros((8, LANES), F32)
    for at, value in enumerate(values):
        value = value + pltpu.roll(value, 64, 1)
        value = value + pltpu.roll(value, 32, 1)
        packed = jnp.where(quarters() == at, value, packed)
    return packed


def second_kernel(
    keep_ref, inside_ref, here_ref, across_ref, side_ref, taps_ref, weights_ref,
    ahead_rows_ref, ahead_lanes_ref, back_lanes_ref, back_rows_ref, twist_ref,
    out_ref, filtered, sums,
):
    count = here_ref.shape[0]
    keep = (keep_ref[0], keep_ref[1], keep_ref[2])
    reach = taps_ref.shape[0] - 1
    sums[...] = jnp.zeros_like(sums)

    @pl.loop(0, ROWS // 8)
    def _(group):
        rows = pl.ds(pl.multiple_of(group * 8, 8), 8)
        taps = [taps_ref[p, rows, :] for p in range(reach + 1)]
        image = back_filter(rows, taps, inside_ref, here_ref, across_ref, keep)
        side = [side_ref[at, rows, :] for at in range(reach + count)]
        image = [value + RIDGE * base for value, base in zip(image, side)]
        for at, value in enumerate(ahead_filter(taps, image)):
            filtered[at, rows, :] = value
        first, second, third = sums[0], sums[1], sums[2]
        for at in range(count):
            base = side[reach + at]
            value = image[reach + at]
            out_ref[group, at] = base
            out_ref[group, count + at] = value
            first = first + base * base
            second = second + base * value
            third = third + value * value
        sums[0] = first
        sums[1] = second
        sums[2] = third

    cos = twist_ref[0]
    sin = twist_ref[1]
    power = jnp.zeros((8, LANES), F32)
    for start in range(0, count, CHUNK):
        spectra = forward_chunk(
            [filtered[start + f] for f in range(CHUNK)], ahead_rows_ref[...], ahead_lanes_ref[...], cos, sin
        )
        weights = weights_ref[start : start + CHUNK].reshape(CHUNK * ROWS, LANES)
        weighted = spectra * weights
        power = power + jnp.sum((weighted * spectra).reshape(CHUNK * ROWS // 8, 8, LANES), 0)
        frames = backward_chunk(weighted, back_lanes_ref[...], back_rows_ref[...], cos, sin)
        for f in range(CHUNK):
            for group in range(ROWS // 8):
                out_ref[group, 2 * count + start + f] = frames[
                    group * 8 : (group + 1) * 8, f * LANES : (f + 1) * LANES
                ]
    totals = pack([sums[0], sums[1], sums[2], power])
    for group in range(ROWS // 8):
        out_ref[group, 3 * count] = totals


def last_kernel(
    place_ref, keep_ref, moved_ref, after_ref, sums_ref, taps_ref,
    solution_ref, residual_ref, kept, left,
):
    parts = moved_ref.shape[0]
    count = (moved_ref.shape[1] - 1) // 3
    reach = taps_ref.shape[0] - 1
    rows = pl.ds(pl.multiple_of(place_ref[0] * 8, 8), 8)
    sums = sums_ref[0:8]
    for at in range(8, sums_ref.shape[0], 8):
        sums = sums + sums_ref[at : at + 8]
    norm, curve, square, power = (
        jnp.sum(jnp.sum(jnp.where(quarters() == at, sums, 0.0), 1, keepdims=True), 0, keepdims=True)
        for at in range(4)
    )
    cube = power + RIDGE * square
    step = norm / curve
    next_norm = step * step * square - norm
    grown = step * square / curve
    next_step = next_norm / (step * (step * cube - grown * square))
    to_base = step + next_step * grown
    to_image = -(next_step * step)
    image_rate = -(step + next_step * grown)
    cube_rate = next_step * step
    to_base, to_image, image_rate, cube_rate = (
        jnp.broadcast_to(value, (8, LANES)) for value in (to_base, to_image, image_rate, cube_rate)
    )
    taps = [taps_ref[p, rows, :] for p in range(reach + 1)]

    def finish(part, tail):
        frames = [moved_ref[part, 2 * count + t] for t in range(count)] + tail
        for at in range(count):
            base = moved_ref[part, at]
            image = moved_ref[part, count + at]
            again = weighted_sum(taps, frames[at : at + reach + 1]) + RIDGE * image
            here = pl.ds(pl.multiple_of((part * count + at) * 8, 8), 8)
            kept[here, :] = to_base * base + to_image * image
            left[here, :] = base + image_rate * image + cube_rate * again

    @pl.loop(0, parts - 1)
    def _(part):
        finish(part, [moved_ref[part + 1, 2 * count + t] for t in range(reach)])

    finish(parts - 1, [after_ref[t] * keep_ref[0] for t in range(reach)])

    for block in range(parts * count // 8):
        for n1 in range(8):
            places = pl.ds(block * 64 + n1, 8, stride=8)
            columns = slice(n1 * LANES, (n1 + 1) * LANES)
            solution_ref[block * 8 : (block + 1) * 8, columns] = kept[places, :]
            residual_ref[block * 8 : (block + 1) * 8, columns] = left[places, :]


def shape(*dims):
    return jax.ShapeDtypeStruct(dims, F32)


def vmem(number):
    return [pl.BlockSpec(memory_space=pltpu.VMEM)] * number


SMEM = pl.BlockSpec(memory_space=pltpu.SMEM)


def local(observed_real, observed_imag, weights, taps):
    ahead_rows, ahead_lanes, back_lanes, back_rows, twist = dft_tables()
    count = weights.shape[0]
    reach = taps.shape[0] - 1
    parts = lax.axis_size("chan")
    devices = lax.axis_size("tm") * parts
    blocks = shape(count, ROWS, LANES)
    groups = lax.axis_size("tm")
    position = lax.axis_index(AXES)
    keep = jnp.stack([position > 0, position < devices - 1, position % 2 == 1]).astype(F32)
    place = lax.axis_index("chan").astype(jnp.int32).reshape(1)
    keep_group = (lax.axis_index("tm") < groups - 1).astype(F32).reshape(1)
    tables = (ahead_rows, ahead_lanes, back_lanes, back_rows, twist)

    def neighbours(block):
        inside = [(i, i ^ 1) for i in range(devices)]
        across = [(i, min(max(((i + 1) ^ 1) - 1, 0), devices - 1)) for i in range(devices)]
        return lax.ppermute(block, AXES, inside), lax.ppermute(block, AXES, across)

    def exchange(value, axis):
        return lax.all_to_all(value, axis, split_axis=0, concat_axis=0, tiled=True)

    seed_inputs = (observed_real, observed_imag, weights, back_lanes, back_rows, twist)
    seeds = pl.pallas_call(
        seed_kernel,
        out_shape=blocks,
        in_specs=[pl.BlockSpec(memory_space=pltpu.HBM)] * 6,
        out_specs=vmem(1)[0],
        scratch_shapes=[pltpu.VMEM(value.shape, value.dtype) for value in seed_inputs]
        + [pltpu.VMEM((count * ROWS, LANES), F32), pltpu.SemaphoreType.DMA((6,))],
        compiler_params=params(62 * 1024 * 1024),
        name="seed",
    )(*seed_inputs)
    inside, across = neighbours(seeds)
    weights, taps = pl.pallas_call(
        arrange_kernel,
        out_shape=(blocks, shape((reach + 1) * ROWS, LANES)),
        in_specs=vmem(2),
        out_specs=tuple(vmem(2)),
        scratch_shapes=[pltpu.VMEM((count * ROWS, LANES), F32)],
        compiler_params=params(),
        cost_estimate=pl.CostEstimate(flops=10**7, bytes_accessed=2 * 10**6, transcendentals=0),
        name="arrange",
    )(weights, taps)
    taps = taps.reshape(reach + 1, ROWS, LANES)

    images, side = pl.pallas_call(
        first_kernel,
        out_shape=(blocks, shape(reach + count, ROWS, LANES)),
        in_specs=[SMEM] + vmem(10),
        out_specs=tuple(vmem(2)),
        scratch_shapes=[pltpu.VMEM((count, ROWS, LANES), F32)],
        compiler_params=params(),
        name="first",
    )(keep, inside, seeds, across, taps, weights, *tables)
    inside, across = neighbours(images)

    outgoing = pl.pallas_call(
        second_kernel,
        out_shape=shape(parts, 3 * count + 1, 8, LANES),
        in_specs=[SMEM] + vmem(11),
        out_specs=vmem(1)[0],
        scratch_shapes=[
            pltpu.VMEM((count, ROWS, LANES), F32),
            pltpu.VMEM((3, 8, LANES), F32),
        ],
        compiler_params=params(),
        name="second",
    )(keep, inside, images, across, side, taps, weights, *tables)

    moved = exchange(outgoing, "chan")
    after = lax.ppermute(
        moved[0, 2 * count : 3 * count], "tm", [((i + 1) % groups, i) for i in range(groups)]
    )
    sums = jnp.sum(moved[:, 3 * count], (0, 1))
    sums = exchange(jnp.broadcast_to(sums, (groups, LANES)), "tm")
    return pl.pallas_call(
        last_kernel,
        out_shape=(shape(parts * count, 8 * LANES), shape(parts * count, 8 * LANES)),
        in_specs=[SMEM, SMEM] + vmem(4),
        out_specs=tuple(vmem(2)),
        scratch_shapes=[
            pltpu.VMEM((parts * count * 8, LANES), F32),
            pltpu.VMEM((parts * count * 8, LANES), F32),
        ],
        compiler_params=params(),
        name="last",
    )(place, keep_group, moved, after, sums, taps)


def solution(mesh):
    placed = (P(AXES, None), P(AXES, None), P(AXES, None), P())
    return jax.shard_map(
        local,
        mesh=mesh,
        in_specs=placed,
        out_specs=(P("tm", "chan"), P("tm", "chan")),
        check_vma=False,
    )
```

```python
import functools
import math

import jax
import jax.numpy as jnp
import numpy as np
from jax import lax
from jax.experimental import pallas as pl
from jax.experimental.pallas import tpu as pltpu
from jax.sharding import PartitionSpec as P

RIDGE = 0.25
ROWS = 64
LANES = 128
CHUNK = 4
F32 = jnp.float32
BF16 = jnp.bfloat16
AXES = ("tm", "chan")
VMEM_BYTES = 16 * 1024 * 1024


def params(limit=VMEM_BYTES):
    return pltpu.CompilerParams(vmem_limit_bytes=limit)


def halves(table):
    high = table.astype(np.float32).astype(jnp.bfloat16)
    low = (table - high.astype(np.float64)).astype(np.float32).astype(jnp.bfloat16)
    return high, low


def dft_tables():
    n1 = np.arange(ROWS)
    n2 = np.arange(LANES)
    k1 = np.arange(ROWS)
    k2 = (2 * np.arange(32)[None, :] + np.arange(2)[:, None]).reshape(-1)
    first = 2.0 * np.pi * (n1[:, None] * k1[None, :] % ROWS) / ROWS
    back_rows = np.concatenate([np.cos(first), -np.sin(first)], 1)
    second = 2.0 * np.pi * (k2[:, None] * n2[None, :] % LANES) / LANES
    scale = 1.0 / math.sqrt(ROWS * ROWS)
    cos = (np.cos(second) * scale).reshape(2, 32, LANES)
    sin = (np.sin(second) * scale).reshape(2, 32, LANES)
    from_real = np.concatenate([cos, sin], 2)
    from_imag = np.concatenate([-sin, cos], 2)
    back_lanes = np.stack([from_real, from_imag], 1).reshape(LANES, 2 * LANES)
    rows_high, rows_low = halves(back_rows)
    lanes_high, lanes_low = halves(back_lanes)
    twist = 2.0 * np.pi * k1[:, None] * n2[None, :] / (ROWS * LANES)
    return (
        np.concatenate([rows_high.T, rows_high.T, rows_low.T], 1),
        np.concatenate([lanes_high.T, lanes_high.T, lanes_low.T], 0),
        np.concatenate([lanes_high, lanes_high, lanes_low], 0),
        np.concatenate([rows_high, rows_high, rows_low], 1),
        np.stack([np.cos(twist), np.sin(twist)]).astype(np.float32),
    )


def split(value):
    high = value.astype(BF16)
    low = (value - high.astype(F32)).astype(BF16)
    return high, low


def dot(left, right):
    return jnp.dot(left, right, preferred_element_type=F32)


def forward_chunk(frames, ahead_rows, ahead_lanes, cos, sin):
    high, low = split(jnp.concatenate(frames, 1))
    mixed = dot(ahead_rows, jnp.concatenate([high, low, high], 0))
    turned = []
    for f in range(len(frames)):
        real = mixed[:ROWS, f * LANES : (f + 1) * LANES]
        imag = mixed[ROWS:, f * LANES : (f + 1) * LANES]
        turned.append(jnp.concatenate([real * cos + imag * sin, imag * cos - real * sin], 1))
    high, low = split(jnp.concatenate(turned, 0))
    return dot(jnp.concatenate([high, low, high], 1), ahead_lanes)


def backward_chunk(spectra, back_lanes, back_rows, cos, sin):
    high, low = split(spectra)
    mixed = dot(jnp.concatenate([high, low, high], 1), back_lanes)
    turned = []
    for f in range(spectra.shape[0] // ROWS):
        real = mixed[f * ROWS : (f + 1) * ROWS, :LANES]
        imag = mixed[f * ROWS : (f + 1) * ROWS, LANES:]
        turned.append(jnp.concatenate([real * cos - imag * sin, real * sin + imag * cos], 0))
    high, low = split(jnp.concatenate(turned, 1))
    return dot(back_rows, jnp.concatenate([high, low, high], 0))


def turn_pair(block):
    flipped = block.T
    low_half = flipped[:ROWS]
    high_half = flipped[ROWS:]
    left = lax.broadcasted_iota(jnp.int32, (ROWS, LANES), 1) < ROWS
    return (
        jnp.where(left, low_half, pltpu.roll(high_half, ROWS, 1)),
        jnp.where(left, pltpu.roll(low_half, ROWS, 1), high_half),
    )


def seed_kernel(*refs):
    sources, out_ref, sent_ref, places, held, semaphore = refs[:6], refs[6], refs[7], refs[8:14], refs[14], refs[15]
    copies = [
        pltpu.make_async_copy(source, place, semaphore.at[at])
        for at, (source, place) in enumerate(zip(sources, places))
    ]
    for copy in copies:
        copy.start()
    real_ref, imag_ref, weights_ref, back_lanes_ref, back_rows_ref, twist_ref = places
    count = real_ref.shape[0]
    for copy in copies:
        copy.wait()
    for j in range(32):
        columns = slice(j * LANES, (j + 1) * LANES)
        weights = weights_ref[:, columns]
        held[pl.ds(j, count, stride=ROWS), :] = weights * real_ref[:, columns]
        held[pl.ds(32 + j, count, stride=ROWS), :] = weights * imag_ref[:, columns]
    cos = twist_ref[0]
    sin = twist_ref[1]
    for start in range(0, count, CHUNK):
        spectra = []
        for f in range(start, start + CHUNK, 2):
            spectra += turn_pair(held[f * ROWS : (f + 2) * ROWS, :])
        frames = backward_chunk(
            jnp.concatenate(spectra, 0), back_lanes_ref[...], back_rows_ref[...], cos, sin
        )
        for f in range(CHUNK):
            frame = frames[:, f * LANES : (f + 1) * LANES]
            out_ref[start + f] = frame
            for group in range(ROWS // 8):
                sent_ref[group, start + f] = frame[group * 8 : (group + 1) * 8]


def arrange_kernel(weights_ref, taps_ref, weights_out, taps_out, held):
    count = weights_ref.shape[0]
    for j in range(32):
        weights = weights_ref[:, j * LANES : (j + 1) * LANES]
        held[pl.ds(j, count, stride=ROWS), :] = weights
        held[pl.ds(32 + j, count, stride=ROWS), :] = weights
    for f in range(0, count, 2):
        first, second = turn_pair(held[f * ROWS : (f + 2) * ROWS, :])
        weights_out[f] = first
        weights_out[f + 1] = second
    for n1 in range(ROWS):
        taps_out[pl.ds(n1, taps_ref.shape[0], stride=ROWS), :] = taps_ref[
            :, n1 * LANES : (n1 + 1) * LANES
        ]


def weighted_sum(taps, values):
    total = taps[0] * values[0]
    for tap, value in zip(taps[1:], values[1:]):
        total = total + tap * value
    return total


def back_filter(rows, taps, inside_ref, here_ref, across_ref, keep):
    reach = len(taps) - 1
    count = here_ref.shape[0]
    odd = jnp.full((8, LANES), keep[2]) > 0.5
    frames = [
        jnp.where(odd, inside_ref[t, rows, :], across_ref[t, rows, :]) for t in range(count - reach, count)
    ]
    frames += [here_ref[t, rows, :] for t in range(count)]
    frames += [
        jnp.where(odd, across_ref[t, rows, :], inside_ref[t, rows, :]) * keep[1] for t in range(reach)
    ]
    result = []
    for at in range(reach + count):
        total = weighted_sum(taps, frames[at : at + reach + 1])
        result.append(total * keep[0] if at < reach else total)
    return result


def ahead_filter(taps, frames):
    reach = len(taps) - 1
    return [
        weighted_sum(taps, [frames[at + reach - tap] for tap in range(reach + 1)])
        for at in range(len(frames) - reach)
    ]


def first_kernel(
    keep_ref, inside_ref, here_ref, across_ref, taps_ref, weights_ref,
    ahead_rows_ref, ahead_lanes_ref, back_lanes_ref, back_rows_ref, twist_ref,
    out_ref, sent_ref, side_ref, filtered,
):
    count = here_ref.shape[0]
    keep = (keep_ref[0], keep_ref[1], keep_ref[2])

    @pl.loop(0, ROWS // 8)
    def _(group):
        rows = pl.ds(pl.multiple_of(group * 8, 8), 8)
        taps = [taps_ref[p, rows, :] for p in range(taps_ref.shape[0])]
        side = back_filter(rows, taps, inside_ref, here_ref, across_ref, keep)
        for at, value in enumerate(side):
            side_ref[at, rows, :] = value
        for at, value in enumerate(ahead_filter(taps, side)):
            filtered[at, rows, :] = value

    cos = twist_ref[0]
    sin = twist_ref[1]
    for start in range(0, count, CHUNK):
        spectra = forward_chunk(
            [filtered[start + f] for f in range(CHUNK)], ahead_rows_ref[...], ahead_lanes_ref[...], cos, sin
        )
        weights = weights_ref[start : start + CHUNK].reshape(CHUNK * ROWS, LANES)
        frames = backward_chunk(spectra * weights, back_lanes_ref[...], back_rows_ref[...], cos, sin)
        for f in range(CHUNK):
            frame = frames[:, f * LANES : (f + 1) * LANES]
            out_ref[start + f] = frame
            for group in range(ROWS // 8):
                sent_ref[group, start + f] = frame[group * 8 : (group + 1) * 8]


def quarters():
    return lax.broadcasted_iota(jnp.int32, (8, LANES), 1) // 32


def pack(values):
    packed = jnp.zeros((8, LANES), F32)
    for at, value in enumerate(values):
        value = value + pltpu.roll(value, 64, 1)
        value = value + pltpu.roll(value, 32, 1)
        packed = jnp.where(quarters() == at, value, packed)
    return packed


def second_kernel(
    keep_ref, inside_ref, here_ref, across_ref, side_ref, taps_ref, weights_ref,
    ahead_rows_ref, ahead_lanes_ref, back_lanes_ref, back_rows_ref, twist_ref,
    out_ref, filtered, sums,
):
    count = here_ref.shape[0]
    keep = (keep_ref[0], keep_ref[1], keep_ref[2])
    reach = taps_ref.shape[0] - 1
    sums[...] = jnp.zeros_like(sums)

    @pl.loop(0, ROWS // 8)
    def _(group):
        rows = pl.ds(pl.multiple_of(group * 8, 8), 8)
        taps = [taps_ref[p, rows, :] for p in range(reach + 1)]
        image = back_filter(rows, taps, inside_ref, here_ref, across_ref, keep)
        side = [side_ref[at, rows, :] for at in range(reach + count)]
        image = [value + RIDGE * base for value, base in zip(image, side)]
        for at, value in enumerate(ahead_filter(taps, image)):
            filtered[at, rows, :] = value
        first, second, third = sums[0], sums[1], sums[2]
        for at in range(count):
            base = side[reach + at]
            value = image[reach + at]
            first = first + base * base
            second = second + base * value
            third = third + value * value
        sums[0] = first
        sums[1] = second
        sums[2] = third

    cos = twist_ref[0]
    sin = twist_ref[1]
    power = jnp.zeros((8, LANES), F32)
    for start in range(0, count, CHUNK):
        spectra = forward_chunk(
            [filtered[start + f] for f in range(CHUNK)], ahead_rows_ref[...], ahead_lanes_ref[...], cos, sin
        )
        weights = weights_ref[start : start + CHUNK].reshape(CHUNK * ROWS, LANES)
        weighted = spectra * weights
        power = power + jnp.sum((weighted * spectra).reshape(CHUNK * ROWS // 8, 8, LANES), 0)
        frames = backward_chunk(weighted, back_lanes_ref[...], back_rows_ref[...], cos, sin)
        for f in range(CHUNK):
            for group in range(ROWS // 8):
                out_ref[group, start + f] = frames[
                    group * 8 : (group + 1) * 8, f * LANES : (f + 1) * LANES
                ]
    totals = pack([sums[0], sums[1], sums[2], power])
    for group in range(ROWS // 8):
        out_ref[group, count] = totals


def local_taps(place_ref, taps_ref):
    rows = pl.ds(pl.multiple_of(place_ref[0] * 8, 8), 8)
    return [taps_ref[p, rows, :] for p in range(taps_ref.shape[0])]


def by_part(moved_ref, after_ref, keep, count, reach, finish):
    parts = moved_ref.shape[0]

    def frames(part):
        return [moved_ref[part, t] for t in range(count)]

    @pl.loop(0, parts - 1)
    def _(part):
        finish(part, frames(part) + [moved_ref[part + 1, t] for t in range(reach)])

    finish(parts - 1, frames(parts - 1) + [after_ref[t] * keep for t in range(reach)])


def rebuild_kernel(
    place_ref, keep_ref, first_ref, first_after_ref, second_ref, second_after_ref, taps_ref, base_ref, image_ref
):
    count = first_ref.shape[1]
    taps = local_taps(place_ref, taps_ref)
    reach = len(taps) - 1

    def base(part, frames):
        for at in range(count):
            base_ref[part, at] = weighted_sum(taps, frames[at : at + reach + 1])

    def image(part, frames):
        for at in range(count):
            image_ref[part, at] = (
                weighted_sum(taps, frames[at : at + reach + 1]) + RIDGE * base_ref[part, at]
            )

    by_part(first_ref, first_after_ref, keep_ref[0], count, reach, base)
    by_part(second_ref, second_after_ref, keep_ref[0], count, reach, image)


def last_kernel(
    place_ref, keep_ref, base_ref, image_ref, moved_ref, after_ref, sums_ref, taps_ref,
    solution_ref, residual_ref, kept, left,
):
    parts, count = base_ref.shape[:2]
    taps = local_taps(place_ref, taps_ref)
    reach = len(taps) - 1
    sums = sums_ref[0:8]
    for at in range(8, sums_ref.shape[0], 8):
        sums = sums + sums_ref[at : at + 8]
    norm, curve, square, power = (
        jnp.sum(jnp.sum(jnp.where(quarters() == at, sums, 0.0), 1, keepdims=True), 0, keepdims=True)
        for at in range(4)
    )
    cube = power + RIDGE * square
    step = norm / curve
    next_norm = step * step * square - norm
    grown = step * square / curve
    next_step = next_norm / (step * (step * cube - grown * square))
    to_base = step + next_step * grown
    to_image = -(next_step * step)
    image_rate = -(step + next_step * grown)
    cube_rate = next_step * step
    to_base, to_image, image_rate, cube_rate = (
        jnp.broadcast_to(value, (8, LANES)) for value in (to_base, to_image, image_rate, cube_rate)
    )

    def finish(part, frames):
        for at in range(count):
            base = base_ref[part, at]
            image = image_ref[part, at]
            again = weighted_sum(taps, frames[at : at + reach + 1]) + RIDGE * image
            here = pl.ds(pl.multiple_of((part * count + at) * 8, 8), 8)
            kept[here, :] = to_base * base + to_image * image
            left[here, :] = base + image_rate * image + cube_rate * again

    by_part(moved_ref, after_ref, keep_ref[0], count, reach, finish)

    for block in range(parts * count // 8):
        for n1 in range(8):
            places = pl.ds(block * 64 + n1, 8, stride=8)
            columns = slice(n1 * LANES, (n1 + 1) * LANES)
            solution_ref[block * 8 : (block + 1) * 8, columns] = kept[places, :]
            residual_ref[block * 8 : (block + 1) * 8, columns] = left[places, :]


def shape(*dims):
    return jax.ShapeDtypeStruct(dims, F32)


def vmem(number):
    return [pl.BlockSpec(memory_space=pltpu.VMEM)] * number


SMEM = pl.BlockSpec(memory_space=pltpu.SMEM)


def local(observed_real, observed_imag, weights, taps):
    ahead_rows, ahead_lanes, back_lanes, back_rows, twist = dft_tables()
    count = weights.shape[0]
    reach = taps.shape[0] - 1
    parts = lax.axis_size("chan")
    devices = lax.axis_size("tm") * parts
    blocks = shape(count, ROWS, LANES)
    groups = lax.axis_size("tm")
    position = lax.axis_index(AXES)
    keep = jnp.stack([position > 0, position < devices - 1, position % 2 == 1]).astype(F32)
    place = lax.axis_index("chan").astype(jnp.int32).reshape(1)
    keep_group = (lax.axis_index("tm") < groups - 1).astype(F32).reshape(1)
    tables = (ahead_rows, ahead_lanes, back_lanes, back_rows, twist)

    def neighbours(block):
        inside = [(i, i ^ 1) for i in range(devices)]
        across = [(i, min(max(((i + 1) ^ 1) - 1, 0), devices - 1)) for i in range(devices)]
        return lax.ppermute(block, AXES, inside), lax.ppermute(block, AXES, across)

    def exchange(value, axis):
        return lax.all_to_all(value, axis, split_axis=0, concat_axis=0, tiled=True)

    def from_later_group(moved):
        return lax.ppermute(moved[0, :count], "tm", [((i + 1) % groups, i) for i in range(groups)])

    seed_inputs = (observed_real, observed_imag, weights, back_lanes, back_rows, twist)
    sent = shape(parts, count, 8, LANES)
    seeds, outgoing = pl.pallas_call(
        seed_kernel,
        out_shape=(blocks, sent),
        in_specs=[pl.BlockSpec(memory_space=pltpu.HBM)] * 6,
        out_specs=tuple(vmem(2)),
        scratch_shapes=[pltpu.VMEM(value.shape, value.dtype) for value in seed_inputs]
        + [pltpu.VMEM((count * ROWS, LANES), F32), pltpu.SemaphoreType.DMA((6,))],
        compiler_params=params(62 * 1024 * 1024),
        name="seed",
    )(*seed_inputs)
    inside, across = neighbours(seeds)
    first_moved = exchange(outgoing, "chan")
    weights, taps = pl.pallas_call(
        arrange_kernel,
        out_shape=(blocks, shape((reach + 1) * ROWS, LANES)),
        in_specs=vmem(2),
        out_specs=tuple(vmem(2)),
        scratch_shapes=[pltpu.VMEM((count * ROWS, LANES), F32)],
        compiler_params=params(),
        cost_estimate=pl.CostEstimate(flops=10**7, bytes_accessed=2 * 10**6, transcendentals=0),
        name="arrange",
    )(weights, taps)
    taps = taps.reshape(reach + 1, ROWS, LANES)

    inside, across, first_moved = lax.optimization_barrier((inside, across, first_moved))
    images, outgoing, side = pl.pallas_call(
        first_kernel,
        out_shape=(blocks, sent, shape(reach + count, ROWS, LANES)),
        in_specs=[SMEM] + vmem(10),
        out_specs=tuple(vmem(3)),
        scratch_shapes=[pltpu.VMEM((count, ROWS, LANES), F32)],
        compiler_params=params(),
        name="first",
    )(keep, inside, seeds, across, taps, weights, *tables)
    inside, across = neighbours(images)
    second_moved = exchange(outgoing, "chan")
    first_after = from_later_group(first_moved)
    inside, across, second_moved, first_after = lax.optimization_barrier(
        (inside, across, second_moved, first_after)
    )

    outgoing = pl.pallas_call(
        second_kernel,
        out_shape=shape(parts, count + 1, 8, LANES),
        in_specs=[SMEM] + vmem(11),
        out_specs=vmem(1)[0],
        scratch_shapes=[
            pltpu.VMEM((count, ROWS, LANES), F32),
            pltpu.VMEM((3, 8, LANES), F32),
        ],
        compiler_params=params(),
        name="second",
    )(keep, inside, images, across, side, taps, weights, *tables)

    moved = exchange(outgoing, "chan")
    after = from_later_group(moved)
    sums = jnp.sum(moved[:, count], (0, 1))
    sums = exchange(jnp.broadcast_to(sums, (groups, LANES)), "tm")
    second_after = from_later_group(second_moved)
    base, image = pl.pallas_call(
        rebuild_kernel,
        out_shape=(sent, sent),
        in_specs=[SMEM, SMEM] + vmem(5),
        out_specs=tuple(vmem(2)),
        compiler_params=params(),
        cost_estimate=pl.CostEstimate(flops=10**7, bytes_accessed=2 * 10**6, transcendentals=0),
        name="rebuild",
    )(place, keep_group, first_moved, first_after, second_moved, second_after, taps)
    return pl.pallas_call(
        last_kernel,
        out_shape=(shape(parts * count, 8 * LANES), shape(parts * count, 8 * LANES)),
        in_specs=[SMEM, SMEM] + vmem(6),
        out_specs=tuple(vmem(2)),
        scratch_shapes=[
            pltpu.VMEM((parts * count * 8, LANES), F32),
            pltpu.VMEM((parts * count * 8, LANES), F32),
        ],
        compiler_params=params(),
        name="last",
    )(place, keep_group, base, image, moved, after, sums, taps)


def solution(mesh):
    placed = (P(AXES, None), P(AXES, None), P(AXES, None), P())
    return jax.shard_map(
        local,
        mesh=mesh,
        in_specs=placed,
        out_specs=(P("tm", "chan"), P("tm", "chan")),
        check_vma=False,
    )
```

```python
import functools
import math

import jax
import jax.numpy as jnp
import numpy as np
from jax import lax
from jax.experimental import pallas as pl
from jax.experimental.pallas import tpu as pltpu
from jax.sharding import PartitionSpec as P

RIDGE = 0.25
ROWS = 64
LANES = 128
CHUNK = 4
F32 = jnp.float32
BF16 = jnp.bfloat16
AXES = ("tm", "chan")
VMEM_BYTES = 16 * 1024 * 1024


def params(limit=VMEM_BYTES):
    return pltpu.CompilerParams(vmem_limit_bytes=limit)


def halves(table):
    high = table.astype(np.float32).astype(jnp.bfloat16)
    low = (table - high.astype(np.float64)).astype(np.float32).astype(jnp.bfloat16)
    return high, low


def dft_tables():
    n1 = np.arange(ROWS)
    n2 = np.arange(LANES)
    k1 = np.arange(ROWS)
    k2 = (2 * np.arange(32)[None, :] + np.arange(2)[:, None]).reshape(-1)
    first = 2.0 * np.pi * (n1[:, None] * k1[None, :] % ROWS) / ROWS
    back_rows = np.concatenate([np.cos(first), -np.sin(first)], 1)
    second = 2.0 * np.pi * (k2[:, None] * n2[None, :] % LANES) / LANES
    scale = 1.0 / math.sqrt(ROWS * ROWS)
    cos = (np.cos(second) * scale).reshape(2, 32, LANES)
    sin = (np.sin(second) * scale).reshape(2, 32, LANES)
    from_real = np.concatenate([cos, sin], 2)
    from_imag = np.concatenate([-sin, cos], 2)
    back_lanes = np.stack([from_real, from_imag], 1).reshape(LANES, 2 * LANES)
    rows_high, rows_low = halves(back_rows)
    lanes_high, lanes_low = halves(back_lanes)
    twist = 2.0 * np.pi * k1[:, None] * n2[None, :] / (ROWS * LANES)
    return (
        np.concatenate([rows_high.T, rows_high.T, rows_low.T], 1),
        np.concatenate([lanes_high.T, lanes_high.T, lanes_low.T], 0),
        np.concatenate([lanes_high, lanes_high, lanes_low], 0),
        np.concatenate([rows_high, rows_high, rows_low], 1),
        np.stack([np.cos(twist), np.sin(twist)]).astype(np.float32),
    )


def split(value):
    high = value.astype(BF16)
    low = (value - high.astype(F32)).astype(BF16)
    return high, low


def dot(left, right):
    return jnp.dot(left, right, preferred_element_type=F32)


def forward_chunk(frames, ahead_rows, ahead_lanes, cos, sin):
    high, low = split(jnp.concatenate(frames, 1))
    mixed = dot(ahead_rows, jnp.concatenate([high, low, high], 0))
    turned = []
    for f in range(len(frames)):
        real = mixed[:ROWS, f * LANES : (f + 1) * LANES]
        imag = mixed[ROWS:, f * LANES : (f + 1) * LANES]
        turned.append(jnp.concatenate([real * cos + imag * sin, imag * cos - real * sin], 1))
    high, low = split(jnp.concatenate(turned, 0))
    return dot(jnp.concatenate([high, low, high], 1), ahead_lanes)


def backward_chunk(spectra, back_lanes, back_rows, cos, sin):
    high, low = split(spectra)
    mixed = dot(jnp.concatenate([high, low, high], 1), back_lanes)
    turned = []
    for f in range(spectra.shape[0] // ROWS):
        real = mixed[f * ROWS : (f + 1) * ROWS, :LANES]
        imag = mixed[f * ROWS : (f + 1) * ROWS, LANES:]
        turned.append(jnp.concatenate([real * cos - imag * sin, real * sin + imag * cos], 0))
    high, low = split(jnp.concatenate(turned, 1))
    return dot(back_rows, jnp.concatenate([high, low, high], 0))


def turn_pair(block):
    flipped = block.T
    low_half = flipped[:ROWS]
    high_half = flipped[ROWS:]
    left = lax.broadcasted_iota(jnp.int32, (ROWS, LANES), 1) < ROWS
    return (
        jnp.where(left, low_half, pltpu.roll(high_half, ROWS, 1)),
        jnp.where(left, pltpu.roll(low_half, ROWS, 1), high_half),
    )


def seed_kernel(*refs):
    sources, out_ref, sent_ref, places, held, semaphore = refs[:6], refs[6], refs[7], refs[8:14], refs[14], refs[15]
    copies = [
        pltpu.make_async_copy(source, place, semaphore.at[at])
        for at, (source, place) in enumerate(zip(sources, places))
    ]
    for copy in copies:
        copy.start()
    real_ref, imag_ref, weights_ref, back_lanes_ref, back_rows_ref, twist_ref = places
    count = real_ref.shape[0]
    for copy in copies:
        copy.wait()
    for j in range(32):
        columns = slice(j * LANES, (j + 1) * LANES)
        weights = weights_ref[:, columns]
        held[pl.ds(j, count, stride=ROWS), :] = weights * real_ref[:, columns]
        held[pl.ds(32 + j, count, stride=ROWS), :] = weights * imag_ref[:, columns]
    cos = twist_ref[0]
    sin = twist_ref[1]
    for start in range(0, count, CHUNK):
        spectra = []
        for f in range(start, start + CHUNK, 2):
            spectra += turn_pair(held[f * ROWS : (f + 2) * ROWS, :])
        frames = backward_chunk(
            jnp.concatenate(spectra, 0), back_lanes_ref[...], back_rows_ref[...], cos, sin
        )
        for f in range(CHUNK):
            frame = frames[:, f * LANES : (f + 1) * LANES]
            out_ref[start + f] = frame
            for group in range(ROWS // 8):
                sent_ref[group, start + f] = frame[group * 8 : (group + 1) * 8]


def arrange_kernel(weights_ref, taps_ref, weights_out, taps_out, held):
    count = weights_ref.shape[0]
    for j in range(32):
        weights = weights_ref[:, j * LANES : (j + 1) * LANES]
        held[pl.ds(j, count, stride=ROWS), :] = weights
        held[pl.ds(32 + j, count, stride=ROWS), :] = weights
    for f in range(0, count, 2):
        first, second = turn_pair(held[f * ROWS : (f + 2) * ROWS, :])
        weights_out[f] = first
        weights_out[f + 1] = second
    for n1 in range(ROWS):
        taps_out[pl.ds(n1, taps_ref.shape[0], stride=ROWS), :] = taps_ref[
            :, n1 * LANES : (n1 + 1) * LANES
        ]


def weighted_sum(taps, values):
    total = taps[0] * values[0]
    for tap, value in zip(taps[1:], values[1:]):
        total = total + tap * value
    return total


def back_filter(rows, taps, inside_ref, here_ref, across_ref, keep):
    reach = len(taps) - 1
    count = here_ref.shape[0]
    odd = jnp.full((8, LANES), keep[2]) > 0.5
    frames = [
        jnp.where(odd, inside_ref[t, rows, :], across_ref[t, rows, :]) for t in range(count - reach, count)
    ]
    frames += [here_ref[t, rows, :] for t in range(count)]
    frames += [
        jnp.where(odd, across_ref[t, rows, :], inside_ref[t, rows, :]) * keep[1] for t in range(reach)
    ]
    result = []
    for at in range(reach + count):
        total = weighted_sum(taps, frames[at : at + reach + 1])
        result.append(total * keep[0] if at < reach else total)
    return result


def ahead_filter(taps, frames):
    reach = len(taps) - 1
    return [
        weighted_sum(taps, [frames[at + reach - tap] for tap in range(reach + 1)])
        for at in range(len(frames) - reach)
    ]


def first_kernel(
    keep_ref, inside_ref, here_ref, across_ref, taps_ref, weights_ref,
    ahead_rows_ref, ahead_lanes_ref, back_lanes_ref, back_rows_ref, twist_ref, _,
    out_ref, sent_ref, side_ref, filtered,
):
    count = here_ref.shape[0]
    keep = (keep_ref[0], keep_ref[1], keep_ref[2])

    @pl.loop(0, ROWS // 8)
    def _(group):
        rows = pl.ds(pl.multiple_of(group * 8, 8), 8)
        taps = [taps_ref[p, rows, :] for p in range(taps_ref.shape[0])]
        side = back_filter(rows, taps, inside_ref, here_ref, across_ref, keep)
        for at, value in enumerate(side):
            side_ref[at, rows, :] = value
        for at, value in enumerate(ahead_filter(taps, side)):
            filtered[at, rows, :] = value

    cos = twist_ref[0]
    sin = twist_ref[1]
    for start in range(0, count, CHUNK):
        spectra = forward_chunk(
            [filtered[start + f] for f in range(CHUNK)], ahead_rows_ref[...], ahead_lanes_ref[...], cos, sin
        )
        weights = weights_ref[start : start + CHUNK].reshape(CHUNK * ROWS, LANES)
        frames = backward_chunk(spectra * weights, back_lanes_ref[...], back_rows_ref[...], cos, sin)
        for f in range(CHUNK):
            frame = frames[:, f * LANES : (f + 1) * LANES]
            out_ref[start + f] = frame
            for group in range(ROWS // 8):
                sent_ref[group, start + f] = frame[group * 8 : (group + 1) * 8]


def quarters():
    return lax.broadcasted_iota(jnp.int32, (8, LANES), 1) // 32


def pack(values):
    packed = jnp.zeros((8, LANES), F32)
    for at, value in enumerate(values):
        value = value + pltpu.roll(value, 64, 1)
        value = value + pltpu.roll(value, 32, 1)
        packed = jnp.where(quarters() == at, value, packed)
    return packed


def second_kernel(
    keep_ref, inside_ref, here_ref, across_ref, side_ref, taps_ref, weights_ref,
    ahead_rows_ref, ahead_lanes_ref, back_lanes_ref, back_rows_ref, twist_ref, _, __,
    out_ref, filtered, sums,
):
    count = here_ref.shape[0]
    keep = (keep_ref[0], keep_ref[1], keep_ref[2])
    reach = taps_ref.shape[0] - 1
    sums[...] = jnp.zeros_like(sums)

    @pl.loop(0, ROWS // 8)
    def _(group):
        rows = pl.ds(pl.multiple_of(group * 8, 8), 8)
        taps = [taps_ref[p, rows, :] for p in range(reach + 1)]
        image = back_filter(rows, taps, inside_ref, here_ref, across_ref, keep)
        side = [side_ref[at, rows, :] for at in range(reach + count)]
        image = [value + RIDGE * base for value, base in zip(image, side)]
        for at, value in enumerate(ahead_filter(taps, image)):
            filtered[at, rows, :] = value
        first, second, third = sums[0], sums[1], sums[2]
        for at in range(count):
            base = side[reach + at]
            value = image[reach + at]
            first = first + base * base
            second = second + base * value
            third = third + value * value
        sums[0] = first
        sums[1] = second
        sums[2] = third

    cos = twist_ref[0]
    sin = twist_ref[1]
    power = jnp.zeros((8, LANES), F32)
    for start in range(0, count, CHUNK):
        spectra = forward_chunk(
            [filtered[start + f] for f in range(CHUNK)], ahead_rows_ref[...], ahead_lanes_ref[...], cos, sin
        )
        weights = weights_ref[start : start + CHUNK].reshape(CHUNK * ROWS, LANES)
        weighted = spectra * weights
        power = power + jnp.sum((weighted * spectra).reshape(CHUNK * ROWS // 8, 8, LANES), 0)
        frames = backward_chunk(weighted, back_lanes_ref[...], back_rows_ref[...], cos, sin)
        for f in range(CHUNK):
            for group in range(ROWS // 8):
                out_ref[group, start + f] = frames[
                    group * 8 : (group + 1) * 8, f * LANES : (f + 1) * LANES
                ]
    totals = pack([sums[0], sums[1], sums[2], power])
    for group in range(ROWS // 8):
        out_ref[group, count] = totals


def local_taps(place_ref, taps_ref):
    rows = pl.ds(pl.multiple_of(place_ref[0] * 8, 8), 8)
    return [taps_ref[p, rows, :] for p in range(taps_ref.shape[0])]


def by_part(moved_ref, after_ref, keep, count, reach, finish):
    parts = moved_ref.shape[0]

    def frames(part):
        return [moved_ref[part, t] for t in range(count)]

    @pl.loop(0, parts - 1)
    def _(part):
        finish(part, frames(part) + [moved_ref[part + 1, t] for t in range(reach)])

    finish(parts - 1, frames(parts - 1) + [after_ref[t] * keep for t in range(reach)])


def rebuild_kernel(
    place_ref, keep_ref, first_ref, first_after_ref, second_ref, second_after_ref, taps_ref, base_ref, image_ref
):
    count = first_ref.shape[1]
    taps = local_taps(place_ref, taps_ref)
    reach = len(taps) - 1

    def base(part, frames):
        for at in range(count):
            base_ref[part, at] = weighted_sum(taps, frames[at : at + reach + 1])

    def image(part, frames):
        for at in range(count):
            image_ref[part, at] = (
                weighted_sum(taps, frames[at : at + reach + 1]) + RIDGE * base_ref[part, at]
            )

    by_part(first_ref, first_after_ref, keep_ref[0], count, reach, base)
    by_part(second_ref, second_after_ref, keep_ref[0], count, reach, image)


def last_kernel(
    place_ref, keep_ref, base_ref, image_ref, moved_ref, after_ref, sums_ref, taps_ref,
    solution_ref, residual_ref, kept, left,
):
    parts, count = base_ref.shape[:2]
    taps = local_taps(place_ref, taps_ref)
    reach = len(taps) - 1
    sums = sums_ref[0:8]
    for at in range(8, sums_ref.shape[0], 8):
        sums = sums + sums_ref[at : at + 8]
    norm, curve, square, power = (
        jnp.sum(jnp.sum(jnp.where(quarters() == at, sums, 0.0), 1, keepdims=True), 0, keepdims=True)
        for at in range(4)
    )
    cube = power + RIDGE * square
    step = norm / curve
    next_norm = step * step * square - norm
    grown = step * square / curve
    next_step = next_norm / (step * (step * cube - grown * square))
    to_base = step + next_step * grown
    to_image = -(next_step * step)
    image_rate = -(step + next_step * grown)
    cube_rate = next_step * step
    to_base, to_image, image_rate, cube_rate = (
        jnp.broadcast_to(value, (8, LANES)) for value in (to_base, to_image, image_rate, cube_rate)
    )

    def finish(part, frames):
        for at in range(count):
            base = base_ref[part, at]
            image = image_ref[part, at]
            again = weighted_sum(taps, frames[at : at + reach + 1]) + RIDGE * image
            here = pl.ds(pl.multiple_of((part * count + at) * 8, 8), 8)
            kept[here, :] = to_base * base + to_image * image
            left[here, :] = base + image_rate * image + cube_rate * again

    by_part(moved_ref, after_ref, keep_ref[0], count, reach, finish)

    for block in range(parts * count // 8):
        for n1 in range(8):
            places = pl.ds(block * 64 + n1, 8, stride=8)
            columns = slice(n1 * LANES, (n1 + 1) * LANES)
            solution_ref[block * 8 : (block + 1) * 8, columns] = kept[places, :]
            residual_ref[block * 8 : (block + 1) * 8, columns] = left[places, :]


def shape(*dims):
    return jax.ShapeDtypeStruct(dims, F32)


def vmem(number):
    return [pl.BlockSpec(memory_space=pltpu.VMEM)] * number


SMEM = pl.BlockSpec(memory_space=pltpu.SMEM)
ANY = pl.BlockSpec(memory_space=pl.ANY)


def local(observed_real, observed_imag, weights, taps):
    ahead_rows, ahead_lanes, back_lanes, back_rows, twist = dft_tables()
    count = weights.shape[0]
    reach = taps.shape[0] - 1
    parts = lax.axis_size("chan")
    devices = lax.axis_size("tm") * parts
    blocks = shape(count, ROWS, LANES)
    groups = lax.axis_size("tm")
    position = lax.axis_index(AXES)
    keep = jnp.stack([position > 0, position < devices - 1, position % 2 == 1]).astype(F32)
    place = lax.axis_index("chan").astype(jnp.int32).reshape(1)
    keep_group = (lax.axis_index("tm") < groups - 1).astype(F32).reshape(1)
    tables = (ahead_rows, ahead_lanes, back_lanes, back_rows, twist)

    def neighbours(block):
        inside = [(i, i ^ 1) for i in range(devices)]
        across = [(i, min(max(((i + 1) ^ 1) - 1, 0), devices - 1)) for i in range(devices)]
        return lax.ppermute(block, AXES, inside), lax.ppermute(block, AXES, across)

    def exchange(value, axis):
        return lax.all_to_all(value, axis, split_axis=0, concat_axis=0, tiled=True)

    def from_later_group(moved):
        return lax.ppermute(moved[0, :count], "tm", [(i + 1, i) for i in range(groups - 1)])

    seed_inputs = (observed_real, observed_imag, weights, back_lanes, back_rows, twist)
    seed_inputs = tuple(pltpu.with_memory_space_constraint(v, pltpu.HBM) for v in seed_inputs)
    sent = shape(parts, count, 8, LANES)
    seeds, outgoing = pl.pallas_call(
        seed_kernel,
        out_shape=(blocks, sent),
        in_specs=[pl.BlockSpec(memory_space=pltpu.HBM)] * 6,
        out_specs=tuple(vmem(2)),
        scratch_shapes=[pltpu.VMEM(value.shape, value.dtype) for value in seed_inputs]
        + [pltpu.VMEM((count * ROWS, LANES), F32), pltpu.SemaphoreType.DMA((6,))],
        compiler_params=params(),
        name="seed",
    )(*seed_inputs)
    inside, across = neighbours(seeds)
    first_moved = exchange(outgoing, "chan")
    weights, taps = pl.pallas_call(
        arrange_kernel,
        out_shape=(blocks, shape((reach + 1) * ROWS, LANES)),
        in_specs=vmem(2),
        out_specs=tuple(vmem(2)),
        scratch_shapes=[pltpu.VMEM((count * ROWS, LANES), F32)],
        compiler_params=params(),
        cost_estimate=pl.CostEstimate(flops=10**7, bytes_accessed=2 * 10**6, transcendentals=0),
        name="arrange",
    )(weights, taps)
    taps = taps.reshape(reach + 1, ROWS, LANES)

    images, outgoing, side = pl.pallas_call(
        first_kernel,
        out_shape=(blocks, sent, shape(reach + count, ROWS, LANES)),
        in_specs=[SMEM] + vmem(10) + [ANY],
        out_specs=tuple(vmem(3)),
        scratch_shapes=[pltpu.VMEM((count, ROWS, LANES), F32)],
        compiler_params=params(),
        name="first",
    )(keep, inside, seeds, across, taps, weights, *tables, first_moved)
    inside, across = neighbours(images)
    second_moved = exchange(outgoing, "chan")
    first_after = from_later_group(first_moved)

    outgoing = pl.pallas_call(
        second_kernel,
        out_shape=shape(parts, count + 1, 8, LANES),
        in_specs=[SMEM] + vmem(11) + [ANY, ANY],
        out_specs=vmem(1)[0],
        scratch_shapes=[
            pltpu.VMEM((count, ROWS, LANES), F32),
            pltpu.VMEM((3, 8, LANES), F32),
        ],
        compiler_params=params(),
        name="second",
    )(keep, inside, images, across, side, taps, weights, *tables, second_moved, first_after)

    moved = exchange(outgoing, "chan")
    after = from_later_group(moved)
    sums = jnp.sum(moved[:, count], (0, 1))
    sums = exchange(jnp.broadcast_to(sums, (groups, LANES)), "tm")
    second_after = from_later_group(second_moved)
    base, image = pl.pallas_call(
        rebuild_kernel,
        out_shape=(sent, sent),
        in_specs=[SMEM, SMEM] + vmem(5),
        out_specs=tuple(vmem(2)),
        compiler_params=params(),
        cost_estimate=pl.CostEstimate(flops=10**7, bytes_accessed=2 * 10**6, transcendentals=0),
        name="rebuild",
    )(place, keep_group, first_moved, first_after, second_moved, second_after, taps)
    return pl.pallas_call(
        last_kernel,
        out_shape=(shape(parts * count, 8 * LANES), shape(parts * count, 8 * LANES)),
        in_specs=[SMEM, SMEM] + vmem(6),
        out_specs=tuple(vmem(2)),
        scratch_shapes=[
            pltpu.VMEM((parts * count * 8, LANES), F32),
            pltpu.VMEM((parts * count * 8, LANES), F32),
        ],
        compiler_params=params(),
        name="last",
    )(place, keep_group, base, image, moved, after, sums, taps)


def solution(mesh):
    placed = (P(AXES, None), P(AXES, None), P(AXES, None), P())
    return jax.shard_map(
        local,
        mesh=mesh,
        in_specs=placed,
        out_specs=(P("tm", "chan"), P("tm", "chan")),
        check_vma=False,
    )
```

```python
import functools
import math

import jax
import jax.numpy as jnp
import numpy as np
from jax import lax
from jax.experimental import pallas as pl
from jax.experimental.pallas import tpu as pltpu
from jax.sharding import PartitionSpec as P

RIDGE = 0.25
ROWS = 64
LANES = 128
CHUNK = 4
F32 = jnp.float32
BF16 = jnp.bfloat16
AXES = ("tm", "chan")
VMEM_BYTES = 16 * 1024 * 1024


def params(limit=VMEM_BYTES):
    return pltpu.CompilerParams(vmem_limit_bytes=limit)


def halves(table):
    high = table.astype(np.float32).astype(jnp.bfloat16)
    low = (table - high.astype(np.float64)).astype(np.float32).astype(jnp.bfloat16)
    return high, low


def dft_tables():
    n1 = np.arange(ROWS)
    n2 = np.arange(LANES)
    k1 = np.arange(ROWS)
    k2 = (2 * np.arange(32)[None, :] + np.arange(2)[:, None]).reshape(-1)
    first = 2.0 * np.pi * (n1[:, None] * k1[None, :] % ROWS) / ROWS
    back_rows = np.concatenate([np.cos(first), -np.sin(first)], 1)
    second = 2.0 * np.pi * (k2[:, None] * n2[None, :] % LANES) / LANES
    scale = 1.0 / math.sqrt(ROWS * ROWS)
    cos = (np.cos(second) * scale).reshape(2, 32, LANES)
    sin = (np.sin(second) * scale).reshape(2, 32, LANES)
    from_real = np.concatenate([cos, sin], 2)
    from_imag = np.concatenate([-sin, cos], 2)
    back_lanes = np.stack([from_real, from_imag], 1).reshape(LANES, 2 * LANES)
    rows_high, rows_low = halves(back_rows)
    lanes_high, lanes_low = halves(back_lanes)
    twist = 2.0 * np.pi * k1[:, None] * n2[None, :] / (ROWS * LANES)
    return (
        np.concatenate([rows_high.T, rows_high.T, rows_low.T], 1),
        np.concatenate([lanes_high.T, lanes_high.T, lanes_low.T], 0),
        np.concatenate([lanes_high, lanes_high, lanes_low], 0),
        np.concatenate([rows_high, rows_high, rows_low], 1),
        np.stack([np.cos(twist), np.sin(twist)]).astype(np.float32),
    )


def split(value):
    high = value.astype(BF16)
    low = (value - high.astype(F32)).astype(BF16)
    return high, low


def dot(left, right):
    return jnp.dot(left, right, preferred_element_type=F32)


def forward_chunk(frames, ahead_rows, ahead_lanes, cos, sin):
    high, low = split(jnp.concatenate(frames, 1))
    mixed = dot(ahead_rows, jnp.concatenate([high, low, high], 0))
    turned = []
    for f in range(len(frames)):
        real = mixed[:ROWS, f * LANES : (f + 1) * LANES]
        imag = mixed[ROWS:, f * LANES : (f + 1) * LANES]
        turned.append(jnp.concatenate([real * cos + imag * sin, imag * cos - real * sin], 1))
    high, low = split(jnp.concatenate(turned, 0))
    return dot(jnp.concatenate([high, low, high], 1), ahead_lanes)


def backward_chunk(spectra, back_lanes, back_rows, cos, sin):
    high, low = split(spectra)
    mixed = dot(jnp.concatenate([high, low, high], 1), back_lanes)
    turned = []
    for f in range(spectra.shape[0] // ROWS):
        real = mixed[f * ROWS : (f + 1) * ROWS, :LANES]
        imag = mixed[f * ROWS : (f + 1) * ROWS, LANES:]
        turned.append(jnp.concatenate([real * cos - imag * sin, real * sin + imag * cos], 0))
    high, low = split(jnp.concatenate(turned, 1))
    return dot(back_rows, jnp.concatenate([high, low, high], 0))


def turn_pair(block):
    flipped = block.T
    low_half = flipped[:ROWS]
    high_half = flipped[ROWS:]
    left = lax.broadcasted_iota(jnp.int32, (ROWS, LANES), 1) < ROWS
    return (
        jnp.where(left, low_half, pltpu.roll(high_half, ROWS, 1)),
        jnp.where(left, pltpu.roll(low_half, ROWS, 1), high_half),
    )


def seed_kernel(*refs):
    sources, out_ref, places, held, semaphore = refs[:6], refs[6], refs[7:13], refs[13], refs[14]
    copies = [
        pltpu.make_async_copy(source, place, semaphore.at[at])
        for at, (source, place) in enumerate(zip(sources, places))
    ]
    for copy in copies:
        copy.start()
    real_ref, imag_ref, weights_ref, back_lanes_ref, back_rows_ref, twist_ref = places
    count = real_ref.shape[0]
    for copy in copies:
        copy.wait()
    for j in range(32):
        columns = slice(j * LANES, (j + 1) * LANES)
        weights = weights_ref[:, columns]
        held[pl.ds(j, count, stride=ROWS), :] = weights * real_ref[:, columns]
        held[pl.ds(32 + j, count, stride=ROWS), :] = weights * imag_ref[:, columns]
    cos = twist_ref[0]
    sin = twist_ref[1]
    for start in range(0, count, CHUNK):
        spectra = []
        for f in range(start, start + CHUNK, 2):
            spectra += turn_pair(held[f * ROWS : (f + 2) * ROWS, :])
        frames = backward_chunk(
            jnp.concatenate(spectra, 0), back_lanes_ref[...], back_rows_ref[...], cos, sin
        )
        for f in range(CHUNK):
            out_ref[start + f] = frames[:, f * LANES : (f + 1) * LANES]


def arrange_kernel(weights_ref, taps_ref, weights_out, taps_out, held):
    count = weights_ref.shape[0]
    for j in range(32):
        weights = weights_ref[:, j * LANES : (j + 1) * LANES]
        held[pl.ds(j, count, stride=ROWS), :] = weights
        held[pl.ds(32 + j, count, stride=ROWS), :] = weights
    for f in range(0, count, 2):
        first, second = turn_pair(held[f * ROWS : (f + 2) * ROWS, :])
        weights_out[f] = first
        weights_out[f + 1] = second
    for n1 in range(ROWS):
        taps_out[pl.ds(n1, taps_ref.shape[0], stride=ROWS), :] = taps_ref[
            :, n1 * LANES : (n1 + 1) * LANES
        ]


def weighted_sum(taps, values):
    total = taps[0] * values[0]
    for tap, value in zip(taps[1:], values[1:]):
        total = total + tap * value
    return total


def back_filter(rows, taps, inside_ref, here_ref, across_ref, keep):
    reach = len(taps) - 1
    count = here_ref.shape[0]
    odd = jnp.full((8, LANES), keep[2]) > 0.5
    frames = [
        jnp.where(odd, inside_ref[t, rows, :], across_ref[t, rows, :]) for t in range(count - reach, count)
    ]
    frames += [here_ref[t, rows, :] for t in range(count)]
    frames += [
        jnp.where(odd, across_ref[t, rows, :], inside_ref[t, rows, :]) * keep[1] for t in range(reach)
    ]
    result = []
    for at in range(reach + count):
        total = weighted_sum(taps, frames[at : at + reach + 1])
        result.append(total * keep[0] if at < reach else total)
    return result


def ahead_filter(taps, frames):
    reach = len(taps) - 1
    return [
        weighted_sum(taps, [frames[at + reach - tap] for tap in range(reach + 1)])
        for at in range(len(frames) - reach)
    ]


def first_kernel(
    keep_ref, inside_ref, here_ref, across_ref, taps_ref, weights_ref,
    ahead_rows_ref, ahead_lanes_ref, back_lanes_ref, back_rows_ref, twist_ref,
    out_ref, side_ref, filtered,
):
    count = here_ref.shape[0]
    keep = (keep_ref[0], keep_ref[1], keep_ref[2])

    @pl.loop(0, ROWS // 8)
    def _(group):
        rows = pl.ds(pl.multiple_of(group * 8, 8), 8)
        taps = [taps_ref[p, rows, :] for p in range(taps_ref.shape[0])]
        side = back_filter(rows, taps, inside_ref, here_ref, across_ref, keep)
        for at, value in enumerate(side):
            side_ref[at, rows, :] = value
        for at, value in enumerate(ahead_filter(taps, side)):
            filtered[at, rows, :] = value

    cos = twist_ref[0]
    sin = twist_ref[1]
    for start in range(0, count, CHUNK):
        spectra = forward_chunk(
            [filtered[start + f] for f in range(CHUNK)], ahead_rows_ref[...], ahead_lanes_ref[...], cos, sin
        )
        weights = weights_ref[start : start + CHUNK].reshape(CHUNK * ROWS, LANES)
        frames = backward_chunk(spectra * weights, back_lanes_ref[...], back_rows_ref[...], cos, sin)
        for f in range(CHUNK):
            out_ref[start + f] = frames[:, f * LANES : (f + 1) * LANES]


def quarters():
    return lax.broadcasted_iota(jnp.int32, (8, LANES), 1) // 32


def pack(values):
    packed = jnp.zeros((8, LANES), F32)
    for at, value in enumerate(values):
        value = value + pltpu.roll(value, 64, 1)
        value = value + pltpu.roll(value, 32, 1)
        packed = jnp.where(quarters() == at, value, packed)
    return packed


def second_kernel(
    keep_ref, inside_ref, here_ref, across_ref, side_ref, taps_ref, weights_ref,
    ahead_rows_ref, ahead_lanes_ref, back_lanes_ref, back_rows_ref, twist_ref,
    out_ref, filtered, sums,
):
    count = here_ref.shape[0]
    keep = (keep_ref[0], keep_ref[1], keep_ref[2])
    reach = taps_ref.shape[0] - 1
    sums[...] = jnp.zeros_like(sums)

    @pl.loop(0, ROWS // 8)
    def _(group):
        rows = pl.ds(pl.multiple_of(group * 8, 8), 8)
        taps = [taps_ref[p, rows, :] for p in range(reach + 1)]
        image = back_filter(rows, taps, inside_ref, here_ref, across_ref, keep)
        side = [side_ref[at, rows, :] for at in range(reach + count)]
        image = [value + RIDGE * base for value, base in zip(image, side)]
        for at, value in enumerate(ahead_filter(taps, image)):
            filtered[at, rows, :] = value
        first, second, third = sums[0], sums[1], sums[2]
        for at in range(count):
            base = side[reach + at]
            value = image[reach + at]
            out_ref[group, at] = base
            out_ref[group, count + at] = value
            first = first + base * base
            second = second + base * value
            third = third + value * value
        sums[0] = first
        sums[1] = second
        sums[2] = third

    cos = twist_ref[0]
    sin = twist_ref[1]
    power = jnp.zeros((8, LANES), F32)
    for start in range(0, count, CHUNK):
        spectra = forward_chunk(
            [filtered[start + f] for f in range(CHUNK)], ahead_rows_ref[...], ahead_lanes_ref[...], cos, sin
        )
        weights = weights_ref[start : start + CHUNK].reshape(CHUNK * ROWS, LANES)
        weighted = spectra * weights
        power = power + jnp.sum((weighted * spectra).reshape(CHUNK * ROWS // 8, 8, LANES), 0)
        frames = backward_chunk(weighted, back_lanes_ref[...], back_rows_ref[...], cos, sin)
        for f in range(CHUNK):
            for group in range(ROWS // 8):
                out_ref[group, 2 * count + start + f] = frames[
                    group * 8 : (group + 1) * 8, f * LANES : (f + 1) * LANES
                ]
    totals = pack([sums[0], sums[1], sums[2], power])
    for group in range(ROWS // 8):
        out_ref[group, 3 * count] = totals


def last_kernel(
    place_ref, keep_ref, moved_ref, after_ref, sums_ref, taps_ref,
    solution_ref, residual_ref, kept, left,
):
    parts = moved_ref.shape[0]
    count = (moved_ref.shape[1] - 1) // 3
    reach = taps_ref.shape[0] - 1
    rows = pl.ds(pl.multiple_of(place_ref[0] * 8, 8), 8)
    sums = sums_ref[0:8]
    for at in range(8, sums_ref.shape[0], 8):
        sums = sums + sums_ref[at : at + 8]
    norm, curve, square, power = (
        jnp.sum(jnp.sum(jnp.where(quarters() == at, sums, 0.0), 1, keepdims=True), 0, keepdims=True)
        for at in range(4)
    )
    cube = power + RIDGE * square
    step = norm / curve
    next_norm = step * step * square - norm
    grown = step * square / curve
    next_step = next_norm / (step * (step * cube - grown * square))
    to_base = step + next_step * grown
    to_image = -(next_step * step)
    image_rate = -(step + next_step * grown)
    cube_rate = next_step * step
    to_base, to_image, image_rate, cube_rate = (
        jnp.broadcast_to(value, (8, LANES)) for value in (to_base, to_image, image_rate, cube_rate)
    )
    taps = [taps_ref[p, rows, :] for p in range(reach + 1)]

    def finish(part, tail):
        frames = [moved_ref[part, 2 * count + t] for t in range(count)] + tail
        for at in range(count):
            base = moved_ref[part, at]
            image = moved_ref[part, count + at]
            again = weighted_sum(taps, frames[at : at + reach + 1]) + RIDGE * image
            here = pl.ds(pl.multiple_of((part * count + at) * 8, 8), 8)
            kept[here, :] = to_base * base + to_image * image
            left[here, :] = base + image_rate * image + cube_rate * again

    @pl.loop(0, parts - 1)
    def _(part):
        finish(part, [moved_ref[part + 1, 2 * count + t] for t in range(reach)])

    finish(parts - 1, [after_ref[t] * keep_ref[0] for t in range(reach)])

    for block in range(parts * count // 8):
        for n1 in range(8):
            places = pl.ds(block * 64 + n1, 8, stride=8)
            columns = slice(n1 * LANES, (n1 + 1) * LANES)
            solution_ref[block * 8 : (block + 1) * 8, columns] = kept[places, :]
            residual_ref[block * 8 : (block + 1) * 8, columns] = left[places, :]


def shape(*dims):
    return jax.ShapeDtypeStruct(dims, F32)


def vmem(number):
    return [pl.BlockSpec(memory_space=pltpu.VMEM)] * number


SMEM = pl.BlockSpec(memory_space=pltpu.SMEM)


def local(observed_real, observed_imag, weights, taps):
    ahead_rows, ahead_lanes, back_lanes, back_rows, twist = dft_tables()
    count = weights.shape[0]
    reach = taps.shape[0] - 1
    parts = lax.axis_size("chan")
    devices = lax.axis_size("tm") * parts
    blocks = shape(count, ROWS, LANES)
    groups = lax.axis_size("tm")
    position = lax.axis_index(AXES)
    keep = jnp.stack([position > 0, position < devices - 1, position % 2 == 1]).astype(F32)
    place = lax.axis_index("chan").astype(jnp.int32).reshape(1)
    keep_group = (lax.axis_index("tm") < groups - 1).astype(F32).reshape(1)
    tables = (ahead_rows, ahead_lanes, back_lanes, back_rows, twist)

    def neighbours(block):
        inside = [(i, i ^ 1) for i in range(devices)]
        across = [(i, min(max(((i + 1) ^ 1) - 1, 0), devices - 1)) for i in range(devices)]
        return lax.ppermute(block, AXES, inside), lax.ppermute(block, AXES, across)

    def exchange(value, axis):
        return lax.all_to_all(value, axis, split_axis=0, concat_axis=0, tiled=True)

    seed_inputs = (observed_real, observed_imag, weights, back_lanes, back_rows, twist)
    seed_inputs = tuple(pltpu.with_memory_space_constraint(v, pltpu.HBM) for v in seed_inputs)
    seeds = pl.pallas_call(
        seed_kernel,
        out_shape=blocks,
        in_specs=[pl.BlockSpec(memory_space=pltpu.HBM)] * 6,
        out_specs=vmem(1)[0],
        scratch_shapes=[pltpu.VMEM(value.shape, value.dtype) for value in seed_inputs]
        + [pltpu.VMEM((count * ROWS, LANES), F32), pltpu.SemaphoreType.DMA((6,))],
        compiler_params=params(),
        name="seed",
    )(*seed_inputs)
    inside, across = neighbours(seeds)
    weights, taps = pl.pallas_call(
        arrange_kernel,
        out_shape=(blocks, shape((reach + 1) * ROWS, LANES)),
        in_specs=vmem(2),
        out_specs=tuple(vmem(2)),
        scratch_shapes=[pltpu.VMEM((count * ROWS, LANES), F32)],
        compiler_params=params(),
        cost_estimate=pl.CostEstimate(flops=10**7, bytes_accessed=2 * 10**6, transcendentals=0),
        name="arrange",
    )(weights, taps)
    taps = taps.reshape(reach + 1, ROWS, LANES)

    images, side = pl.pallas_call(
        first_kernel,
        out_shape=(blocks, shape(reach + count, ROWS, LANES)),
        in_specs=[SMEM] + vmem(10),
        out_specs=tuple(vmem(2)),
        scratch_shapes=[pltpu.VMEM((count, ROWS, LANES), F32)],
        compiler_params=params(),
        name="first",
    )(keep, inside, seeds, across, taps, weights, *tables)
    inside, across = neighbours(images)

    outgoing = pl.pallas_call(
        second_kernel,
        out_shape=shape(parts, 3 * count + 1, 8, LANES),
        in_specs=[SMEM] + vmem(11),
        out_specs=vmem(1)[0],
        scratch_shapes=[
            pltpu.VMEM((count, ROWS, LANES), F32),
            pltpu.VMEM((3, 8, LANES), F32),
        ],
        compiler_params=params(),
        name="second",
    )(keep, inside, images, across, side, taps, weights, *tables)

    moved = exchange(outgoing, "chan")
    after = lax.ppermute(
        moved[0, 2 * count : 3 * count], "tm", [(i + 1, i) for i in range(groups - 1)]
    )
    sums = jnp.sum(moved[:, 3 * count], (0, 1))
    sums = exchange(jnp.broadcast_to(sums, (groups, LANES)), "tm")
    return pl.pallas_call(
        last_kernel,
        out_shape=(shape(parts * count, 8 * LANES), shape(parts * count, 8 * LANES)),
        in_specs=[SMEM, SMEM] + vmem(4),
        out_specs=tuple(vmem(2)),
        scratch_shapes=[
            pltpu.VMEM((parts * count * 8, LANES), F32),
            pltpu.VMEM((parts * count * 8, LANES), F32),
        ],
        compiler_params=params(),
        name="last",
    )(place, keep_group, moved, after, sums, taps)


def solution(mesh):
    placed = (P(AXES, None), P(AXES, None), P(AXES, None), P())
    return jax.shard_map(
        local,
        mesh=mesh,
        in_specs=placed,
        out_specs=(P("tm", "chan"), P("tm", "chan")),
        check_vma=False,
    )
```

```python
import functools
import math

import jax
import jax.numpy as jnp
import numpy as np
from jax import lax
from jax.experimental import pallas as pl
from jax.experimental.pallas import tpu as pltpu
from jax.sharding import PartitionSpec as P

RIDGE = 0.25
ROWS = 64
LANES = 128
CHUNK = 16
F32 = jnp.float32
BF16 = jnp.bfloat16
AXES = ("tm", "chan")
VMEM_BYTES = 16 * 1024 * 1024


def params(limit=VMEM_BYTES):
    return pltpu.CompilerParams(vmem_limit_bytes=limit)


def halves(table):
    high = table.astype(np.float32).astype(jnp.bfloat16)
    low = (table - high.astype(np.float64)).astype(np.float32).astype(jnp.bfloat16)
    return high, low


def dft_tables():
    n1 = np.arange(ROWS)
    n2 = np.arange(LANES)
    k1 = np.arange(ROWS)
    k2 = (2 * np.arange(32)[None, :] + np.arange(2)[:, None]).reshape(-1)
    first = 2.0 * np.pi * (n1[:, None] * k1[None, :] % ROWS) / ROWS
    back_rows = np.concatenate([np.cos(first), -np.sin(first)], 1)
    second = 2.0 * np.pi * (k2[:, None] * n2[None, :] % LANES) / LANES
    scale = 1.0 / math.sqrt(ROWS * ROWS)
    cos = (np.cos(second) * scale).reshape(2, 32, LANES)
    sin = (np.sin(second) * scale).reshape(2, 32, LANES)
    from_real = np.concatenate([cos, sin], 2)
    from_imag = np.concatenate([-sin, cos], 2)
    back_lanes = np.stack([from_real, from_imag], 1).reshape(LANES, 2 * LANES)
    rows_high, rows_low = halves(back_rows)
    lanes_high, lanes_low = halves(back_lanes)
    twist = 2.0 * np.pi * k1[:, None] * n2[None, :] / (ROWS * LANES)
    return (
        np.concatenate([rows_high.T, rows_high.T, rows_low.T], 1),
        np.concatenate([lanes_high.T, lanes_low.T], 1),
        np.concatenate([lanes_high, lanes_high, lanes_low], 0),
        np.block([[rows_high, rows_high], [rows_low, np.zeros_like(rows_low)]]),
        np.stack([np.cos(twist), np.sin(twist)]).astype(np.float32),
    )


def split(value):
    high = value.astype(BF16)
    low = (value - high.astype(F32)).astype(BF16)
    return high, low


def dot(left, right):
    return jnp.dot(left, right, preferred_element_type=F32)


def forward_chunk(frames, ahead_rows, ahead_lanes, cos, sin):
    high, low = split(jnp.concatenate(frames, 1))
    mixed = dot(ahead_rows, jnp.concatenate([high, low, high], 0))
    turned = []
    for f in range(len(frames)):
        real = mixed[:ROWS, f * LANES : (f + 1) * LANES]
        imag = mixed[ROWS:, f * LANES : (f + 1) * LANES]
        turned.append(jnp.concatenate([real * cos + imag * sin, imag * cos - real * sin], 1))
    high, low = split(jnp.concatenate(turned, 0))
    wide = dot(high, ahead_lanes)
    return wide[:, :LANES] + wide[:, LANES:] + dot(low, ahead_lanes[:, :LANES])


def backward_chunk(spectra, back_lanes, back_rows, cos, sin):
    high, low = split(spectra)
    mixed = dot(jnp.concatenate([high, low, high], 1), back_lanes)
    turned = []
    for f in range(spectra.shape[0] // ROWS):
        real = mixed[f * ROWS : (f + 1) * ROWS, :LANES]
        imag = mixed[f * ROWS : (f + 1) * ROWS, LANES:]
        turned.append(jnp.concatenate([real * cos - imag * sin, real * sin + imag * cos], 0))
    high, low = split(jnp.concatenate(turned, 1))
    tall = dot(back_rows, jnp.concatenate([high, low], 0))
    return tall[:ROWS] + tall[ROWS:]


def turn_pair(block):
    flipped = block.T
    low_half = flipped[:ROWS]
    high_half = flipped[ROWS:]
    left = lax.broadcasted_iota(jnp.int32, (ROWS, LANES), 1) < ROWS
    return (
        jnp.where(left, low_half, pltpu.roll(high_half, ROWS, 1)),
        jnp.where(left, pltpu.roll(low_half, ROWS, 1), high_half),
    )


def seed_kernel(*refs):
    sources, out_ref, places, held, semaphore = refs[:6], refs[6], refs[7:13], refs[13], refs[14]
    copies = [
        pltpu.make_async_copy(source, place, semaphore.at[at])
        for at, (source, place) in enumerate(zip(sources, places))
    ]
    for copy in copies:
        copy.start()
    real_ref, imag_ref, weights_ref, back_lanes_ref, back_rows_ref, twist_ref = places
    count = real_ref.shape[0]
    for copy in copies:
        copy.wait()
    for j in range(32):
        columns = slice(j * LANES, (j + 1) * LANES)
        weights = weights_ref[:, columns]
        held[pl.ds(j, count, stride=ROWS), :] = weights * real_ref[:, columns]
        held[pl.ds(32 + j, count, stride=ROWS), :] = weights * imag_ref[:, columns]
    cos = twist_ref[0]
    sin = twist_ref[1]
    for start in range(0, count, CHUNK):
        spectra = []
        for f in range(start, start + CHUNK, 2):
            spectra += turn_pair(held[f * ROWS : (f + 2) * ROWS, :])
        frames = backward_chunk(
            jnp.concatenate(spectra, 0), back_lanes_ref[...], back_rows_ref[...], cos, sin
        )
        for f in range(CHUNK):
            out_ref[start + f] = frames[:, f * LANES : (f + 1) * LANES]


def arrange_kernel(weights_ref, taps_ref, weights_out, taps_out, held):
    count = weights_ref.shape[0]
    for j in range(32):
        weights = weights_ref[:, j * LANES : (j + 1) * LANES]
        held[pl.ds(j, count, stride=ROWS), :] = weights
        held[pl.ds(32 + j, count, stride=ROWS), :] = weights
    for f in range(0, count, 2):
        first, second = turn_pair(held[f * ROWS : (f + 2) * ROWS, :])
        weights_out[f] = first
        weights_out[f + 1] = second
    for n1 in range(ROWS):
        taps_out[pl.ds(n1, taps_ref.shape[0], stride=ROWS), :] = taps_ref[
            :, n1 * LANES : (n1 + 1) * LANES
        ]


def weighted_sum(taps, values):
    total = taps[0] * values[0]
    for tap, value in zip(taps[1:], values[1:]):
        total = total + tap * value
    return total


def back_filter(rows, taps, inside_ref, here_ref, across_ref, keep):
    reach = len(taps) - 1
    count = here_ref.shape[0]
    odd = jnp.full((8, LANES), keep[2]) > 0.5
    frames = [
        jnp.where(odd, inside_ref[t, rows, :], across_ref[t, rows, :]) for t in range(count - reach, count)
    ]
    frames += [here_ref[t, rows, :] for t in range(count)]
    frames += [
        jnp.where(odd, across_ref[t, rows, :], inside_ref[t, rows, :]) * keep[1] for t in range(reach)
    ]
    result = []
    for at in range(reach + count):
        total = weighted_sum(taps, frames[at : at + reach + 1])
        result.append(total * keep[0] if at < reach else total)
    return result


def ahead_filter(taps, frames):
    reach = len(taps) - 1
    return [
        weighted_sum(taps, [frames[at + reach - tap] for tap in range(reach + 1)])
        for at in range(len(frames) - reach)
    ]


def first_kernel(
    keep_ref, inside_ref, here_ref, across_ref, taps_ref, weights_ref,
    ahead_rows_ref, ahead_lanes_ref, back_lanes_ref, back_rows_ref, twist_ref,
    out_ref, side_ref, filtered,
):
    count = here_ref.shape[0]
    keep = (keep_ref[0], keep_ref[1], keep_ref[2])

    @pl.loop(0, ROWS // 8)
    def _(group):
        rows = pl.ds(pl.multiple_of(group * 8, 8), 8)
        taps = [taps_ref[p, rows, :] for p in range(taps_ref.shape[0])]
        side = back_filter(rows, taps, inside_ref, here_ref, across_ref, keep)
        for at, value in enumerate(side):
            side_ref[at, rows, :] = value
        for at, value in enumerate(ahead_filter(taps, side)):
            filtered[at, rows, :] = value

    cos = twist_ref[0]
    sin = twist_ref[1]
    for start in range(0, count, CHUNK):
        spectra = forward_chunk(
            [filtered[start + f] for f in range(CHUNK)], ahead_rows_ref[...], ahead_lanes_ref[...], cos, sin
        )
        weights = weights_ref[start : start + CHUNK].reshape(CHUNK * ROWS, LANES)
        frames = backward_chunk(spectra * weights, back_lanes_ref[...], back_rows_ref[...], cos, sin)
        for f in range(CHUNK):
            out_ref[start + f] = frames[:, f * LANES : (f + 1) * LANES]


def quarters(rows):
    return lax.broadcasted_iota(jnp.int32, (rows, LANES), 1) // 32


def pack(values):
    packed = jnp.zeros((8, LANES), F32)
    for at, value in enumerate(values):
        value = value + pltpu.roll(value, 64, 1)
        value = value + pltpu.roll(value, 32, 1)
        packed = jnp.where(quarters(8) == at, value, packed)
    return packed


def second_kernel(
    keep_ref, inside_ref, here_ref, across_ref, side_ref, taps_ref, weights_ref,
    ahead_rows_ref, ahead_lanes_ref, back_lanes_ref, back_rows_ref, twist_ref,
    out_ref, filtered, sums,
):
    count = here_ref.shape[0]
    keep = (keep_ref[0], keep_ref[1], keep_ref[2])
    reach = taps_ref.shape[0] - 1
    sums[...] = jnp.zeros_like(sums)

    @pl.loop(0, ROWS // 8)
    def _(group):
        rows = pl.ds(pl.multiple_of(group * 8, 8), 8)
        taps = [taps_ref[p, rows, :] for p in range(reach + 1)]
        image = back_filter(rows, taps, inside_ref, here_ref, across_ref, keep)
        side = [side_ref[at, rows, :] for at in range(reach + count)]
        image = [value + RIDGE * base for value, base in zip(image, side)]
        for at, value in enumerate(ahead_filter(taps, image)):
            filtered[at, rows, :] = value
        first, second, third = sums[0], sums[1], sums[2]
        for at in range(count):
            base = side[reach + at]
            value = image[reach + at]
            out_ref[group, at] = base
            out_ref[group, count + at] = value
            first = first + base * base
            second = second + base * value
            third = third + value * value
        sums[0] = first
        sums[1] = second
        sums[2] = third

    cos = twist_ref[0]
    sin = twist_ref[1]
    power = jnp.zeros((8, LANES), F32)
    for start in range(0, count, CHUNK):
        spectra = forward_chunk(
            [filtered[start + f] for f in range(CHUNK)], ahead_rows_ref[...], ahead_lanes_ref[...], cos, sin
        )
        weights = weights_ref[start : start + CHUNK].reshape(CHUNK * ROWS, LANES)
        weighted = spectra * weights
        power = power + jnp.sum((weighted * spectra).reshape(CHUNK * ROWS // 8, 8, LANES), 0)
        frames = backward_chunk(weighted, back_lanes_ref[...], back_rows_ref[...], cos, sin)
        for f in range(CHUNK):
            for group in range(ROWS // 8):
                out_ref[group, 2 * count + start + f] = frames[
                    group * 8 : (group + 1) * 8, f * LANES : (f + 1) * LANES
                ]
    totals = pack([sums[0], sums[1], sums[2], power])
    for group in range(ROWS // 8):
        out_ref[group, 3 * count] = totals


def tail_kernel(moved_ref, frames_ref, sums_ref):
    count = frames_ref.shape[0]
    frames_ref[...] = moved_ref[0, 2 * count : 3 * count]
    total = moved_ref[0, 3 * count]
    for part in range(1, moved_ref.shape[0]):
        total = total + moved_ref[part, 3 * count]
    sums_ref[...] = jnp.broadcast_to((total[:4] + total[4:])[None], sums_ref.shape)


def last_kernel(
    place_ref, keep_ref, moved_ref, after_ref, sums_ref, taps_ref,
    solution_ref, residual_ref, kept, left,
):
    parts = moved_ref.shape[0]
    count = (moved_ref.shape[1] - 1) // 3
    reach = taps_ref.shape[0] - 1
    rows = pl.ds(pl.multiple_of(place_ref[0] * 8, 8), 8)
    sums = jnp.sum(sums_ref[...], 0)
    norm, curve, square, power = (
        jnp.sum(jnp.sum(jnp.where(quarters(4) == at, sums, 0.0), 1, keepdims=True), 0, keepdims=True)
        for at in range(4)
    )
    cube = power + RIDGE * square
    step = norm / curve
    next_norm = step * step * square - norm
    grown = step * square / curve
    next_step = next_norm / (step * (step * cube - grown * square))
    to_base = step + next_step * grown
    to_image = -(next_step * step)
    image_rate = -(step + next_step * grown)
    cube_rate = next_step * step
    to_base, to_image, image_rate, cube_rate = (
        jnp.broadcast_to(value, (8, LANES)) for value in (to_base, to_image, image_rate, cube_rate)
    )
    taps = [taps_ref[p, rows, :] for p in range(reach + 1)]

    def finish(part, tail):
        frames = [moved_ref[part, 2 * count + t] for t in range(count)] + tail
        for at in range(count):
            base = moved_ref[part, at]
            image = moved_ref[part, count + at]
            again = weighted_sum(taps, frames[at : at + reach + 1]) + RIDGE * image
            here = pl.ds(pl.multiple_of((part * count + at) * 8, 8), 8)
            kept[here, :] = to_base * base + to_image * image
            left[here, :] = base + image_rate * image + cube_rate * again

    @pl.loop(0, parts - 1)
    def _(part):
        finish(part, [moved_ref[part + 1, 2 * count + t] for t in range(reach)])

    finish(parts - 1, [after_ref[t] * keep_ref[0] for t in range(reach)])

    for block in range(parts * count // 8):
        for n1 in range(8):
            places = pl.ds(block * 64 + n1, 8, stride=8)
            columns = slice(n1 * LANES, (n1 + 1) * LANES)
            solution_ref[block * 8 : (block + 1) * 8, columns] = kept[places, :]
            residual_ref[block * 8 : (block + 1) * 8, columns] = left[places, :]


def shape(*dims):
    return jax.ShapeDtypeStruct(dims, F32)


def vmem(number):
    return [pl.BlockSpec(memory_space=pltpu.VMEM)] * number


SMEM = pl.BlockSpec(memory_space=pltpu.SMEM)


def local(observed_real, observed_imag, weights, taps):
    ahead_rows, ahead_lanes, back_lanes, back_rows, twist = dft_tables()
    count = weights.shape[0]
    reach = taps.shape[0] - 1
    parts = lax.axis_size("chan")
    devices = lax.axis_size("tm") * parts
    blocks = shape(count, ROWS, LANES)
    groups = lax.axis_size("tm")
    position = lax.axis_index(AXES)
    keep = jnp.stack([position > 0, position < devices - 1, position % 2 == 1]).astype(F32)
    place = lax.axis_index("chan").astype(jnp.int32).reshape(1)
    keep_group = (lax.axis_index("tm") < groups - 1).astype(F32).reshape(1)
    tables = (ahead_rows, ahead_lanes, back_lanes, back_rows, twist)

    def neighbours(block):
        inside = [(i, i ^ 1) for i in range(devices)]
        across = [(i, min(max(((i + 1) ^ 1) - 1, 0), devices - 1)) for i in range(devices)]
        return lax.ppermute(block, AXES, inside), lax.ppermute(block, AXES, across)

    def exchange(value, axis):
        return lax.all_to_all(value, axis, split_axis=0, concat_axis=0, tiled=True)

    seed_inputs = (observed_real, observed_imag, weights, back_lanes, back_rows, twist)
    seed_inputs = tuple(pltpu.with_memory_space_constraint(v, pltpu.HBM) for v in seed_inputs)
    seeds = pl.pallas_call(
        seed_kernel,
        out_shape=blocks,
        in_specs=[pl.BlockSpec(memory_space=pltpu.HBM)] * 6,
        out_specs=vmem(1)[0],
        scratch_shapes=[pltpu.VMEM(value.shape, value.dtype) for value in seed_inputs]
        + [pltpu.VMEM((count * ROWS, LANES), F32), pltpu.SemaphoreType.DMA((6,))],
        compiler_params=params(),
        name="seed",
    )(*seed_inputs)
    inside, across = neighbours(seeds)
    weights, taps = pl.pallas_call(
        arrange_kernel,
        out_shape=(blocks, shape((reach + 1) * ROWS, LANES)),
        in_specs=vmem(2),
        out_specs=tuple(vmem(2)),
        scratch_shapes=[pltpu.VMEM((count * ROWS, LANES), F32)],
        compiler_params=params(),
        cost_estimate=pl.CostEstimate(flops=10**7, bytes_accessed=2 * 10**6, transcendentals=0),
        name="arrange",
    )(weights, taps)
    taps = taps.reshape(reach + 1, ROWS, LANES)

    images, side = pl.pallas_call(
        first_kernel,
        out_shape=(blocks, shape(reach + count, ROWS, LANES)),
        in_specs=[SMEM] + vmem(10),
        out_specs=tuple(vmem(2)),
        scratch_shapes=[pltpu.VMEM((count, ROWS, LANES), F32)],
        compiler_params=params(),
        name="first",
    )(keep, inside, seeds, across, taps, weights, *tables)
    inside, across = neighbours(images)

    outgoing = pl.pallas_call(
        second_kernel,
        out_shape=shape(parts, 3 * count + 1, 8, LANES),
        in_specs=[SMEM] + vmem(11),
        out_specs=vmem(1)[0],
        scratch_shapes=[
            pltpu.VMEM((count, ROWS, LANES), F32),
            pltpu.VMEM((3, 8, LANES), F32),
        ],
        compiler_params=params(),
        name="second",
    )(keep, inside, images, across, side, taps, weights, *tables)

    moved = exchange(outgoing, "chan")
    after, sums = pl.pallas_call(
        tail_kernel,
        out_shape=(shape(count, 8, LANES), shape(groups, 4, LANES)),
        in_specs=vmem(1),
        out_specs=tuple(vmem(2)),
        compiler_params=params(),
        name="tail",
    )(moved)
    after = lax.ppermute(after, "tm", [(i + 1, i) for i in range(groups - 1)])
    sums = exchange(sums, "tm")
    return pl.pallas_call(
        last_kernel,
        out_shape=(shape(parts * count, 8 * LANES), shape(parts * count, 8 * LANES)),
        in_specs=[SMEM, SMEM] + vmem(4),
        out_specs=tuple(vmem(2)),
        scratch_shapes=[
            pltpu.VMEM((parts * count * 8, LANES), F32),
            pltpu.VMEM((parts * count * 8, LANES), F32),
        ],
        compiler_params=params(),
        name="last",
    )(place, keep_group, moved, after, sums, taps)


def solution(mesh):
    placed = (P(AXES, None), P(AXES, None), P(AXES, None), P())
    return jax.shard_map(
        local,
        mesh=mesh,
        in_specs=placed,
        out_specs=(P("tm", "chan"), P("tm", "chan")),
        check_vma=False,
    )
```

```python
import functools
import math

import jax
import jax.numpy as jnp
import numpy as np
from jax import lax
from jax.experimental import pallas as pl
from jax.experimental.pallas import tpu as pltpu
from jax.sharding import PartitionSpec as P

RIDGE = 0.25
ROWS = 64
LANES = 128
CHUNK = 16
F32 = jnp.float32
BF16 = jnp.bfloat16
AXES = ("tm", "chan")
VMEM_BYTES = 16 * 1024 * 1024


def params(limit=VMEM_BYTES):
    return pltpu.CompilerParams(vmem_limit_bytes=limit)


def halves(table):
    high = table.astype(np.float32).astype(jnp.bfloat16)
    low = (table - high.astype(np.float64)).astype(np.float32).astype(jnp.bfloat16)
    return high, low


def dft_tables():
    n1 = np.arange(ROWS)
    n2 = np.arange(LANES)
    k1 = np.arange(ROWS)
    k2 = (2 * np.arange(32)[None, :] + np.arange(2)[:, None]).reshape(-1)
    first = 2.0 * np.pi * (n1[:, None] * k1[None, :] % ROWS) / ROWS
    back_rows = np.concatenate([np.cos(first), -np.sin(first)], 1)
    second = 2.0 * np.pi * (k2[:, None] * n2[None, :] % LANES) / LANES
    scale = 1.0 / math.sqrt(ROWS * ROWS)
    cos = (np.cos(second) * scale).reshape(2, 32, LANES)
    sin = (np.sin(second) * scale).reshape(2, 32, LANES)
    from_real = np.concatenate([cos, sin], 2)
    from_imag = np.concatenate([-sin, cos], 2)
    back_lanes = np.stack([from_real, from_imag], 1).reshape(LANES, 2 * LANES)
    rows_high, rows_low = halves(back_rows)
    lanes_high, lanes_low = halves(back_lanes)
    twist = 2.0 * np.pi * k1[:, None] * n2[None, :] / (ROWS * LANES)
    return (
        np.concatenate([rows_high.T, rows_high.T, rows_low.T], 1),
        np.concatenate([lanes_high.T, lanes_low.T], 1),
        np.concatenate([lanes_high, lanes_high, lanes_low], 0),
        np.block([[rows_high, rows_high], [rows_low, np.zeros_like(rows_low)]]),
        np.stack([np.cos(twist), np.sin(twist)]).astype(np.float32),
    )


def split(value):
    high = value.astype(BF16)
    low = (value - high.astype(F32)).astype(BF16)
    return high, low


def dot(left, right):
    return jnp.dot(left, right, preferred_element_type=F32)


def forward_chunk(frames, ahead_rows, ahead_lanes, cos, sin):
    high, low = split(jnp.concatenate(frames, 1))
    mixed = dot(ahead_rows, jnp.concatenate([high, low, high], 0))
    turned = []
    for f in range(len(frames)):
        real = mixed[:ROWS, f * LANES : (f + 1) * LANES]
        imag = mixed[ROWS:, f * LANES : (f + 1) * LANES]
        turned.append(jnp.concatenate([real * cos + imag * sin, imag * cos - real * sin], 1))
    high, low = split(jnp.concatenate(turned, 0))
    wide = dot(high, ahead_lanes)
    return wide[:, :LANES] + wide[:, LANES:] + dot(low, ahead_lanes[:, :LANES])


def backward_chunk(spectra, back_lanes, back_rows, cos, sin):
    high, low = split(spectra)
    mixed = dot(jnp.concatenate([high, low, high], 1), back_lanes)
    turned = []
    for f in range(spectra.shape[0] // ROWS):
        real = mixed[f * ROWS : (f + 1) * ROWS, :LANES]
        imag = mixed[f * ROWS : (f + 1) * ROWS, LANES:]
        turned.append(jnp.concatenate([real * cos - imag * sin, real * sin + imag * cos], 0))
    high, low = split(jnp.concatenate(turned, 1))
    tall = dot(back_rows, jnp.concatenate([high, low], 0))
    return tall[:ROWS] + tall[ROWS:]


def turn_pair(block):
    flipped = block.T
    low_half = flipped[:ROWS]
    high_half = flipped[ROWS:]
    left = lax.broadcasted_iota(jnp.int32, (ROWS, LANES), 1) < ROWS
    return (
        jnp.where(left, low_half, pltpu.roll(high_half, ROWS, 1)),
        jnp.where(left, pltpu.roll(low_half, ROWS, 1), high_half),
    )


def seed_kernel(*refs):
    sources, out_ref, places, held, semaphore = refs[:6], refs[6], refs[7:13], refs[13], refs[14]
    copies = [
        pltpu.make_async_copy(source, place, semaphore.at[at])
        for at, (source, place) in enumerate(zip(sources, places))
    ]
    for copy in copies:
        copy.start()
    real_ref, imag_ref, weights_ref, back_lanes_ref, back_rows_ref, twist_ref = places
    count = real_ref.shape[0]
    for copy in copies:
        copy.wait()
    for j in range(32):
        columns = slice(j * LANES, (j + 1) * LANES)
        weights = weights_ref[:, columns]
        held[pl.ds(j, count, stride=ROWS), :] = weights * real_ref[:, columns]
        held[pl.ds(32 + j, count, stride=ROWS), :] = weights * imag_ref[:, columns]
    cos = twist_ref[0]
    sin = twist_ref[1]
    for start in range(0, count, CHUNK):
        spectra = []
        for f in range(start, start + CHUNK, 2):
            spectra += turn_pair(held[f * ROWS : (f + 2) * ROWS, :])
        frames = backward_chunk(
            jnp.concatenate(spectra, 0), back_lanes_ref[...], back_rows_ref[...], cos, sin
        )
        for f in range(CHUNK):
            out_ref[start + f] = frames[:, f * LANES : (f + 1) * LANES]


def arrange_kernel(weights_ref, taps_ref, weights_out, taps_out, held):
    count = weights_ref.shape[0]
    for j in range(32):
        weights = weights_ref[:, j * LANES : (j + 1) * LANES]
        held[pl.ds(j, count, stride=ROWS), :] = weights
        held[pl.ds(32 + j, count, stride=ROWS), :] = weights
    for f in range(0, count, 2):
        first, second = turn_pair(held[f * ROWS : (f + 2) * ROWS, :])
        weights_out[f] = first
        weights_out[f + 1] = second
    for n1 in range(ROWS):
        taps_out[pl.ds(n1, taps_ref.shape[0], stride=ROWS), :] = taps_ref[
            :, n1 * LANES : (n1 + 1) * LANES
        ]


def weighted_sum(taps, values):
    total = taps[0] * values[0]
    for tap, value in zip(taps[1:], values[1:]):
        total = total + tap * value
    return total


def back_filter(rows, taps, inside_ref, here_ref, across_ref, keep):
    reach = len(taps) - 1
    count = here_ref.shape[0]
    odd = jnp.full((8, LANES), keep[2]) > 0.5
    frames = [
        jnp.where(odd, inside_ref[t, rows, :], across_ref[t, rows, :]) for t in range(count - reach, count)
    ]
    frames += [here_ref[t, rows, :] for t in range(count)]
    frames += [
        jnp.where(odd, across_ref[t, rows, :], inside_ref[t, rows, :]) * keep[1] for t in range(reach)
    ]
    result = []
    for at in range(reach + count):
        total = weighted_sum(taps, frames[at : at + reach + 1])
        result.append(total * keep[0] if at < reach else total)
    return result


def ahead_filter(taps, frames):
    reach = len(taps) - 1
    return [
        weighted_sum(taps, [frames[at + reach - tap] for tap in range(reach + 1)])
        for at in range(len(frames) - reach)
    ]


def first_kernel(
    keep_ref, inside_ref, here_ref, across_ref, taps_ref, weights_ref,
    ahead_rows_ref, ahead_lanes_ref, back_lanes_ref, back_rows_ref, twist_ref,
    out_ref, side_ref, filtered,
):
    count = here_ref.shape[0]
    keep = (keep_ref[0], keep_ref[1], keep_ref[2])

    @pl.loop(0, ROWS // 8)
    def _(group):
        rows = pl.ds(pl.multiple_of(group * 8, 8), 8)
        taps = [taps_ref[p, rows, :] for p in range(taps_ref.shape[0])]
        side = back_filter(rows, taps, inside_ref, here_ref, across_ref, keep)
        for at, value in enumerate(side):
            side_ref[at, rows, :] = value
        for at, value in enumerate(ahead_filter(taps, side)):
            filtered[at, rows, :] = value

    cos = twist_ref[0]
    sin = twist_ref[1]
    for start in range(0, count, CHUNK):
        spectra = forward_chunk(
            [filtered[start + f] for f in range(CHUNK)], ahead_rows_ref[...], ahead_lanes_ref[...], cos, sin
        )
        weights = weights_ref[start : start + CHUNK].reshape(CHUNK * ROWS, LANES)
        frames = backward_chunk(spectra * weights, back_lanes_ref[...], back_rows_ref[...], cos, sin)
        for f in range(CHUNK):
            out_ref[start + f] = frames[:, f * LANES : (f + 1) * LANES]


def quarters(rows):
    return lax.broadcasted_iota(jnp.int32, (rows, LANES), 1) // 32


def pack(values):
    packed = jnp.zeros((8, LANES), F32)
    for at, value in enumerate(values):
        value = value + pltpu.roll(value, 64, 1)
        value = value + pltpu.roll(value, 32, 1)
        packed = jnp.where(quarters(8) == at, value, packed)
    return packed


def second_kernel(
    keep_ref, inside_ref, here_ref, across_ref, side_ref, taps_ref, weights_ref,
    ahead_rows_ref, ahead_lanes_ref, back_lanes_ref, back_rows_ref, twist_ref,
    out_ref, filtered, sums,
):
    count = here_ref.shape[0]
    keep = (keep_ref[0], keep_ref[1], keep_ref[2])
    reach = taps_ref.shape[0] - 1
    sums[...] = jnp.zeros_like(sums)

    @pl.loop(0, ROWS // 8)
    def _(group):
        rows = pl.ds(pl.multiple_of(group * 8, 8), 8)
        taps = [taps_ref[p, rows, :] for p in range(reach + 1)]
        image = back_filter(rows, taps, inside_ref, here_ref, across_ref, keep)
        side = [side_ref[at, rows, :] for at in range(reach + count)]
        image = [value + RIDGE * base for value, base in zip(image, side)]
        for at, value in enumerate(ahead_filter(taps, image)):
            filtered[at, rows, :] = value
        first, second, third = sums[0], sums[1], sums[2]
        for at in range(count):
            base = side[reach + at]
            value = image[reach + at]
            out_ref[group, at] = base
            out_ref[group, count + at] = value
            first = first + base * base
            second = second + base * value
            third = third + value * value
        sums[0] = first
        sums[1] = second
        sums[2] = third

    cos = twist_ref[0]
    sin = twist_ref[1]
    power = jnp.zeros((8, LANES), F32)
    for start in range(0, count, CHUNK):
        spectra = forward_chunk(
            [filtered[start + f] for f in range(CHUNK)], ahead_rows_ref[...], ahead_lanes_ref[...], cos, sin
        )
        weights = weights_ref[start : start + CHUNK].reshape(CHUNK * ROWS, LANES)
        weighted = spectra * weights
        power = power + jnp.sum((weighted * spectra).reshape(CHUNK * ROWS // 8, 8, LANES), 0)
        frames = backward_chunk(weighted, back_lanes_ref[...], back_rows_ref[...], cos, sin)
        for f in range(CHUNK):
            for group in range(ROWS // 8):
                out_ref[group, 2 * count + start + f] = frames[
                    group * 8 : (group + 1) * 8, f * LANES : (f + 1) * LANES
                ]
    totals = pack([sums[0], sums[1], sums[2], power])
    for group in range(ROWS // 8):
        out_ref[group, 3 * count] = totals


def tail_kernel(moved_ref, frames_ref, sums_ref):
    count = frames_ref.shape[0]
    frames_ref[...] = moved_ref[0, 2 * count : 3 * count]
    total = moved_ref[0, 3 * count]
    for part in range(1, moved_ref.shape[0]):
        total = total + moved_ref[part, 3 * count]
    sums_ref[...] = jnp.broadcast_to((total[:4] + total[4:])[None], sums_ref.shape)


def local_taps(place_ref, taps_ref):
    rows = pl.ds(pl.multiple_of(place_ref[0] * 8, 8), 8)
    return [taps_ref[p, rows, :] for p in range(taps_ref.shape[0])]


def to_rows(held, out_ref, first, frames):
    for block in range(frames // 8):
        for n1 in range(8):
            places = pl.ds(block * 64 + n1, 8, stride=8)
            columns = slice(n1 * LANES, (n1 + 1) * LANES)
            out_ref[first + block * 8 : first + (block + 1) * 8, columns] = held[places, :]


def prepare_kernel(place_ref, moved_ref, taps_ref, base_ref, image_ref, again_ref, base_held, image_held, again_held):
    parts = moved_ref.shape[0]
    count = (moved_ref.shape[1] - 1) // 3
    taps = local_taps(place_ref, taps_ref)
    reach = len(taps) - 1

    @pl.loop(0, parts)
    def _(part):
        for at in range(count):
            here = pl.ds(pl.multiple_of((part * count + at) * 8, 8), 8)
            base_held[here, :] = moved_ref[part, at]
            image_held[here, :] = moved_ref[part, count + at]

    @pl.loop(0, parts - 1)
    def _(part):
        frames = [moved_ref[part, 2 * count + t] for t in range(count)]
        frames += [moved_ref[part + 1, 2 * count + t] for t in range(reach)]
        for at in range(count):
            here = pl.ds(pl.multiple_of((part * count + at) * 8, 8), 8)
            again_held[here, :] = weighted_sum(taps, frames[at : at + reach + 1])

    to_rows(base_held, base_ref, 0, parts * count)
    to_rows(image_held, image_ref, 0, parts * count)
    to_rows(again_held, again_ref, 0, (parts - 1) * count)


def last_kernel(
    place_ref, keep_ref, moved_ref, base_ref, image_ref, again_ref, after_ref, sums_ref, taps_ref,
    solution_ref, residual_ref, held, rest, fetched, semaphore,
):
    copy = pltpu.make_async_copy(again_ref, fetched, semaphore)
    copy.start()
    parts = moved_ref.shape[0]
    count = (moved_ref.shape[1] - 1) // 3
    taps = local_taps(place_ref, taps_ref)
    reach = len(taps) - 1
    frames = [moved_ref[parts - 1, 2 * count + t] for t in range(count)]
    frames += [after_ref[t] * keep_ref[0] for t in range(reach)]
    for at in range(count):
        held[at * 8 : (at + 1) * 8, :] = weighted_sum(taps, frames[at : at + reach + 1])
    to_rows(held, rest, 0, count)
    sums = jnp.sum(sums_ref[...], 0)
    norm, curve, square, power = (
        jnp.sum(jnp.sum(jnp.where(quarters(4) == at, sums, 0.0), 1, keepdims=True), 0, keepdims=True)
        for at in range(4)
    )
    cube = power + RIDGE * square
    step = norm / curve
    next_norm = step * step * square - norm
    grown = step * square / curve
    next_step = next_norm / (step * (step * cube - grown * square))
    to_base = step + next_step * grown
    to_image = -(next_step * step)
    cube_rate = next_step * step
    image_rate = RIDGE * cube_rate - (step + next_step * grown)
    to_base, to_image, image_rate, cube_rate = (
        jnp.broadcast_to(value, (8, 8 * LANES)) for value in (to_base, to_image, image_rate, cube_rate)
    )

    def finish(rows, again):
        base = base_ref[rows, :]
        image = image_ref[rows, :]
        solution_ref[rows, :] = to_base * base + to_image * image
        residual_ref[rows, :] = base + image_rate * image + cube_rate * again

    for block in range(count // 8):
        finish(pl.ds((parts - 1) * count + block * 8, 8), rest[block * 8 : (block + 1) * 8, :])
    copy.wait()

    @pl.loop(0, (parts - 1) * count // 8)
    def _(block):
        rows = pl.ds(pl.multiple_of(block * 8, 8), 8)
        finish(rows, fetched[rows, :])


def shape(*dims):
    return jax.ShapeDtypeStruct(dims, F32)


def vmem(number):
    return [pl.BlockSpec(memory_space=pltpu.VMEM)] * number


SMEM = pl.BlockSpec(memory_space=pltpu.SMEM)
HBM = pl.BlockSpec(memory_space=pltpu.HBM)


def local(observed_real, observed_imag, weights, taps):
    ahead_rows, ahead_lanes, back_lanes, back_rows, twist = dft_tables()
    count = weights.shape[0]
    reach = taps.shape[0] - 1
    parts = lax.axis_size("chan")
    devices = lax.axis_size("tm") * parts
    blocks = shape(count, ROWS, LANES)
    groups = lax.axis_size("tm")
    position = lax.axis_index(AXES)
    keep = jnp.stack([position > 0, position < devices - 1, position % 2 == 1]).astype(F32)
    place = lax.axis_index("chan").astype(jnp.int32).reshape(1)
    keep_group = (lax.axis_index("tm") < groups - 1).astype(F32).reshape(1)
    tables = (ahead_rows, ahead_lanes, back_lanes, back_rows, twist)

    def neighbours(block):
        inside = [(i, i ^ 1) for i in range(devices)]
        across = [(i, min(max(((i + 1) ^ 1) - 1, 0), devices - 1)) for i in range(devices)]
        return lax.ppermute(block, AXES, inside), lax.ppermute(block, AXES, across)

    def exchange(value, axis):
        return lax.all_to_all(value, axis, split_axis=0, concat_axis=0, tiled=True)

    seed_inputs = (observed_real, observed_imag, weights, back_lanes, back_rows, twist)
    seed_inputs = tuple(pltpu.with_memory_space_constraint(v, pltpu.HBM) for v in seed_inputs)
    seeds = pl.pallas_call(
        seed_kernel,
        out_shape=blocks,
        in_specs=[pl.BlockSpec(memory_space=pltpu.HBM)] * 6,
        out_specs=vmem(1)[0],
        scratch_shapes=[pltpu.VMEM(value.shape, value.dtype) for value in seed_inputs]
        + [pltpu.VMEM((count * ROWS, LANES), F32), pltpu.SemaphoreType.DMA((6,))],
        compiler_params=params(),
        name="seed",
    )(*seed_inputs)
    inside, across = neighbours(seeds)
    weights, taps = pl.pallas_call(
        arrange_kernel,
        out_shape=(blocks, shape((reach + 1) * ROWS, LANES)),
        in_specs=vmem(2),
        out_specs=tuple(vmem(2)),
        scratch_shapes=[pltpu.VMEM((count * ROWS, LANES), F32)],
        compiler_params=params(),
        cost_estimate=pl.CostEstimate(flops=10**7, bytes_accessed=2 * 10**6, transcendentals=0),
        name="arrange",
    )(weights, taps)
    taps = taps.reshape(reach + 1, ROWS, LANES)

    images, side = pl.pallas_call(
        first_kernel,
        out_shape=(blocks, shape(reach + count, ROWS, LANES)),
        in_specs=[SMEM] + vmem(10),
        out_specs=tuple(vmem(2)),
        scratch_shapes=[pltpu.VMEM((count, ROWS, LANES), F32)],
        compiler_params=params(),
        name="first",
    )(keep, inside, seeds, across, taps, weights, *tables)
    inside, across = neighbours(images)

    outgoing = pl.pallas_call(
        second_kernel,
        out_shape=shape(parts, 3 * count + 1, 8, LANES),
        in_specs=[SMEM] + vmem(11),
        out_specs=vmem(1)[0],
        scratch_shapes=[
            pltpu.VMEM((count, ROWS, LANES), F32),
            pltpu.VMEM((3, 8, LANES), F32),
        ],
        compiler_params=params(),
        name="second",
    )(keep, inside, images, across, side, taps, weights, *tables)

    moved = exchange(outgoing, "chan")
    after, sums = pl.pallas_call(
        tail_kernel,
        out_shape=(shape(count, 8, LANES), shape(groups, 4, LANES)),
        in_specs=vmem(1),
        out_specs=tuple(vmem(2)),
        compiler_params=params(),
        name="tail",
    )(moved)
    after = lax.ppermute(after, "tm", [(i + 1, i) for i in range(groups - 1)])
    sums = exchange(sums, "tm")
    whole = shape(parts * count, 8 * LANES)
    base, image, again = pl.pallas_call(
        prepare_kernel,
        out_shape=(whole, whole, shape((parts - 1) * count, 8 * LANES)),
        in_specs=[SMEM] + vmem(2),
        out_specs=tuple(vmem(3)),
        scratch_shapes=[pltpu.VMEM((parts * count * 8, LANES), F32)] * 3,
        compiler_params=params(),
        cost_estimate=pl.CostEstimate(flops=10**7, bytes_accessed=3 * 10**6, transcendentals=0),
        name="prepare",
    )(place, moved, taps)
    again = pltpu.with_memory_space_constraint(again, pltpu.HBM)
    return pl.pallas_call(
        last_kernel,
        out_shape=(whole, whole),
        in_specs=[SMEM, SMEM] + vmem(3) + [HBM] + vmem(3),
        out_specs=tuple(vmem(2)),
        scratch_shapes=[
            pltpu.VMEM((count * 8, LANES), F32),
            pltpu.VMEM((count, 8 * LANES), F32),
            pltpu.VMEM(again.shape, F32),
            pltpu.SemaphoreType.DMA,
        ],
        compiler_params=params(),
        name="last",
    )(place, keep_group, moved, base, image, again, after, sums, taps)


def solution(mesh):
    placed = (P(AXES, None), P(AXES, None), P(AXES, None), P())
    return jax.shard_map(
        local,
        mesh=mesh,
        in_specs=placed,
        out_specs=(P("tm", "chan"), P("tm", "chan")),
        check_vma=False,
    )
```

```python
import functools
import math

import jax
import jax.numpy as jnp
import numpy as np
from jax import lax
from jax.experimental import pallas as pl
from jax.experimental.pallas import tpu as pltpu
from jax.sharding import PartitionSpec as P

RIDGE = 0.25
ROWS = 64
LANES = 128
CHUNK = 16
F32 = jnp.float32
BF16 = jnp.bfloat16
AXES = ("tm", "chan")
VMEM_BYTES = 16 * 1024 * 1024


def params(limit=VMEM_BYTES):
    return pltpu.CompilerParams(vmem_limit_bytes=limit)


def halves(table):
    high = table.astype(np.float32).astype(jnp.bfloat16)
    low = (table - high.astype(np.float64)).astype(np.float32).astype(jnp.bfloat16)
    return high, low


def dft_tables():
    n1 = np.arange(ROWS)
    n2 = np.arange(LANES)
    k1 = np.arange(ROWS)
    k2 = (2 * np.arange(32)[None, :] + np.arange(2)[:, None]).reshape(-1)
    first = 2.0 * np.pi * (n1[:, None] * k1[None, :] % ROWS) / ROWS
    back_rows = np.concatenate([np.cos(first), -np.sin(first)], 1)
    second = 2.0 * np.pi * (k2[:, None] * n2[None, :] % LANES) / LANES
    scale = 1.0 / math.sqrt(ROWS * ROWS)
    cos = (np.cos(second) * scale).reshape(2, 32, LANES)
    sin = (np.sin(second) * scale).reshape(2, 32, LANES)
    from_real = np.concatenate([cos, sin], 2)
    from_imag = np.concatenate([-sin, cos], 2)
    back_lanes = np.stack([from_real, from_imag], 1).reshape(LANES, 2 * LANES)
    rows_high, rows_low = halves(back_rows)
    lanes_high, lanes_low = halves(back_lanes)
    twist = 2.0 * np.pi * k1[:, None] * n2[None, :] / (ROWS * LANES)
    return (
        np.concatenate([rows_high.T, rows_high.T, rows_low.T], 1),
        np.concatenate([lanes_high.T, lanes_low.T], 1),
        np.concatenate([lanes_high, lanes_high, lanes_low], 0),
        np.block([[rows_high, rows_high], [rows_low, np.zeros_like(rows_low)]]),
        np.stack([np.cos(twist), np.sin(twist)]).astype(np.float32),
    )


def split(value):
    high = value.astype(BF16)
    low = (value - high.astype(F32)).astype(BF16)
    return high, low


def dot(left, right):
    return jnp.dot(left, right, preferred_element_type=F32)


def forward_chunk(frames, ahead_rows, ahead_lanes, cos, sin):
    high, low = split(jnp.concatenate(frames, 1))
    mixed = dot(ahead_rows, jnp.concatenate([high, low, high], 0))
    turned = []
    for f in range(len(frames)):
        real = mixed[:ROWS, f * LANES : (f + 1) * LANES]
        imag = mixed[ROWS:, f * LANES : (f + 1) * LANES]
        turned.append(jnp.concatenate([real * cos + imag * sin, imag * cos - real * sin], 1))
    high, low = split(jnp.concatenate(turned, 0))
    wide = dot(high, ahead_lanes)
    return wide[:, :LANES] + wide[:, LANES:] + dot(low, ahead_lanes[:, :LANES])


def backward_chunk(spectra, back_lanes, back_rows, cos, sin):
    high, low = split(spectra)
    mixed = dot(jnp.concatenate([high, low, high], 1), back_lanes)
    turned = []
    for f in range(spectra.shape[0] // ROWS):
        real = mixed[f * ROWS : (f + 1) * ROWS, :LANES]
        imag = mixed[f * ROWS : (f + 1) * ROWS, LANES:]
        turned.append(jnp.concatenate([real * cos - imag * sin, real * sin + imag * cos], 0))
    high, low = split(jnp.concatenate(turned, 1))
    tall = dot(back_rows, jnp.concatenate([high, low], 0))
    return tall[:ROWS] + tall[ROWS:]


def turn_pair(block):
    flipped = block.T
    low_half = flipped[:ROWS]
    high_half = flipped[ROWS:]
    left = lax.broadcasted_iota(jnp.int32, (ROWS, LANES), 1) < ROWS
    return (
        jnp.where(left, low_half, pltpu.roll(high_half, ROWS, 1)),
        jnp.where(left, pltpu.roll(low_half, ROWS, 1), high_half),
    )


def seed_kernel(*refs):
    sources, out_ref, places, held, semaphore = refs[:6], refs[6], refs[7:13], refs[13], refs[14]
    copies = [
        pltpu.make_async_copy(source, place, semaphore.at[at])
        for at, (source, place) in enumerate(zip(sources, places))
    ]
    for copy in copies:
        copy.start()
    real_ref, imag_ref, weights_ref, back_lanes_ref, back_rows_ref, twist_ref = places
    count = real_ref.shape[0]
    for copy in copies:
        copy.wait()
    for j in range(32):
        columns = slice(j * LANES, (j + 1) * LANES)
        weights = weights_ref[:, columns]
        held[pl.ds(j, count, stride=ROWS), :] = weights * real_ref[:, columns]
        held[pl.ds(32 + j, count, stride=ROWS), :] = weights * imag_ref[:, columns]
    cos = twist_ref[0]
    sin = twist_ref[1]
    for start in range(0, count, CHUNK):
        spectra = []
        for f in range(start, start + CHUNK, 2):
            spectra += turn_pair(held[f * ROWS : (f + 2) * ROWS, :])
        frames = backward_chunk(
            jnp.concatenate(spectra, 0), back_lanes_ref[...], back_rows_ref[...], cos, sin
        )
        for f in range(CHUNK):
            out_ref[start + f] = frames[:, f * LANES : (f + 1) * LANES]


def arrange_kernel(weights_ref, taps_ref, weights_out, taps_out, held):
    count = weights_ref.shape[0]
    for j in range(32):
        weights = weights_ref[:, j * LANES : (j + 1) * LANES]
        held[pl.ds(j, count, stride=ROWS), :] = weights
        held[pl.ds(32 + j, count, stride=ROWS), :] = weights
    for f in range(0, count, 2):
        first, second = turn_pair(held[f * ROWS : (f + 2) * ROWS, :])
        weights_out[f] = first
        weights_out[f + 1] = second
    for n1 in range(ROWS):
        taps_out[pl.ds(n1, taps_ref.shape[0], stride=ROWS), :] = taps_ref[
            :, n1 * LANES : (n1 + 1) * LANES
        ]


def weighted_sum(taps, values):
    total = taps[0] * values[0]
    for tap, value in zip(taps[1:], values[1:]):
        total = total + tap * value
    return total


def back_filter(rows, taps, inside_ref, here_ref, across_ref, keep):
    reach = len(taps) - 1
    count = here_ref.shape[0]
    odd = jnp.full((8, LANES), keep[2]) > 0.5
    frames = [
        jnp.where(odd, inside_ref[t, rows, :], across_ref[t, rows, :]) for t in range(count - reach, count)
    ]
    frames += [here_ref[t, rows, :] for t in range(count)]
    frames += [
        jnp.where(odd, across_ref[t, rows, :], inside_ref[t, rows, :]) * keep[1] for t in range(reach)
    ]
    result = []
    for at in range(reach + count):
        total = weighted_sum(taps, frames[at : at + reach + 1])
        result.append(total * keep[0] if at < reach else total)
    return result


def ahead_filter(taps, frames):
    reach = len(taps) - 1
    return [
        weighted_sum(taps, [frames[at + reach - tap] for tap in range(reach + 1)])
        for at in range(len(frames) - reach)
    ]


def first_kernel(
    keep_ref, inside_ref, here_ref, across_ref, taps_ref, weights_ref,
    ahead_rows_ref, ahead_lanes_ref, back_lanes_ref, back_rows_ref, twist_ref,
    out_ref, side_ref, filtered,
):
    count = here_ref.shape[0]
    keep = (keep_ref[0], keep_ref[1], keep_ref[2])

    @pl.loop(0, ROWS // 8)
    def _(group):
        rows = pl.ds(pl.multiple_of(group * 8, 8), 8)
        taps = [taps_ref[p, rows, :] for p in range(taps_ref.shape[0])]
        side = back_filter(rows, taps, inside_ref, here_ref, across_ref, keep)
        for at, value in enumerate(side):
            side_ref[at, rows, :] = value
        for at, value in enumerate(ahead_filter(taps, side)):
            filtered[at, rows, :] = value

    cos = twist_ref[0]
    sin = twist_ref[1]
    for start in range(0, count, CHUNK):
        spectra = forward_chunk(
            [filtered[start + f] for f in range(CHUNK)], ahead_rows_ref[...], ahead_lanes_ref[...], cos, sin
        )
        weights = weights_ref[start : start + CHUNK].reshape(CHUNK * ROWS, LANES)
        frames = backward_chunk(spectra * weights, back_lanes_ref[...], back_rows_ref[...], cos, sin)
        for f in range(CHUNK):
            out_ref[start + f] = frames[:, f * LANES : (f + 1) * LANES]


def quarters(rows):
    return lax.broadcasted_iota(jnp.int32, (rows, LANES), 1) // 32


def pack(values):
    packed = jnp.zeros((8, LANES), F32)
    for at, value in enumerate(values):
        value = value + pltpu.roll(value, 64, 1)
        value = value + pltpu.roll(value, 32, 1)
        packed = jnp.where(quarters(8) == at, value, packed)
    return packed


def second_kernel(
    place_ref, keep_ref, inside_ref, here_ref, across_ref, side_ref, taps_ref, weights_ref,
    ahead_rows_ref, ahead_lanes_ref, back_lanes_ref, back_rows_ref, twist_ref,
    out_ref, *rest,
):
    lanes, (filtered, sums, staged, semaphore) = rest[:8], rest[8:]
    copies = [
        pltpu.make_async_copy(staged.at[d], lane, semaphore.at[d]) for d, lane in enumerate(lanes)
    ]
    count = here_ref.shape[0]
    keep = (keep_ref[0], keep_ref[1], keep_ref[2])
    reach = taps_ref.shape[0] - 1
    sums[...] = jnp.zeros_like(sums)

    @pl.loop(0, ROWS // 8)
    def _(group):
        rows = pl.ds(pl.multiple_of(group * 8, 8), 8)
        taps = [taps_ref[p, rows, :] for p in range(reach + 1)]
        image = back_filter(rows, taps, inside_ref, here_ref, across_ref, keep)
        side = [side_ref[at, rows, :] for at in range(reach + count)]
        image = [value + RIDGE * base for value, base in zip(image, side)]
        for at, value in enumerate(ahead_filter(taps, image)):
            filtered[at, rows, :] = value
        first, second, third = sums[0], sums[1], sums[2]
        for at in range(count):
            base = side[reach + at]
            value = image[reach + at]
            staged[group ^ place_ref[0], at] = base
            staged[group ^ place_ref[0], count + at] = value
            first = first + base * base
            second = second + base * value
            third = third + value * value
        sums[0] = first
        sums[1] = second
        sums[2] = third

    for copy in copies:
        copy.start()
    cos = twist_ref[0]
    sin = twist_ref[1]
    power = jnp.zeros((8, LANES), F32)
    for start in range(0, count, CHUNK):
        spectra = forward_chunk(
            [filtered[start + f] for f in range(CHUNK)], ahead_rows_ref[...], ahead_lanes_ref[...], cos, sin
        )
        weights = weights_ref[start : start + CHUNK].reshape(CHUNK * ROWS, LANES)
        weighted = spectra * weights
        power = power + jnp.sum((weighted * spectra).reshape(CHUNK * ROWS // 8, 8, LANES), 0)
        frames = backward_chunk(weighted, back_lanes_ref[...], back_rows_ref[...], cos, sin)
        for f in range(CHUNK):
            for group in range(ROWS // 8):
                out_ref[group, start + f] = frames[
                    group * 8 : (group + 1) * 8, f * LANES : (f + 1) * LANES
                ]
    totals = pack([sums[0], sums[1], sums[2], power])
    for group in range(ROWS // 8):
        out_ref[group, count] = totals
    for copy in copies:
        copy.wait()


def tail_kernel(moved_ref, frames_ref, sums_ref):
    count = frames_ref.shape[0]
    frames_ref[...] = moved_ref[0, :count]
    total = moved_ref[0, count]
    for part in range(1, moved_ref.shape[0]):
        total = total + moved_ref[part, count]
    sums_ref[...] = jnp.broadcast_to((total[:4] + total[4:])[None], sums_ref.shape)


def last_kernel(place_ref, keep_ref, moved_ref, after_ref, sums_ref, taps_ref, *rest):
    lanes, (solution_ref, residual_ref, kept, left, pairs) = rest[:8], rest[8:]
    parts, count = moved_ref.shape[0], moved_ref.shape[1] - 1
    reach = taps_ref.shape[0] - 1
    rows = pl.ds(pl.multiple_of(place_ref[0] * 8, 8), 8)
    for d, lane in enumerate(lanes):
        pairs[place_ref[0] ^ d] = lane[...]
    sums = jnp.sum(sums_ref[...], 0)
    norm, curve, square, power = (
        jnp.sum(jnp.sum(jnp.where(quarters(4) == at, sums, 0.0), 1, keepdims=True), 0, keepdims=True)
        for at in range(4)
    )
    cube = power + RIDGE * square
    step = norm / curve
    next_norm = step * step * square - norm
    grown = step * square / curve
    next_step = next_norm / (step * (step * cube - grown * square))
    to_base = step + next_step * grown
    to_image = -(next_step * step)
    image_rate = -(step + next_step * grown)
    cube_rate = next_step * step
    to_base, to_image, image_rate, cube_rate = (
        jnp.broadcast_to(value, (8, LANES)) for value in (to_base, to_image, image_rate, cube_rate)
    )
    taps = [taps_ref[p, rows, :] for p in range(reach + 1)]

    def finish(part, tail):
        frames = [moved_ref[part, t] for t in range(count)] + tail
        for at in range(count):
            base = pairs[part, at]
            image = pairs[part, count + at]
            again = weighted_sum(taps, frames[at : at + reach + 1]) + RIDGE * image
            here = pl.ds(pl.multiple_of((part * count + at) * 8, 8), 8)
            kept[here, :] = to_base * base + to_image * image
            left[here, :] = base + image_rate * image + cube_rate * again

    @pl.loop(0, parts - 1)
    def _(part):
        finish(part, [moved_ref[part + 1, t] for t in range(reach)])

    finish(parts - 1, [after_ref[t] * keep_ref[0] for t in range(reach)])

    for block in range(parts * count // 8):
        for n1 in range(8):
            places = pl.ds(block * 64 + n1, 8, stride=8)
            columns = slice(n1 * LANES, (n1 + 1) * LANES)
            solution_ref[block * 8 : (block + 1) * 8, columns] = kept[places, :]
            residual_ref[block * 8 : (block + 1) * 8, columns] = left[places, :]


def shape(*dims):
    return jax.ShapeDtypeStruct(dims, F32)


def vmem(number):
    return [pl.BlockSpec(memory_space=pltpu.VMEM)] * number


SMEM = pl.BlockSpec(memory_space=pltpu.SMEM)


def local(observed_real, observed_imag, weights, taps):
    ahead_rows, ahead_lanes, back_lanes, back_rows, twist = dft_tables()
    count = weights.shape[0]
    reach = taps.shape[0] - 1
    parts = lax.axis_size("chan")
    devices = lax.axis_size("tm") * parts
    blocks = shape(count, ROWS, LANES)
    groups = lax.axis_size("tm")
    position = lax.axis_index(AXES)
    keep = jnp.stack([position > 0, position < devices - 1, position % 2 == 1]).astype(F32)
    place = lax.axis_index("chan").astype(jnp.int32).reshape(1)
    keep_group = (lax.axis_index("tm") < groups - 1).astype(F32).reshape(1)
    tables = (ahead_rows, ahead_lanes, back_lanes, back_rows, twist)

    def neighbours(block):
        inside = [(i, i ^ 1) for i in range(devices)]
        across = [(i, min(max(((i + 1) ^ 1) - 1, 0), devices - 1)) for i in range(devices)]
        return lax.ppermute(block, AXES, inside), lax.ppermute(block, AXES, across)

    def exchange(value, axis):
        return lax.all_to_all(value, axis, split_axis=0, concat_axis=0, tiled=True)

    seed_inputs = (observed_real, observed_imag, weights, back_lanes, back_rows, twist)
    seed_inputs = tuple(pltpu.with_memory_space_constraint(v, pltpu.HBM) for v in seed_inputs)
    seeds = pl.pallas_call(
        seed_kernel,
        out_shape=blocks,
        in_specs=[pl.BlockSpec(memory_space=pltpu.HBM)] * 6,
        out_specs=vmem(1)[0],
        scratch_shapes=[pltpu.VMEM(value.shape, value.dtype) for value in seed_inputs]
        + [pltpu.VMEM((count * ROWS, LANES), F32), pltpu.SemaphoreType.DMA((6,))],
        compiler_params=params(),
        name="seed",
    )(*seed_inputs)
    inside, across = neighbours(seeds)
    weights, taps = pl.pallas_call(
        arrange_kernel,
        out_shape=(blocks, shape((reach + 1) * ROWS, LANES)),
        in_specs=vmem(2),
        out_specs=tuple(vmem(2)),
        scratch_shapes=[pltpu.VMEM((count * ROWS, LANES), F32)],
        compiler_params=params(),
        cost_estimate=pl.CostEstimate(flops=10**7, bytes_accessed=2 * 10**6, transcendentals=0),
        name="arrange",
    )(weights, taps)
    taps = taps.reshape(reach + 1, ROWS, LANES)

    images, side = pl.pallas_call(
        first_kernel,
        out_shape=(blocks, shape(reach + count, ROWS, LANES)),
        in_specs=[SMEM] + vmem(10),
        out_specs=tuple(vmem(2)),
        scratch_shapes=[pltpu.VMEM((count, ROWS, LANES), F32)],
        compiler_params=params(),
        name="first",
    )(keep, inside, seeds, across, taps, weights, *tables)
    inside, across = neighbours(images)

    outgoing, *lanes = pl.pallas_call(
        second_kernel,
        out_shape=(shape(parts, count + 1, 8, LANES),) + (shape(2 * count, 8, LANES),) * 8,
        in_specs=[SMEM, SMEM] + vmem(11),
        out_specs=tuple(vmem(9)),
        scratch_shapes=[
            pltpu.VMEM((count, ROWS, LANES), F32),
            pltpu.VMEM((3, 8, LANES), F32),
            pltpu.VMEM((parts, 2 * count, 8, LANES), F32),
            pltpu.SemaphoreType.DMA((8,)),
        ],
        compiler_params=params(),
        name="second",
    )(place, keep, inside, images, across, side, taps, weights, *tables)

    moved = exchange(outgoing, "chan")
    moved, lanes = lax.optimization_barrier((moved, lanes))
    lanes = lanes[:1] + [
        lax.ppermute(lanes[d], AXES, [(i, i ^ d) for i in range(devices)]) for d in range(1, 8)
    ]
    after, sums = pl.pallas_call(
        tail_kernel,
        out_shape=(shape(count, 8, LANES), shape(groups, 4, LANES)),
        in_specs=vmem(1),
        out_specs=tuple(vmem(2)),
        compiler_params=params(),
        name="tail",
    )(moved)
    after = lax.ppermute(after, "tm", [(i + 1, i) for i in range(groups - 1)])
    sums = exchange(sums, "tm")
    return pl.pallas_call(
        last_kernel,
        out_shape=(shape(parts * count, 8 * LANES), shape(parts * count, 8 * LANES)),
        in_specs=[SMEM, SMEM] + vmem(12),
        out_specs=tuple(vmem(2)),
        scratch_shapes=[
            pltpu.VMEM((parts * count * 8, LANES), F32),
            pltpu.VMEM((parts * count * 8, LANES), F32),
            pltpu.VMEM((parts, 2 * count, 8, LANES), F32),
        ],
        compiler_params=params(),
        name="last",
    )(place, keep_group, moved, after, sums, taps, *lanes)


def solution(mesh):
    placed = (P(AXES, None), P(AXES, None), P(AXES, None), P())
    return jax.shard_map(
        local,
        mesh=mesh,
        in_specs=placed,
        out_specs=(P("tm", "chan"), P("tm", "chan")),
        check_vma=False,
    )
```

```python
import functools
import math

import jax
import jax.numpy as jnp
import numpy as np
from jax import lax
from jax.experimental import pallas as pl
from jax.experimental.pallas import tpu as pltpu
from jax.sharding import PartitionSpec as P

RIDGE = 0.25
ROWS = 64
LANES = 128
CHUNK = 16
F32 = jnp.float32
BF16 = jnp.bfloat16
AXES = ("tm", "chan")
VMEM_BYTES = 16 * 1024 * 1024


def params(limit=VMEM_BYTES):
    return pltpu.CompilerParams(vmem_limit_bytes=limit)


def halves(table):
    high = table.astype(np.float32).astype(jnp.bfloat16)
    low = (table - high.astype(np.float64)).astype(np.float32).astype(jnp.bfloat16)
    return high, low


def dft_tables():
    n1 = np.arange(ROWS)
    n2 = np.arange(LANES)
    k1 = np.arange(ROWS)
    k2 = (2 * np.arange(32)[None, :] + np.arange(2)[:, None]).reshape(-1)
    first = 2.0 * np.pi * (n1[:, None] * k1[None, :] % ROWS) / ROWS
    back_rows = np.concatenate([np.cos(first), -np.sin(first)], 1)
    second = 2.0 * np.pi * (k2[:, None] * n2[None, :] % LANES) / LANES
    scale = 1.0 / math.sqrt(ROWS * ROWS)
    cos = (np.cos(second) * scale).reshape(2, 32, LANES)
    sin = (np.sin(second) * scale).reshape(2, 32, LANES)
    from_real = np.concatenate([cos, sin], 2)
    from_imag = np.concatenate([-sin, cos], 2)
    back_lanes = np.stack([from_real, from_imag], 1).reshape(LANES, 2 * LANES)
    rows_high, rows_low = halves(back_rows)
    lanes_high, lanes_low = halves(back_lanes)
    twist = 2.0 * np.pi * k1[:, None] * n2[None, :] / (ROWS * LANES)
    return (
        np.concatenate([rows_high.T, rows_high.T, rows_low.T], 1),
        np.concatenate([lanes_high.T, lanes_low.T], 1),
        np.concatenate([lanes_high, lanes_high, lanes_low], 0),
        np.block([[rows_high, rows_high], [rows_low, np.zeros_like(rows_low)]]),
        np.stack([np.cos(twist), np.sin(twist)]).astype(np.float32),
    )


def split(value):
    high = value.astype(BF16)
    low = (value - high.astype(F32)).astype(BF16)
    return high, low


def dot(left, right):
    return jnp.dot(left, right, preferred_element_type=F32)


def forward_chunk(frames, ahead_rows, ahead_lanes, cos, sin):
    high, low = split(jnp.concatenate(frames, 1))
    mixed = dot(ahead_rows, jnp.concatenate([high, low, high], 0))
    turned = []
    for f in range(len(frames)):
        real = mixed[:ROWS, f * LANES : (f + 1) * LANES]
        imag = mixed[ROWS:, f * LANES : (f + 1) * LANES]
        turned.append(jnp.concatenate([real * cos + imag * sin, imag * cos - real * sin], 1))
    high, low = split(jnp.concatenate(turned, 0))
    wide = dot(high, ahead_lanes)
    return wide[:, :LANES] + wide[:, LANES:] + dot(low, ahead_lanes[:, :LANES])


def backward_chunk(spectra, back_lanes, back_rows, cos, sin):
    high, low = split(spectra)
    mixed = dot(jnp.concatenate([high, low, high], 1), back_lanes)
    turned = []
    for f in range(spectra.shape[0] // ROWS):
        real = mixed[f * ROWS : (f + 1) * ROWS, :LANES]
        imag = mixed[f * ROWS : (f + 1) * ROWS, LANES:]
        turned.append(jnp.concatenate([real * cos - imag * sin, real * sin + imag * cos], 0))
    high, low = split(jnp.concatenate(turned, 1))
    tall = dot(back_rows, jnp.concatenate([high, low], 0))
    return tall[:ROWS] + tall[ROWS:]


def turn_pair(block):
    flipped = block.T
    low_half = flipped[:ROWS]
    high_half = flipped[ROWS:]
    left = lax.broadcasted_iota(jnp.int32, (ROWS, LANES), 1) < ROWS
    return (
        jnp.where(left, low_half, pltpu.roll(high_half, ROWS, 1)),
        jnp.where(left, pltpu.roll(low_half, ROWS, 1), high_half),
    )


def seed_kernel(*refs):
    sources, out_ref, places, held, semaphore = refs[:6], refs[6], refs[7:13], refs[13], refs[14]
    copies = [
        pltpu.make_async_copy(source, place, semaphore.at[at])
        for at, (source, place) in enumerate(zip(sources, places))
    ]
    for copy in copies:
        copy.start()
    real_ref, imag_ref, weights_ref, back_lanes_ref, back_rows_ref, twist_ref = places
    count = real_ref.shape[0]
    for copy in copies:
        copy.wait()
    for j in range(32):
        columns = slice(j * LANES, (j + 1) * LANES)
        weights = weights_ref[:, columns]
        held[pl.ds(j, count, stride=ROWS), :] = weights * real_ref[:, columns]
        held[pl.ds(32 + j, count, stride=ROWS), :] = weights * imag_ref[:, columns]
    cos = twist_ref[0]
    sin = twist_ref[1]
    for start in range(0, count, CHUNK):
        spectra = []
        for f in range(start, start + CHUNK, 2):
            spectra += turn_pair(held[f * ROWS : (f + 2) * ROWS, :])
        frames = backward_chunk(
            jnp.concatenate(spectra, 0), back_lanes_ref[...], back_rows_ref[...], cos, sin
        )
        for f in range(CHUNK):
            out_ref[start + f] = frames[:, f * LANES : (f + 1) * LANES]


def arrange_kernel(weights_ref, taps_ref, weights_out, taps_out, held):
    count = weights_ref.shape[0]
    for j in range(32):
        weights = weights_ref[:, j * LANES : (j + 1) * LANES]
        held[pl.ds(j, count, stride=ROWS), :] = weights
        held[pl.ds(32 + j, count, stride=ROWS), :] = weights
    for f in range(0, count, 2):
        first, second = turn_pair(held[f * ROWS : (f + 2) * ROWS, :])
        weights_out[f] = first
        weights_out[f + 1] = second
    for n1 in range(ROWS):
        taps_out[pl.ds(n1, taps_ref.shape[0], stride=ROWS), :] = taps_ref[
            :, n1 * LANES : (n1 + 1) * LANES
        ]


def weighted_sum(taps, values):
    total = taps[0] * values[0]
    for tap, value in zip(taps[1:], values[1:]):
        total = total + tap * value
    return total


def back_filter(rows, taps, inside_ref, here_ref, across_ref, keep):
    reach = len(taps) - 1
    count = here_ref.shape[0]
    odd = jnp.full((8, LANES), keep[2]) > 0.5
    frames = [
        jnp.where(odd, inside_ref[t, rows, :], across_ref[t, rows, :]) for t in range(count - reach, count)
    ]
    frames += [here_ref[t, rows, :] for t in range(count)]
    frames += [
        jnp.where(odd, across_ref[t, rows, :], inside_ref[t, rows, :]) * keep[1] for t in range(reach)
    ]
    result = []
    for at in range(reach + count):
        total = weighted_sum(taps, frames[at : at + reach + 1])
        result.append(total * keep[0] if at < reach else total)
    return result


def ahead_filter(taps, frames):
    reach = len(taps) - 1
    return [
        weighted_sum(taps, [frames[at + reach - tap] for tap in range(reach + 1)])
        for at in range(len(frames) - reach)
    ]


def first_kernel(
    keep_ref, inside_ref, here_ref, across_ref, taps_ref, weights_ref,
    ahead_rows_ref, ahead_lanes_ref, back_lanes_ref, back_rows_ref, twist_ref,
    out_ref, side_ref, filtered,
):
    count = here_ref.shape[0]
    keep = (keep_ref[0], keep_ref[1], keep_ref[2])

    @pl.loop(0, ROWS // 8)
    def _(group):
        rows = pl.ds(pl.multiple_of(group * 8, 8), 8)
        taps = [taps_ref[p, rows, :] for p in range(taps_ref.shape[0])]
        side = back_filter(rows, taps, inside_ref, here_ref, across_ref, keep)
        for at, value in enumerate(side):
            side_ref[at, rows, :] = value
        for at, value in enumerate(ahead_filter(taps, side)):
            filtered[at, rows, :] = value

    cos = twist_ref[0]
    sin = twist_ref[1]
    for start in range(0, count, CHUNK):
        spectra = forward_chunk(
            [filtered[start + f] for f in range(CHUNK)], ahead_rows_ref[...], ahead_lanes_ref[...], cos, sin
        )
        weights = weights_ref[start : start + CHUNK].reshape(CHUNK * ROWS, LANES)
        frames = backward_chunk(spectra * weights, back_lanes_ref[...], back_rows_ref[...], cos, sin)
        for f in range(CHUNK):
            out_ref[start + f] = frames[:, f * LANES : (f + 1) * LANES]


def quarters(rows):
    return lax.broadcasted_iota(jnp.int32, (rows, LANES), 1) // 32


def pack(values):
    packed = jnp.zeros((8, LANES), F32)
    for at, value in enumerate(values):
        value = value + pltpu.roll(value, 64, 1)
        value = value + pltpu.roll(value, 32, 1)
        packed = jnp.where(quarters(8) == at, value, packed)
    return packed


def second_kernel(
    place_ref, keep_ref, inside_ref, here_ref, across_ref, side_ref, taps_ref, weights_ref,
    ahead_rows_ref, ahead_lanes_ref, back_lanes_ref, back_rows_ref, twist_ref,
    out_ref, *rest,
):
    lanes, (filtered, sums, staged) = rest[:8], rest[8:]
    count = here_ref.shape[0]
    keep = (keep_ref[0], keep_ref[1], keep_ref[2])
    reach = taps_ref.shape[0] - 1
    sums[...] = jnp.zeros_like(sums)

    @pl.loop(0, ROWS // 8)
    def _(group):
        rows = pl.ds(pl.multiple_of(group * 8, 8), 8)
        taps = [taps_ref[p, rows, :] for p in range(reach + 1)]
        image = back_filter(rows, taps, inside_ref, here_ref, across_ref, keep)
        side = [side_ref[at, rows, :] for at in range(reach + count)]
        image = [value + RIDGE * base for value, base in zip(image, side)]
        for at, value in enumerate(ahead_filter(taps, image)):
            filtered[at, rows, :] = value
        first, second, third = sums[0], sums[1], sums[2]
        for at in range(count):
            base = side[reach + at]
            value = image[reach + at]
            staged[group ^ place_ref[0], at] = base
            staged[group ^ place_ref[0], count + at] = value
            first = first + base * base
            second = second + base * value
            third = third + value * value
        sums[0] = first
        sums[1] = second
        sums[2] = third

    for d, lane in enumerate(lanes):
        lane[...] = staged[d]
    cos = twist_ref[0]
    sin = twist_ref[1]
    power = jnp.zeros((8, LANES), F32)
    for start in range(0, count, CHUNK):
        spectra = forward_chunk(
            [filtered[start + f] for f in range(CHUNK)], ahead_rows_ref[...], ahead_lanes_ref[...], cos, sin
        )
        weights = weights_ref[start : start + CHUNK].reshape(CHUNK * ROWS, LANES)
        weighted = spectra * weights
        power = power + jnp.sum((weighted * spectra).reshape(CHUNK * ROWS // 8, 8, LANES), 0)
        frames = backward_chunk(weighted, back_lanes_ref[...], back_rows_ref[...], cos, sin)
        for f in range(CHUNK):
            for group in range(ROWS // 8):
                out_ref[group, start + f] = frames[
                    group * 8 : (group + 1) * 8, f * LANES : (f + 1) * LANES
                ]
    totals = pack([sums[0], sums[1], sums[2], power])
    for group in range(ROWS // 8):
        out_ref[group, count] = totals


def tail_kernel(moved_ref, frames_ref, sums_ref):
    count = frames_ref.shape[0]
    frames_ref[...] = moved_ref[0, :count]
    total = moved_ref[0, count]
    for part in range(1, moved_ref.shape[0]):
        total = total + moved_ref[part, count]
    sums_ref[...] = jnp.broadcast_to(total[None], sums_ref.shape)


def last_kernel(place_ref, keep_ref, moved_ref, after_ref, sums_ref, taps_ref, *rest):
    lanes, (solution_ref, residual_ref, kept, left, pairs) = rest[:8], rest[8:]
    parts, count = moved_ref.shape[0], moved_ref.shape[1] - 1
    reach = taps_ref.shape[0] - 1
    rows = pl.ds(pl.multiple_of(place_ref[0] * 8, 8), 8)
    for d, lane in enumerate(lanes):
        pairs[place_ref[0] ^ d] = lane[...]
    sums = jnp.sum(sums_ref[...], 0)
    norm, curve, square, power = (
        jnp.sum(jnp.sum(jnp.where(quarters(8) == at, sums, 0.0), 1, keepdims=True), 0, keepdims=True)
        for at in range(4)
    )
    cube = power + RIDGE * square
    step = norm / curve
    next_norm = step * step * square - norm
    grown = step * square / curve
    next_step = next_norm / (step * (step * cube - grown * square))
    to_base = step + next_step * grown
    to_image = -(next_step * step)
    image_rate = -(step + next_step * grown)
    cube_rate = next_step * step
    to_base, to_image, image_rate, cube_rate = (
        jnp.broadcast_to(value, (8, LANES)) for value in (to_base, to_image, image_rate, cube_rate)
    )
    taps = [taps_ref[p, rows, :] for p in range(reach + 1)]

    def finish(part, tail):
        frames = [moved_ref[part, t] for t in range(count)] + tail
        for at in range(count):
            base = pairs[part, at]
            image = pairs[part, count + at]
            again = weighted_sum(taps, frames[at : at + reach + 1]) + RIDGE * image
            here = pl.ds(pl.multiple_of((part * count + at) * 8, 8), 8)
            kept[here, :] = to_base * base + to_image * image
            left[here, :] = base + image_rate * image + cube_rate * again

    @pl.loop(0, parts - 1)
    def _(part):
        finish(part, [moved_ref[part + 1, t] for t in range(reach)])

    finish(parts - 1, [after_ref[t] * keep_ref[0] for t in range(reach)])

    for block in range(parts * count // 8):
        for n1 in range(8):
            places = pl.ds(block * 64 + n1, 8, stride=8)
            columns = slice(n1 * LANES, (n1 + 1) * LANES)
            solution_ref[block * 8 : (block + 1) * 8, columns] = kept[places, :]
            residual_ref[block * 8 : (block + 1) * 8, columns] = left[places, :]


def shape(*dims):
    return jax.ShapeDtypeStruct(dims, F32)


def vmem(number):
    return [pl.BlockSpec(memory_space=pltpu.VMEM)] * number


SMEM = pl.BlockSpec(memory_space=pltpu.SMEM)


def local(observed_real, observed_imag, weights, taps):
    ahead_rows, ahead_lanes, back_lanes, back_rows, twist = dft_tables()
    count = weights.shape[0]
    reach = taps.shape[0] - 1
    parts = lax.axis_size("chan")
    devices = lax.axis_size("tm") * parts
    blocks = shape(count, ROWS, LANES)
    groups = lax.axis_size("tm")
    position = lax.axis_index(AXES)
    keep = jnp.stack([position > 0, position < devices - 1, position % 2 == 1]).astype(F32)
    place = lax.axis_index("chan").astype(jnp.int32).reshape(1)
    keep_group = (lax.axis_index("tm") < groups - 1).astype(F32).reshape(1)
    tables = (ahead_rows, ahead_lanes, back_lanes, back_rows, twist)

    def neighbours(block):
        inside = [(i, i ^ 1) for i in range(devices)]
        across = [(i, min(max(((i + 1) ^ 1) - 1, 0), devices - 1)) for i in range(devices)]
        return lax.ppermute(block, AXES, inside), lax.ppermute(block, AXES, across)

    def exchange(value, axis):
        return lax.all_to_all(value, axis, split_axis=0, concat_axis=0, tiled=True)

    seed_inputs = (observed_real, observed_imag, weights, back_lanes, back_rows, twist)
    seed_inputs = tuple(pltpu.with_memory_space_constraint(v, pltpu.HBM) for v in seed_inputs)
    seeds = pl.pallas_call(
        seed_kernel,
        out_shape=blocks,
        in_specs=[pl.BlockSpec(memory_space=pltpu.HBM)] * 6,
        out_specs=vmem(1)[0],
        scratch_shapes=[pltpu.VMEM(value.shape, value.dtype) for value in seed_inputs]
        + [pltpu.VMEM((count * ROWS, LANES), F32), pltpu.SemaphoreType.DMA((6,))],
        compiler_params=params(),
        name="seed",
    )(*seed_inputs)
    inside, across = neighbours(seeds)
    weights, taps = pl.pallas_call(
        arrange_kernel,
        out_shape=(blocks, shape((reach + 1) * ROWS, LANES)),
        in_specs=vmem(2),
        out_specs=tuple(vmem(2)),
        scratch_shapes=[pltpu.VMEM((count * ROWS, LANES), F32)],
        compiler_params=params(),
        cost_estimate=pl.CostEstimate(flops=10**7, bytes_accessed=2 * 10**6, transcendentals=0),
        name="arrange",
    )(weights, taps)
    taps = taps.reshape(reach + 1, ROWS, LANES)

    images, side = pl.pallas_call(
        first_kernel,
        out_shape=(blocks, shape(reach + count, ROWS, LANES)),
        in_specs=[SMEM] + vmem(10),
        out_specs=tuple(vmem(2)),
        scratch_shapes=[pltpu.VMEM((count, ROWS, LANES), F32)],
        compiler_params=params(),
        name="first",
    )(keep, inside, seeds, across, taps, weights, *tables)
    inside, across = neighbours(images)

    outgoing, *lanes = pl.pallas_call(
        second_kernel,
        out_shape=(shape(parts, count + 1, 8, LANES),) + (shape(2 * count, 8, LANES),) * 8,
        in_specs=[SMEM, SMEM] + vmem(11),
        out_specs=tuple(vmem(9)),
        scratch_shapes=[
            pltpu.VMEM((count, ROWS, LANES), F32),
            pltpu.VMEM((3, 8, LANES), F32),
            pltpu.VMEM((parts, 2 * count, 8, LANES), F32),
        ],
        compiler_params=params(),
        name="second",
    )(place, keep, inside, images, across, side, taps, weights, *tables)

    moved = exchange(outgoing, "chan")
    moved, lanes = lax.optimization_barrier((moved, lanes))
    lanes = lanes[:1] + [
        lax.ppermute(lanes[d], AXES, [(i, i ^ d) for i in range(devices)]) for d in range(1, 8)
    ]
    after, sums = pl.pallas_call(
        tail_kernel,
        out_shape=(shape(count, 8, LANES), shape(groups, 8, LANES)),
        in_specs=vmem(1),
        out_specs=tuple(vmem(2)),
        compiler_params=params(),
        name="tail",
    )(moved)
    after = lax.ppermute(after, "tm", [(i + 1, i) for i in range(groups - 1)])
    sums = exchange(sums, "tm")
    return pl.pallas_call(
        last_kernel,
        out_shape=(shape(parts * count, 8 * LANES), shape(parts * count, 8 * LANES)),
        in_specs=[SMEM, SMEM] + vmem(12),
        out_specs=tuple(vmem(2)),
        scratch_shapes=[
            pltpu.VMEM((parts * count * 8, LANES), F32),
            pltpu.VMEM((parts * count * 8, LANES), F32),
            pltpu.VMEM((parts, 2 * count, 8, LANES), F32),
        ],
        compiler_params=params(),
        name="last",
    )(place, keep_group, moved, after, sums, taps, *lanes)


def solution(mesh):
    placed = (P(AXES, None), P(AXES, None), P(AXES, None), P())
    return jax.shard_map(
        local,
        mesh=mesh,
        in_specs=placed,
        out_specs=(P("tm", "chan"), P("tm", "chan")),
        check_vma=False,
    )
```

```python
import functools
import math

import jax
import jax.numpy as jnp
import numpy as np
from jax import lax
from jax.experimental import pallas as pl
from jax.experimental.pallas import tpu as pltpu
from jax.sharding import PartitionSpec as P

RIDGE = 0.25
ROWS = 64
LANES = 128
CHUNK = 16
F32 = jnp.float32
BF16 = jnp.bfloat16
AXES = ("tm", "chan")
VMEM_BYTES = 16 * 1024 * 1024


def params(limit=VMEM_BYTES):
    return pltpu.CompilerParams(vmem_limit_bytes=limit)


def halves(table):
    high = table.astype(np.float32).astype(jnp.bfloat16)
    low = (table - high.astype(np.float64)).astype(np.float32).astype(jnp.bfloat16)
    return high, low


def dft_tables():
    n1 = np.arange(ROWS)
    n2 = np.arange(LANES)
    k1 = np.arange(ROWS)
    k2 = (2 * np.arange(32)[None, :] + np.arange(2)[:, None]).reshape(-1)
    first = 2.0 * np.pi * (n1[:, None] * k1[None, :] % ROWS) / ROWS
    back_rows = np.concatenate([np.cos(first), -np.sin(first)], 1)
    second = 2.0 * np.pi * (k2[:, None] * n2[None, :] % LANES) / LANES
    scale = 1.0 / math.sqrt(ROWS * ROWS)
    cos = (np.cos(second) * scale).reshape(2, 32, LANES)
    sin = (np.sin(second) * scale).reshape(2, 32, LANES)
    from_real = np.concatenate([cos, sin], 2)
    from_imag = np.concatenate([-sin, cos], 2)
    back_lanes = np.stack([from_real, from_imag], 1).reshape(LANES, 2 * LANES)
    rows_high, rows_low = halves(back_rows)
    lanes_high, lanes_low = halves(back_lanes)
    twist = 2.0 * np.pi * k1[:, None] * n2[None, :] / (ROWS * LANES)
    return (
        np.concatenate([rows_high.T, rows_high.T, rows_low.T], 1),
        np.concatenate([lanes_high.T, lanes_low.T], 1),
        np.concatenate([lanes_high, lanes_high, lanes_low], 0),
        np.block([[rows_high, rows_high], [rows_low, np.zeros_like(rows_low)]]),
        np.stack([np.cos(twist), np.sin(twist)]).astype(np.float32),
    )


def split(value):
    high = value.astype(BF16)
    low = (value - high.astype(F32)).astype(BF16)
    return high, low


def dot(left, right):
    return jnp.dot(left, right, preferred_element_type=F32)


def forward_chunk(frames, ahead_rows, ahead_lanes, cos, sin):
    high, low = split(jnp.concatenate(frames, 1))
    mixed = dot(ahead_rows, jnp.concatenate([high, low, high], 0))
    turned = []
    for f in range(len(frames)):
        real = mixed[:ROWS, f * LANES : (f + 1) * LANES]
        imag = mixed[ROWS:, f * LANES : (f + 1) * LANES]
        turned.append(jnp.concatenate([real * cos + imag * sin, imag * cos - real * sin], 1))
    high, low = split(jnp.concatenate(turned, 0))
    wide = dot(high, ahead_lanes)
    return wide[:, :LANES] + wide[:, LANES:] + dot(low, ahead_lanes[:, :LANES])


def backward_chunk(spectra, back_lanes, back_rows, cos, sin):
    high, low = split(spectra)
    mixed = dot(jnp.concatenate([high, low, high], 1), back_lanes)
    turned = []
    for f in range(spectra.shape[0] // ROWS):
        real = mixed[f * ROWS : (f + 1) * ROWS, :LANES]
        imag = mixed[f * ROWS : (f + 1) * ROWS, LANES:]
        turned.append(jnp.concatenate([real * cos - imag * sin, real * sin + imag * cos], 0))
    high, low = split(jnp.concatenate(turned, 1))
    tall = dot(back_rows, jnp.concatenate([high, low], 0))
    return tall[:ROWS] + tall[ROWS:]


def turn_pair(block):
    flipped = block.T
    low_half = flipped[:ROWS]
    high_half = flipped[ROWS:]
    left = lax.broadcasted_iota(jnp.int32, (ROWS, LANES), 1) < ROWS
    return (
        jnp.where(left, low_half, pltpu.roll(high_half, ROWS, 1)),
        jnp.where(left, pltpu.roll(low_half, ROWS, 1), high_half),
    )


def seed_kernel(*refs):
    sources, out_ref, places, held, semaphore = refs[:6], refs[6], refs[7:13], refs[13], refs[14]
    copies = [
        pltpu.make_async_copy(source, place, semaphore.at[at])
        for at, (source, place) in enumerate(zip(sources, places))
    ]
    for copy in copies:
        copy.start()
    real_ref, imag_ref, weights_ref, back_lanes_ref, back_rows_ref, twist_ref = places
    count = real_ref.shape[0]
    for copy in copies:
        copy.wait()
    for j in range(32):
        columns = slice(j * LANES, (j + 1) * LANES)
        weights = weights_ref[:, columns]
        held[pl.ds(j, count, stride=ROWS), :] = weights * real_ref[:, columns]
        held[pl.ds(32 + j, count, stride=ROWS), :] = weights * imag_ref[:, columns]
    cos = twist_ref[0]
    sin = twist_ref[1]
    for start in range(0, count, CHUNK):
        spectra = []
        for f in range(start, start + CHUNK, 2):
            spectra += turn_pair(held[f * ROWS : (f + 2) * ROWS, :])
        frames = backward_chunk(
            jnp.concatenate(spectra, 0), back_lanes_ref[...], back_rows_ref[...], cos, sin
        )
        for f in range(CHUNK):
            out_ref[start + f] = frames[:, f * LANES : (f + 1) * LANES]


def arrange_kernel(weights_ref, taps_ref, weights_out, taps_out, held):
    count = weights_ref.shape[0]
    for j in range(32):
        weights = weights_ref[:, j * LANES : (j + 1) * LANES]
        held[pl.ds(j, count, stride=ROWS), :] = weights
        held[pl.ds(32 + j, count, stride=ROWS), :] = weights
    for f in range(0, count, 2):
        first, second = turn_pair(held[f * ROWS : (f + 2) * ROWS, :])
        weights_out[f] = first
        weights_out[f + 1] = second
    for n1 in range(ROWS):
        taps_out[pl.ds(n1, taps_ref.shape[0], stride=ROWS), :] = taps_ref[
            :, n1 * LANES : (n1 + 1) * LANES
        ]


def weighted_sum(taps, values):
    total = taps[0] * values[0]
    for tap, value in zip(taps[1:], values[1:]):
        total = total + tap * value
    return total


def back_filter(rows, taps, inside_ref, here_ref, across_ref, keep):
    reach = len(taps) - 1
    count = here_ref.shape[0]
    odd = jnp.full((8, LANES), keep[2]) > 0.5
    frames = [
        jnp.where(odd, inside_ref[t, rows, :], across_ref[t, rows, :]) for t in range(count - reach, count)
    ]
    frames += [here_ref[t, rows, :] for t in range(count)]
    frames += [
        jnp.where(odd, across_ref[t, rows, :], inside_ref[t, rows, :]) * keep[1] for t in range(reach)
    ]
    result = []
    for at in range(reach + count):
        total = weighted_sum(taps, frames[at : at + reach + 1])
        result.append(total * keep[0] if at < reach else total)
    return result


def ahead_filter(taps, frames):
    reach = len(taps) - 1
    return [
        weighted_sum(taps, [frames[at + reach - tap] for tap in range(reach + 1)])
        for at in range(len(frames) - reach)
    ]


def first_kernel(
    keep_ref, inside_ref, here_ref, across_ref, taps_ref, weights_ref,
    ahead_rows_ref, ahead_lanes_ref, back_lanes_ref, back_rows_ref, twist_ref,
    out_ref, side_ref, filtered,
):
    count = here_ref.shape[0]
    keep = (keep_ref[0], keep_ref[1], keep_ref[2])

    @pl.loop(0, ROWS // 8)
    def _(group):
        rows = pl.ds(pl.multiple_of(group * 8, 8), 8)
        taps = [taps_ref[p, rows, :] for p in range(taps_ref.shape[0])]
        side = back_filter(rows, taps, inside_ref, here_ref, across_ref, keep)
        for at, value in enumerate(side):
            side_ref[at, rows, :] = value
        for at, value in enumerate(ahead_filter(taps, side)):
            filtered[at, rows, :] = value

    cos = twist_ref[0]
    sin = twist_ref[1]
    for start in range(0, count, CHUNK):
        spectra = forward_chunk(
            [filtered[start + f] for f in range(CHUNK)], ahead_rows_ref[...], ahead_lanes_ref[...], cos, sin
        )
        weights = weights_ref[start : start + CHUNK].reshape(CHUNK * ROWS, LANES)
        frames = backward_chunk(spectra * weights, back_lanes_ref[...], back_rows_ref[...], cos, sin)
        for f in range(CHUNK):
            out_ref[start + f] = frames[:, f * LANES : (f + 1) * LANES]


def quarters(rows):
    return lax.broadcasted_iota(jnp.int32, (rows, LANES), 1) // 32


def pack(values):
    packed = jnp.zeros((8, LANES), F32)
    for at, value in enumerate(values):
        value = value + pltpu.roll(value, 64, 1)
        value = value + pltpu.roll(value, 32, 1)
        packed = jnp.where(quarters(8) == at, value, packed)
    return packed


def second_kernel(
    place_ref, keep_ref, inside_ref, here_ref, across_ref, side_ref, taps_ref, weights_ref,
    ahead_rows_ref, ahead_lanes_ref, back_lanes_ref, back_rows_ref, twist_ref,
    out_ref, *rest,
):
    lanes, (filtered, sums, staged) = rest[:8], rest[8:]
    count = here_ref.shape[0]
    keep = (keep_ref[0], keep_ref[1], keep_ref[2])
    reach = taps_ref.shape[0] - 1
    sums[...] = jnp.zeros_like(sums)

    @pl.loop(0, ROWS // 8)
    def _(group):
        rows = pl.ds(pl.multiple_of(group * 8, 8), 8)
        taps = [taps_ref[p, rows, :] for p in range(reach + 1)]
        image = back_filter(rows, taps, inside_ref, here_ref, across_ref, keep)
        side = [side_ref[at, rows, :] for at in range(reach + count)]
        image = [value + RIDGE * base for value, base in zip(image, side)]
        for at, value in enumerate(ahead_filter(taps, image)):
            filtered[at, rows, :] = value
        first, second, third = sums[0], sums[1], sums[2]
        for at in range(count):
            base = side[reach + at]
            value = image[reach + at]
            staged[group ^ place_ref[0], at] = base
            staged[group ^ place_ref[0], count + at] = value
            first = first + base * base
            second = second + base * value
            third = third + value * value
        sums[0] = first
        sums[1] = second
        sums[2] = third

    for d, lane in enumerate(lanes):
        lane[...] = staged[d]
    cos = twist_ref[0]
    sin = twist_ref[1]
    power = jnp.zeros((8, LANES), F32)
    for start in range(0, count, CHUNK):
        spectra = forward_chunk(
            [filtered[start + f] for f in range(CHUNK)], ahead_rows_ref[...], ahead_lanes_ref[...], cos, sin
        )
        weights = weights_ref[start : start + CHUNK].reshape(CHUNK * ROWS, LANES)
        weighted = spectra * weights
        power = power + jnp.sum((weighted * spectra).reshape(CHUNK * ROWS // 8, 8, LANES), 0)
        frames = backward_chunk(weighted, back_lanes_ref[...], back_rows_ref[...], cos, sin)
        for f in range(CHUNK):
            for group in range(ROWS // 8):
                out_ref[group, start + f] = frames[
                    group * 8 : (group + 1) * 8, f * LANES : (f + 1) * LANES
                ]
    totals = pack([sums[0], sums[1], sums[2], power])
    for group in range(ROWS // 8):
        out_ref[group, count] = totals


def tail_kernel(moved_ref, _, __, frames_ref, sums_ref):
    count = frames_ref.shape[0]
    frames_ref[...] = moved_ref[0, :count]
    total = moved_ref[0, count]
    for part in range(1, moved_ref.shape[0]):
        total = total + moved_ref[part, count]
    sums_ref[...] = jnp.broadcast_to((total[:4] + total[4:])[None], sums_ref.shape)


def last_kernel(place_ref, keep_ref, moved_ref, after_ref, sums_ref, taps_ref, *rest):
    lanes, (solution_ref, residual_ref, kept, left, pairs) = rest[:8], rest[8:]
    parts, count = moved_ref.shape[0], moved_ref.shape[1] - 1
    reach = taps_ref.shape[0] - 1
    rows = pl.ds(pl.multiple_of(place_ref[0] * 8, 8), 8)
    for d, lane in enumerate(lanes):
        pairs[place_ref[0] ^ d] = lane[...]
    sums = jnp.sum(sums_ref[...], 0)
    norm, curve, square, power = (
        jnp.sum(jnp.sum(jnp.where(quarters(4) == at, sums, 0.0), 1, keepdims=True), 0, keepdims=True)
        for at in range(4)
    )
    cube = power + RIDGE * square
    step = norm / curve
    next_norm = step * step * square - norm
    grown = step * square / curve
    next_step = next_norm / (step * (step * cube - grown * square))
    to_base = step + next_step * grown
    to_image = -(next_step * step)
    image_rate = -(step + next_step * grown)
    cube_rate = next_step * step
    to_base, to_image, image_rate, cube_rate = (
        jnp.broadcast_to(value, (8, LANES)) for value in (to_base, to_image, image_rate, cube_rate)
    )
    taps = [taps_ref[p, rows, :] for p in range(reach + 1)]

    def finish(part, tail):
        frames = [moved_ref[part, t] for t in range(count)] + tail
        for at in range(count):
            base = pairs[part, at]
            image = pairs[part, count + at]
            again = weighted_sum(taps, frames[at : at + reach + 1]) + RIDGE * image
            here = pl.ds(pl.multiple_of((part * count + at) * 8, 8), 8)
            kept[here, :] = to_base * base + to_image * image
            left[here, :] = base + image_rate * image + cube_rate * again

    @pl.loop(0, parts - 1)
    def _(part):
        finish(part, [moved_ref[part + 1, t] for t in range(reach)])

    finish(parts - 1, [after_ref[t] * keep_ref[0] for t in range(reach)])

    for block in range(parts * count // 8):
        for n1 in range(8):
            places = pl.ds(block * 64 + n1, 8, stride=8)
            columns = slice(n1 * LANES, (n1 + 1) * LANES)
            solution_ref[block * 8 : (block + 1) * 8, columns] = kept[places, :]
            residual_ref[block * 8 : (block + 1) * 8, columns] = left[places, :]


def shape(*dims):
    return jax.ShapeDtypeStruct(dims, F32)


def vmem(number):
    return [pl.BlockSpec(memory_space=pltpu.VMEM)] * number


SMEM = pl.BlockSpec(memory_space=pltpu.SMEM)
ANY = pl.BlockSpec(memory_space=pl.ANY)


def local(observed_real, observed_imag, weights, taps):
    ahead_rows, ahead_lanes, back_lanes, back_rows, twist = dft_tables()
    count = weights.shape[0]
    reach = taps.shape[0] - 1
    parts = lax.axis_size("chan")
    devices = lax.axis_size("tm") * parts
    blocks = shape(count, ROWS, LANES)
    groups = lax.axis_size("tm")
    position = lax.axis_index(AXES)
    keep = jnp.stack([position > 0, position < devices - 1, position % 2 == 1]).astype(F32)
    place = lax.axis_index("chan").astype(jnp.int32).reshape(1)
    keep_group = (lax.axis_index("tm") < groups - 1).astype(F32).reshape(1)
    tables = (ahead_rows, ahead_lanes, back_lanes, back_rows, twist)

    def neighbours(block):
        inside = [(i, i ^ 1) for i in range(devices)]
        across = [(i, min(max(((i + 1) ^ 1) - 1, 0), devices - 1)) for i in range(devices)]
        return lax.ppermute(block, AXES, inside), lax.ppermute(block, AXES, across)

    def exchange(value, axis):
        return lax.all_to_all(value, axis, split_axis=0, concat_axis=0, tiled=True)

    seed_inputs = (observed_real, observed_imag, weights, back_lanes, back_rows, twist)
    seed_inputs = tuple(pltpu.with_memory_space_constraint(v, pltpu.HBM) for v in seed_inputs)
    seeds = pl.pallas_call(
        seed_kernel,
        out_shape=blocks,
        in_specs=[pl.BlockSpec(memory_space=pltpu.HBM)] * 6,
        out_specs=vmem(1)[0],
        scratch_shapes=[pltpu.VMEM(value.shape, value.dtype) for value in seed_inputs]
        + [pltpu.VMEM((count * ROWS, LANES), F32), pltpu.SemaphoreType.DMA((6,))],
        compiler_params=params(),
        name="seed",
    )(*seed_inputs)
    inside, across = neighbours(seeds)
    weights, taps = pl.pallas_call(
        arrange_kernel,
        out_shape=(blocks, shape((reach + 1) * ROWS, LANES)),
        in_specs=vmem(2),
        out_specs=tuple(vmem(2)),
        scratch_shapes=[pltpu.VMEM((count * ROWS, LANES), F32)],
        compiler_params=params(),
        cost_estimate=pl.CostEstimate(flops=10**7, bytes_accessed=2 * 10**6, transcendentals=0),
        name="arrange",
    )(weights, taps)
    taps = taps.reshape(reach + 1, ROWS, LANES)

    images, side = pl.pallas_call(
        first_kernel,
        out_shape=(blocks, shape(reach + count, ROWS, LANES)),
        in_specs=[SMEM] + vmem(10),
        out_specs=tuple(vmem(2)),
        scratch_shapes=[pltpu.VMEM((count, ROWS, LANES), F32)],
        compiler_params=params(),
        name="first",
    )(keep, inside, seeds, across, taps, weights, *tables)
    inside, across = neighbours(images)

    outgoing, *lanes = pl.pallas_call(
        second_kernel,
        out_shape=(shape(parts, count + 1, 8, LANES),) + (shape(2 * count, 8, LANES),) * 8,
        in_specs=[SMEM, SMEM] + vmem(11),
        out_specs=tuple(vmem(9)),
        scratch_shapes=[
            pltpu.VMEM((count, ROWS, LANES), F32),
            pltpu.VMEM((3, 8, LANES), F32),
            pltpu.VMEM((parts, 2 * count, 8, LANES), F32),
        ],
        compiler_params=params(),
        name="second",
    )(place, keep, inside, images, across, side, taps, weights, *tables)

    moved = exchange(outgoing, "chan")
    moved, lanes = lax.optimization_barrier((moved, lanes))
    lanes = lanes[:1] + [
        lax.ppermute(lanes[d], AXES, [(i, i ^ d) for i in range(devices)]) for d in range(1, 8)
    ]
    after, sums = pl.pallas_call(
        tail_kernel,
        out_shape=(shape(count, 8, LANES), shape(groups, 4, LANES)),
        in_specs=vmem(1) + [ANY, ANY],
        out_specs=tuple(vmem(2)),
        compiler_params=params(),
        name="tail",
    )(moved, lanes[1], lanes[2])
    after = lax.ppermute(after, "tm", [(i + 1, i) for i in range(groups - 1)])
    sums = exchange(sums, "tm")
    return pl.pallas_call(
        last_kernel,
        out_shape=(shape(parts * count, 8 * LANES), shape(parts * count, 8 * LANES)),
        in_specs=[SMEM, SMEM] + vmem(12),
        out_specs=tuple(vmem(2)),
        scratch_shapes=[
            pltpu.VMEM((parts * count * 8, LANES), F32),
            pltpu.VMEM((parts * count * 8, LANES), F32),
            pltpu.VMEM((parts, 2 * count, 8, LANES), F32),
        ],
        compiler_params=params(),
        name="last",
    )(place, keep_group, moved, after, sums, taps, *lanes)


def solution(mesh):
    placed = (P(AXES, None), P(AXES, None), P(AXES, None), P())
    return jax.shard_map(
        local,
        mesh=mesh,
        in_specs=placed,
        out_specs=(P("tm", "chan"), P("tm", "chan")),
        check_vma=False,
    )
```

```python
import functools
import math

import jax
import jax.numpy as jnp
import numpy as np
from jax import lax
from jax.experimental import pallas as pl
from jax.experimental.pallas import tpu as pltpu
from jax.sharding import PartitionSpec as P

RIDGE = 0.25
ROWS = 64
LANES = 128
CHUNK = 16
F32 = jnp.float32
BF16 = jnp.bfloat16
AXES = ("tm", "chan")
VMEM_BYTES = 16 * 1024 * 1024


def params(limit=VMEM_BYTES):
    return pltpu.CompilerParams(vmem_limit_bytes=limit)


def halves(table):
    high = table.astype(np.float32).astype(jnp.bfloat16)
    low = (table - high.astype(np.float64)).astype(np.float32).astype(jnp.bfloat16)
    return high, low


def dft_tables():
    n1 = np.arange(ROWS)
    n2 = np.arange(LANES)
    k1 = np.arange(ROWS)
    k2 = (2 * np.arange(32)[None, :] + np.arange(2)[:, None]).reshape(-1)
    first = 2.0 * np.pi * (n1[:, None] * k1[None, :] % ROWS) / ROWS
    back_rows = np.concatenate([np.cos(first), -np.sin(first)], 1)
    second = 2.0 * np.pi * (k2[:, None] * n2[None, :] % LANES) / LANES
    scale = 1.0 / math.sqrt(ROWS * ROWS)
    cos = (np.cos(second) * scale).reshape(2, 32, LANES)
    sin = (np.sin(second) * scale).reshape(2, 32, LANES)
    from_real = np.concatenate([cos, sin], 2)
    from_imag = np.concatenate([-sin, cos], 2)
    back_lanes = np.stack([from_real, from_imag], 1).reshape(LANES, 2 * LANES)
    rows_high, rows_low = halves(back_rows)
    lanes_high, lanes_low = halves(back_lanes)
    twist = 2.0 * np.pi * k1[:, None] * n2[None, :] / (ROWS * LANES)
    return (
        np.concatenate([rows_high.T, rows_high.T, rows_low.T], 1),
        np.concatenate([lanes_high.T, lanes_low.T], 1),
        np.concatenate([lanes_high, lanes_high, lanes_low], 0),
        np.block([[rows_high, rows_high], [rows_low, np.zeros_like(rows_low)]]),
        np.stack([np.cos(twist), np.sin(twist)]).astype(np.float32),
    )


def split(value):
    high = value.astype(BF16)
    low = (value - high.astype(F32)).astype(BF16)
    return high, low


def dot(left, right):
    return jnp.dot(left, right, preferred_element_type=F32)


def forward_chunk(frames, ahead_rows, ahead_lanes, cos, sin):
    high, low = split(jnp.concatenate(frames, 1))
    mixed = dot(ahead_rows, jnp.concatenate([high, low, high], 0))
    turned = []
    for f in range(len(frames)):
        real = mixed[:ROWS, f * LANES : (f + 1) * LANES]
        imag = mixed[ROWS:, f * LANES : (f + 1) * LANES]
        turned.append(jnp.concatenate([real * cos + imag * sin, imag * cos - real * sin], 1))
    high, low = split(jnp.concatenate(turned, 0))
    wide = dot(high, ahead_lanes)
    return wide[:, :LANES] + wide[:, LANES:] + dot(low, ahead_lanes[:, :LANES])


def backward_chunk(spectra, back_lanes, back_rows, cos, sin):
    high, low = split(spectra)
    mixed = dot(jnp.concatenate([high, low, high], 1), back_lanes)
    turned = []
    for f in range(spectra.shape[0] // ROWS):
        real = mixed[f * ROWS : (f + 1) * ROWS, :LANES]
        imag = mixed[f * ROWS : (f + 1) * ROWS, LANES:]
        turned.append(jnp.concatenate([real * cos - imag * sin, real * sin + imag * cos], 0))
    high, low = split(jnp.concatenate(turned, 1))
    tall = dot(back_rows, jnp.concatenate([high, low], 0))
    return tall[:ROWS] + tall[ROWS:]


def turn_pair(block):
    flipped = block.T
    low_half = flipped[:ROWS]
    high_half = flipped[ROWS:]
    left = lax.broadcasted_iota(jnp.int32, (ROWS, LANES), 1) < ROWS
    return (
        jnp.where(left, low_half, pltpu.roll(high_half, ROWS, 1)),
        jnp.where(left, pltpu.roll(low_half, ROWS, 1), high_half),
    )


def seed_kernel(*refs):
    sources, out_ref, edge_ref, places, held, semaphore = (
        refs[:6], refs[6], refs[7], refs[8:14], refs[14], refs[15]
    )
    real_ref, imag_ref, weights_ref, back_lanes_ref, back_rows_ref, twist_ref = places
    count = real_ref.shape[0]
    half = count // 2
    pieces = [
        [
            pltpu.make_async_copy(
                source.at[pl.ds(at * half, half)], place.at[pl.ds(at * half, half)], semaphore.at[at * 3 + which]
            )
            for which, (source, place) in enumerate(zip(sources[:3], places[:3]))
        ]
        for at in range(2)
    ]
    tables = [
        pltpu.make_async_copy(source, place, semaphore.at[6 + which])
        for which, (source, place) in enumerate(zip(sources[3:], places[3:]))
    ]
    for copy in pieces[0] + pieces[1] + tables:
        copy.start()
    for at in range(2):
        for copy in pieces[at]:
            copy.wait()
        rows = slice(at * half, (at + 1) * half)
        for j in range(32):
            columns = slice(j * LANES, (j + 1) * LANES)
            weights = weights_ref[rows, columns]
            first = at * half * ROWS + j
            held[pl.ds(first, half, stride=ROWS), :] = weights * real_ref[rows, columns]
            held[pl.ds(first + 32, half, stride=ROWS), :] = weights * imag_ref[rows, columns]
    for copy in tables:
        copy.wait()
    cos = twist_ref[0]
    sin = twist_ref[1]
    for start in range(0, count, CHUNK):
        spectra = []
        for f in range(start, start + CHUNK, 2):
            spectra += turn_pair(held[f * ROWS : (f + 2) * ROWS, :])
        frames = backward_chunk(
            jnp.concatenate(spectra, 0), back_lanes_ref[...], back_rows_ref[...], cos, sin
        )
        keep_frames(frames, out_ref, edge_ref)


def arrange_kernel(weights_ref, taps_ref, weights_out, taps_out, held):
    count = weights_ref.shape[0]
    for j in range(32):
        weights = weights_ref[:, j * LANES : (j + 1) * LANES]
        held[pl.ds(j, count, stride=ROWS), :] = weights
        held[pl.ds(32 + j, count, stride=ROWS), :] = weights
    for f in range(0, count, 2):
        first, second = turn_pair(held[f * ROWS : (f + 2) * ROWS, :])
        weights_out[f] = first
        weights_out[f + 1] = second
    for n1 in range(ROWS):
        taps_out[pl.ds(n1, taps_ref.shape[0], stride=ROWS), :] = taps_ref[
            :, n1 * LANES : (n1 + 1) * LANES
        ]


def keep_frames(frames, out_ref, edge_ref):
    count = out_ref.shape[0]
    odd = jnp.full((ROWS, LANES), lax.axis_index("chan") % 2) > 0
    frames = [frames[:, f * LANES : (f + 1) * LANES] for f in range(count)]
    for f in range(count):
        out_ref[f] = frames[f]
    for f in range(count - 1):
        edge_ref[f] = jnp.where(odd, frames[f + 1], frames[f])


def weighted_sum(taps, values):
    total = taps[0] * values[0]
    for tap, value in zip(taps[1:], values[1:]):
        total = total + tap * value
    return total


def back_filter(rows, taps, inside_ref, here_ref, across_ref, keep):
    reach = len(taps) - 1
    count = here_ref.shape[0]
    odd = jnp.full((8, LANES), keep[2]) > 0.5
    frames = [
        jnp.where(odd, inside_ref[t, rows, :], across_ref[t - 1, rows, :]) for t in range(1, count)
    ]
    frames += [here_ref[t, rows, :] for t in range(count)]
    frames += [
        jnp.where(odd, across_ref[t, rows, :], inside_ref[t, rows, :]) * keep[1] for t in range(reach)
    ]
    result = []
    for at in range(reach + count):
        total = weighted_sum(taps, frames[at : at + reach + 1])
        result.append(total * keep[0] if at < reach else total)
    return result


def ahead_filter(taps, frames):
    reach = len(taps) - 1
    return [
        weighted_sum(taps, [frames[at + reach - tap] for tap in range(reach + 1)])
        for at in range(len(frames) - reach)
    ]


def first_kernel(
    keep_ref, inside_ref, here_ref, across_ref, taps_ref, weights_ref,
    ahead_rows_ref, ahead_lanes_ref, back_lanes_ref, back_rows_ref, twist_ref,
    out_ref, edge_ref, side_ref, filtered,
):
    count = here_ref.shape[0]
    keep = (keep_ref[0], keep_ref[1], keep_ref[2])

    @pl.loop(0, ROWS // 8)
    def _(group):
        rows = pl.ds(pl.multiple_of(group * 8, 8), 8)
        taps = [taps_ref[p, rows, :] for p in range(taps_ref.shape[0])]
        side = back_filter(rows, taps, inside_ref, here_ref, across_ref, keep)
        for at, value in enumerate(side):
            side_ref[at, rows, :] = value
        for at, value in enumerate(ahead_filter(taps, side)):
            filtered[at, rows, :] = value

    cos = twist_ref[0]
    sin = twist_ref[1]
    for start in range(0, count, CHUNK):
        spectra = forward_chunk(
            [filtered[start + f] for f in range(CHUNK)], ahead_rows_ref[...], ahead_lanes_ref[...], cos, sin
        )
        weights = weights_ref[start : start + CHUNK].reshape(CHUNK * ROWS, LANES)
        frames = backward_chunk(spectra * weights, back_lanes_ref[...], back_rows_ref[...], cos, sin)
        keep_frames(frames, out_ref, edge_ref)


def quarters(rows):
    return lax.broadcasted_iota(jnp.int32, (rows, LANES), 1) // 32


def pack(values):
    packed = jnp.zeros((8, LANES), F32)
    for at, value in enumerate(values):
        value = value + pltpu.roll(value, 64, 1)
        value = value + pltpu.roll(value, 32, 1)
        packed = jnp.where(quarters(8) == at, value, packed)
    return packed


def second_kernel(
    place_ref, keep_ref, inside_ref, here_ref, across_ref, side_ref, taps_ref, weights_ref,
    ahead_rows_ref, ahead_lanes_ref, back_lanes_ref, back_rows_ref, twist_ref,
    out_ref, *rest,
):
    lanes, (filtered, sums, staged) = rest[:8], rest[8:]
    count = here_ref.shape[0]
    keep = (keep_ref[0], keep_ref[1], keep_ref[2])
    reach = taps_ref.shape[0] - 1
    sums[...] = jnp.zeros_like(sums)

    @pl.loop(0, ROWS // 8)
    def _(group):
        rows = pl.ds(pl.multiple_of(group * 8, 8), 8)
        taps = [taps_ref[p, rows, :] for p in range(reach + 1)]
        image = back_filter(rows, taps, inside_ref, here_ref, across_ref, keep)
        side = [side_ref[at, rows, :] for at in range(reach + count)]
        image = [value + RIDGE * base for value, base in zip(image, side)]
        for at, value in enumerate(ahead_filter(taps, image)):
            filtered[at, rows, :] = value
        first, second, third = sums[0], sums[1], sums[2]
        for at in range(count):
            base = side[reach + at]
            value = image[reach + at]
            staged[group ^ place_ref[0], at] = base
            staged[group ^ place_ref[0], count + at] = value
            first = first + base * base
            second = second + base * value
            third = third + value * value
        sums[0] = first
        sums[1] = second
        sums[2] = third

    for d, lane in enumerate(lanes):
        lane[...] = staged[d]
    cos = twist_ref[0]
    sin = twist_ref[1]
    power = jnp.zeros((8, LANES), F32)
    for start in range(0, count, CHUNK):
        spectra = forward_chunk(
            [filtered[start + f] for f in range(CHUNK)], ahead_rows_ref[...], ahead_lanes_ref[...], cos, sin
        )
        weights = weights_ref[start : start + CHUNK].reshape(CHUNK * ROWS, LANES)
        weighted = spectra * weights
        power = power + jnp.sum((weighted * spectra).reshape(CHUNK * ROWS // 8, 8, LANES), 0)
        frames = backward_chunk(weighted, back_lanes_ref[...], back_rows_ref[...], cos, sin)
        for f in range(CHUNK):
            for group in range(ROWS // 8):
                out_ref[group, start + f] = frames[
                    group * 8 : (group + 1) * 8, f * LANES : (f + 1) * LANES
                ]
    totals = pack([sums[0], sums[1], sums[2], power])
    for group in range(ROWS // 8):
        out_ref[group, count] = totals


def tail_kernel(moved_ref, _, __, frames_ref, sums_ref):
    count = frames_ref.shape[0]
    frames_ref[...] = moved_ref[0, :count]
    total = moved_ref[0, count]
    for part in range(1, moved_ref.shape[0]):
        total = total + moved_ref[part, count]
    sums_ref[...] = jnp.broadcast_to((total[:4] + total[4:])[None], sums_ref.shape)


def last_kernel(place_ref, keep_ref, moved_ref, after_ref, sums_ref, taps_ref, *rest):
    lanes, (*outputs, kept, left, pairs, kept_rows, left_rows, semaphore) = rest[:8], rest[8:]
    parts, count = moved_ref.shape[0], moved_ref.shape[1] - 1
    reach = taps_ref.shape[0] - 1
    rows = pl.ds(pl.multiple_of(place_ref[0] * 8, 8), 8)
    for d, lane in enumerate(lanes):
        pairs[place_ref[0] ^ d] = lane[...]
    sums = jnp.sum(sums_ref[...], 0)
    norm, curve, square, power = (
        jnp.sum(jnp.sum(jnp.where(quarters(4) == at, sums, 0.0), 1, keepdims=True), 0, keepdims=True)
        for at in range(4)
    )
    cube = power + RIDGE * square
    step = norm / curve
    next_norm = step * step * square - norm
    grown = step * square / curve
    next_step = next_norm / (step * (step * cube - grown * square))
    to_base = step + next_step * grown
    to_image = -(next_step * step)
    image_rate = -(step + next_step * grown)
    cube_rate = next_step * step
    to_base, to_image, image_rate, cube_rate = (
        jnp.broadcast_to(value, (8, LANES)) for value in (to_base, to_image, image_rate, cube_rate)
    )
    taps = [taps_ref[p, rows, :] for p in range(reach + 1)]

    def finish(part, tail):
        frames = [moved_ref[part, t] for t in range(count)] + tail
        for at in range(count):
            base = pairs[part, at]
            image = pairs[part, count + at]
            again = weighted_sum(taps, frames[at : at + reach + 1]) + RIDGE * image
            here = slice(at * 8, (at + 1) * 8)
            kept[here, :] = to_base * base + to_image * image
            left[here, :] = base + image_rate * image + cube_rate * again
        for block in range(count // 8):
            ready = pl.ds(pl.multiple_of(part * count + block * 8, 8), 8)
            for n1 in range(8):
                places = pl.ds(block * 64 + n1, 8, stride=8)
                columns = slice(n1 * LANES, (n1 + 1) * LANES)
                kept_rows[ready, columns] = kept[places, :]
                left_rows[ready, columns] = left[places, :]
        for copy in copies(part):
            copy.start()

    def copies(part):
        ready = pl.ds(pl.multiple_of(part * count, 8), count)
        return [
            pltpu.make_async_copy(held.at[ready], output.at[ready], semaphore.at[which, part])
            for which, (held, output) in enumerate(zip((kept_rows, left_rows), outputs))
        ]

    @pl.loop(0, parts - 1)
    def _(part):
        finish(part, [moved_ref[part + 1, t] for t in range(reach)])

    finish(parts - 1, [after_ref[t] * keep_ref[0] for t in range(reach)])
    for part in range(parts):
        for copy in copies(part):
            copy.wait()


def shape(*dims):
    return jax.ShapeDtypeStruct(dims, F32)


def vmem(number):
    return [pl.BlockSpec(memory_space=pltpu.VMEM)] * number


SMEM = pl.BlockSpec(memory_space=pltpu.SMEM)
ANY = pl.BlockSpec(memory_space=pl.ANY)


def local(observed_real, observed_imag, weights, taps):
    ahead_rows, ahead_lanes, back_lanes, back_rows, twist = dft_tables()
    count = weights.shape[0]
    reach = taps.shape[0] - 1
    parts = lax.axis_size("chan")
    devices = lax.axis_size("tm") * parts
    blocks = shape(count, ROWS, LANES)
    groups = lax.axis_size("tm")
    position = lax.axis_index(AXES)
    keep = jnp.stack([position > 0, position < devices - 1, position % 2 == 1]).astype(F32)
    place = lax.axis_index("chan").astype(jnp.int32).reshape(1)
    keep_group = (lax.axis_index("tm") < groups - 1).astype(F32).reshape(1)
    tables = (ahead_rows, ahead_lanes, back_lanes, back_rows, twist)

    def neighbours(block, edge):
        inside = [(i, i ^ 1) for i in range(devices)]
        across = [(i, min(max(((i + 1) ^ 1) - 1, 0), devices - 1)) for i in range(devices)]
        return lax.ppermute(block, AXES, inside), lax.ppermute(edge, AXES, across)

    def exchange(value, axis):
        return lax.all_to_all(value, axis, split_axis=0, concat_axis=0, tiled=True)

    seed_inputs = (observed_real, observed_imag, weights, back_lanes, back_rows, twist)
    seed_inputs = tuple(pltpu.with_memory_space_constraint(v, pltpu.HBM) for v in seed_inputs)
    edge = shape(count - 1, ROWS, LANES)
    seeds, edges = pl.pallas_call(
        seed_kernel,
        out_shape=(blocks, edge),
        in_specs=[pl.BlockSpec(memory_space=pltpu.HBM)] * 6,
        out_specs=tuple(vmem(2)),
        scratch_shapes=[pltpu.VMEM(value.shape, value.dtype) for value in seed_inputs]
        + [pltpu.VMEM((count * ROWS, LANES), F32), pltpu.SemaphoreType.DMA((9,))],
        compiler_params=params(),
        name="seed",
    )(*seed_inputs)
    inside, across = neighbours(seeds, edges)
    weights, taps = pl.pallas_call(
        arrange_kernel,
        out_shape=(blocks, shape((reach + 1) * ROWS, LANES)),
        in_specs=vmem(2),
        out_specs=tuple(vmem(2)),
        scratch_shapes=[pltpu.VMEM((count * ROWS, LANES), F32)],
        compiler_params=params(),
        cost_estimate=pl.CostEstimate(flops=10**7, bytes_accessed=2 * 10**6, transcendentals=0),
        name="arrange",
    )(weights, taps)
    taps = taps.reshape(reach + 1, ROWS, LANES)

    images, edges, side = pl.pallas_call(
        first_kernel,
        out_shape=(blocks, edge, shape(reach + count, ROWS, LANES)),
        in_specs=[SMEM] + vmem(10),
        out_specs=tuple(vmem(3)),
        scratch_shapes=[pltpu.VMEM((count, ROWS, LANES), F32)],
        compiler_params=params(),
        name="first",
    )(keep, inside, seeds, across, taps, weights, *tables)
    inside, across = neighbours(images, edges)

    outgoing, *lanes = pl.pallas_call(
        second_kernel,
        out_shape=(shape(parts, count + 1, 8, LANES),) + (shape(2 * count, 8, LANES),) * 8,
        in_specs=[SMEM, SMEM] + vmem(11),
        out_specs=tuple(vmem(9)),
        scratch_shapes=[
            pltpu.VMEM((count, ROWS, LANES), F32),
            pltpu.VMEM((3, 8, LANES), F32),
            pltpu.VMEM((parts, 2 * count, 8, LANES), F32),
        ],
        compiler_params=params(),
        name="second",
    )(place, keep, inside, images, across, side, taps, weights, *tables)

    moved = exchange(outgoing, "chan")
    moved, lanes = lax.optimization_barrier((moved, lanes))
    lanes = lanes[:1] + [
        lax.ppermute(lanes[d], AXES, [(i, i ^ d) for i in range(devices)]) for d in range(1, 8)
    ]
    after, sums = pl.pallas_call(
        tail_kernel,
        out_shape=(shape(count, 8, LANES), shape(groups, 4, LANES)),
        in_specs=vmem(1) + [ANY, ANY],
        out_specs=tuple(vmem(2)),
        compiler_params=params(),
        name="tail",
    )(moved, lanes[1], lanes[2])
    after = lax.ppermute(after, "tm", [(i + 1, i) for i in range(groups - 1)])
    sums = exchange(sums, "tm")
    return pl.pallas_call(
        last_kernel,
        out_shape=(shape(parts * count, 8 * LANES), shape(parts * count, 8 * LANES)),
        in_specs=[SMEM, SMEM] + vmem(12),
        out_specs=(pl.BlockSpec(memory_space=pltpu.HBM),) * 2,
        scratch_shapes=[
            pltpu.VMEM((count * 8, LANES), F32),
            pltpu.VMEM((count * 8, LANES), F32),
            pltpu.VMEM((parts, 2 * count, 8, LANES), F32),
            pltpu.VMEM((parts * count, 8 * LANES), F32),
            pltpu.VMEM((parts * count, 8 * LANES), F32),
            pltpu.SemaphoreType.DMA((2, parts)),
        ],
        compiler_params=params(),
        name="last",
    )(place, keep_group, moved, after, sums, taps, *lanes)


def solution(mesh):
    placed = (P(AXES, None), P(AXES, None), P(AXES, None), P())
    return jax.shard_map(
        local,
        mesh=mesh,
        in_specs=placed,
        out_specs=(P("tm", "chan"), P("tm", "chan")),
        check_vma=False,
    )
```

```python
import functools
import math

import jax
import jax.numpy as jnp
import numpy as np
from jax import lax
from jax.experimental import pallas as pl
from jax.experimental.pallas import tpu as pltpu
from jax.sharding import PartitionSpec as P

RIDGE = 0.25
ROWS = 64
LANES = 128
CHUNK = 16
F32 = jnp.float32
BF16 = jnp.bfloat16
AXES = ("tm", "chan")
VMEM_BYTES = 16 * 1024 * 1024


def params(limit=VMEM_BYTES):
    return pltpu.CompilerParams(vmem_limit_bytes=limit)


def halves(table):
    high = table.astype(np.float32).astype(jnp.bfloat16)
    low = (table - high.astype(np.float64)).astype(np.float32).astype(jnp.bfloat16)
    return high, low


def dft_tables():
    n1 = np.arange(ROWS)
    n2 = np.arange(LANES)
    k1 = np.arange(ROWS)
    k2 = (2 * np.arange(32)[None, :] + np.arange(2)[:, None]).reshape(-1)
    first = 2.0 * np.pi * (n1[:, None] * k1[None, :] % ROWS) / ROWS
    back_rows = np.concatenate([np.cos(first), -np.sin(first)], 1)
    second = 2.0 * np.pi * (k2[:, None] * n2[None, :] % LANES) / LANES
    scale = 1.0 / math.sqrt(ROWS * ROWS)
    cos = (np.cos(second) * scale).reshape(2, 32, LANES)
    sin = (np.sin(second) * scale).reshape(2, 32, LANES)
    from_real = np.concatenate([cos, sin], 2)
    from_imag = np.concatenate([-sin, cos], 2)
    back_lanes = np.stack([from_real, from_imag], 1).reshape(LANES, 2 * LANES)
    rows_high, rows_low = halves(back_rows)
    lanes_high, lanes_low = halves(back_lanes)
    twist = 2.0 * np.pi * k1[:, None] * n2[None, :] / (ROWS * LANES)
    return (
        np.concatenate([rows_high.T, rows_high.T, rows_low.T], 1),
        np.concatenate([lanes_high.T, lanes_low.T], 1),
        np.concatenate([lanes_high, lanes_high, lanes_low], 0),
        np.block([[rows_high, rows_high], [rows_low, np.zeros_like(rows_low)]]),
        np.stack([np.cos(twist), np.sin(twist)]).astype(np.float32),
    )


def split(value):
    high = value.astype(BF16)
    low = (value - high.astype(F32)).astype(BF16)
    return high, low


def dot(left, right):
    return jnp.dot(left, right, preferred_element_type=F32)


def forward_chunk(frames, ahead_rows, ahead_lanes, cos, sin):
    high, low = split(jnp.concatenate(frames, 1))
    mixed = dot(ahead_rows, jnp.concatenate([high, low, high], 0))
    turned = []
    for f in range(len(frames)):
        real = mixed[:ROWS, f * LANES : (f + 1) * LANES]
        imag = mixed[ROWS:, f * LANES : (f + 1) * LANES]
        turned.append(jnp.concatenate([real * cos + imag * sin, imag * cos - real * sin], 1))
    high, low = split(jnp.concatenate(turned, 0))
    wide = dot(high, ahead_lanes)
    return wide[:, :LANES] + wide[:, LANES:] + dot(low, ahead_lanes[:, :LANES])


def backward_chunk(spectra, back_lanes, back_rows, cos, sin):
    high, low = split(spectra)
    mixed = dot(jnp.concatenate([high, low, high], 1), back_lanes)
    turned = []
    for f in range(spectra.shape[0] // ROWS):
        real = mixed[f * ROWS : (f + 1) * ROWS, :LANES]
        imag = mixed[f * ROWS : (f + 1) * ROWS, LANES:]
        turned.append(jnp.concatenate([real * cos - imag * sin, real * sin + imag * cos], 0))
    high, low = split(jnp.concatenate(turned, 1))
    tall = dot(back_rows, jnp.concatenate([high, low], 0))
    return tall[:ROWS] + tall[ROWS:]


def turn_pair(block):
    flipped = block.T
    low_half = flipped[:ROWS]
    high_half = flipped[ROWS:]
    left = lax.broadcasted_iota(jnp.int32, (ROWS, LANES), 1) < ROWS
    return (
        jnp.where(left, low_half, pltpu.roll(high_half, ROWS, 1)),
        jnp.where(left, pltpu.roll(low_half, ROWS, 1), high_half),
    )


def seed_kernel(*refs):
    sources, out_ref, places, held, semaphore = refs[:6], refs[6], refs[7:13], refs[13], refs[14]
    copies = [
        pltpu.make_async_copy(source, place, semaphore.at[at])
        for at, (source, place) in enumerate(zip(sources, places))
    ]
    for copy in copies:
        copy.start()
    real_ref, imag_ref, weights_ref, back_lanes_ref, back_rows_ref, twist_ref = places
    count = real_ref.shape[0]
    for copy in copies:
        copy.wait()
    for j in range(32):
        columns = slice(j * LANES, (j + 1) * LANES)
        weights = weights_ref[:, columns]
        held[pl.ds(j, count, stride=ROWS), :] = weights * real_ref[:, columns]
        held[pl.ds(32 + j, count, stride=ROWS), :] = weights * imag_ref[:, columns]
    cos = twist_ref[0]
    sin = twist_ref[1]
    for start in range(0, count, CHUNK):
        spectra = []
        for f in range(start, start + CHUNK, 2):
            spectra += turn_pair(held[f * ROWS : (f + 2) * ROWS, :])
        frames = backward_chunk(
            jnp.concatenate(spectra, 0), back_lanes_ref[...], back_rows_ref[...], cos, sin
        )
        for f in range(CHUNK):
            out_ref[start + f] = frames[:, f * LANES : (f + 1) * LANES]


def arrange_kernel(weights_ref, taps_ref, weights_out, taps_out, held):
    count = weights_ref.shape[0]
    for j in range(32):
        weights = weights_ref[:, j * LANES : (j + 1) * LANES]
        held[pl.ds(j, count, stride=ROWS), :] = weights
        held[pl.ds(32 + j, count, stride=ROWS), :] = weights
    for f in range(0, count, 2):
        first, second = turn_pair(held[f * ROWS : (f + 2) * ROWS, :])
        weights_out[f] = first
        weights_out[f + 1] = second
    for n1 in range(ROWS):
        taps_out[pl.ds(n1, taps_ref.shape[0], stride=ROWS), :] = taps_ref[
            :, n1 * LANES : (n1 + 1) * LANES
        ]


def weighted_sum(taps, values):
    total = taps[0] * values[0]
    for tap, value in zip(taps[1:], values[1:]):
        total = total + tap * value
    return total


def back_filter(rows, taps, inside_ref, here_ref, across_ref, keep):
    reach = len(taps) - 1
    count = here_ref.shape[0]
    odd = jnp.full((8, LANES), keep[2]) > 0.5
    frames = [
        jnp.where(odd, inside_ref[t, rows, :], across_ref[t, rows, :]) for t in range(count - reach, count)
    ]
    frames += [here_ref[t, rows, :] for t in range(count)]
    frames += [
        jnp.where(odd, across_ref[t, rows, :], inside_ref[t, rows, :]) * keep[1] for t in range(reach)
    ]
    result = []
    for at in range(reach + count):
        total = weighted_sum(taps, frames[at : at + reach + 1])
        result.append(total * keep[0] if at < reach else total)
    return result


def ahead_filter(taps, frames):
    reach = len(taps) - 1
    return [
        weighted_sum(taps, [frames[at + reach - tap] for tap in range(reach + 1)])
        for at in range(len(frames) - reach)
    ]


def first_kernel(
    keep_ref, inside_ref, here_ref, across_ref, taps_ref, weights_ref,
    ahead_rows_ref, ahead_lanes_ref, back_lanes_ref, back_rows_ref, twist_ref,
    out_ref, side_ref, filtered,
):
    count = here_ref.shape[0]
    keep = (keep_ref[0], keep_ref[1], keep_ref[2])

    @pl.loop(0, ROWS // 8)
    def _(group):
        rows = pl.ds(pl.multiple_of(group * 8, 8), 8)
        taps = [taps_ref[p, rows, :] for p in range(taps_ref.shape[0])]
        side = back_filter(rows, taps, inside_ref, here_ref, across_ref, keep)
        for at, value in enumerate(side):
            side_ref[at, rows, :] = value
        for at, value in enumerate(ahead_filter(taps, side)):
            filtered[at, rows, :] = value

    cos = twist_ref[0]
    sin = twist_ref[1]
    for start in range(0, count, CHUNK):
        spectra = forward_chunk(
            [filtered[start + f] for f in range(CHUNK)], ahead_rows_ref[...], ahead_lanes_ref[...], cos, sin
        )
        weights = weights_ref[start : start + CHUNK].reshape(CHUNK * ROWS, LANES)
        frames = backward_chunk(spectra * weights, back_lanes_ref[...], back_rows_ref[...], cos, sin)
        for f in range(CHUNK):
            out_ref[start + f] = frames[:, f * LANES : (f + 1) * LANES]


def quarters(rows):
    return lax.broadcasted_iota(jnp.int32, (rows, LANES), 1) // 32


def pack(values):
    packed = jnp.zeros((8, LANES), F32)
    for at, value in enumerate(values):
        value = value + pltpu.roll(value, 64, 1)
        value = value + pltpu.roll(value, 32, 1)
        packed = jnp.where(quarters(8) == at, value, packed)
    return packed


def second_kernel(
    place_ref, keep_ref, inside_ref, here_ref, across_ref, side_ref, taps_ref, weights_ref,
    ahead_rows_ref, ahead_lanes_ref, back_lanes_ref, back_rows_ref, twist_ref,
    out_ref, *rest,
):
    own_ref, other_ref, filtered, sums, staged = rest
    count = here_ref.shape[0]
    keep = (keep_ref[0], keep_ref[1], keep_ref[2])
    reach = taps_ref.shape[0] - 1
    sums[...] = jnp.zeros_like(sums)

    @pl.loop(0, ROWS // 8)
    def _(group):
        rows = pl.ds(pl.multiple_of(group * 8, 8), 8)
        taps = [taps_ref[p, rows, :] for p in range(reach + 1)]
        image = back_filter(rows, taps, inside_ref, here_ref, across_ref, keep)
        side = [side_ref[at, rows, :] for at in range(reach + count)]
        image = [value + RIDGE * base for value, base in zip(image, side)]
        for at, value in enumerate(ahead_filter(taps, image)):
            filtered[at, rows, :] = value
        first, second, third = sums[0], sums[1], sums[2]
        for at in range(count):
            base = side[reach + at]
            value = image[reach + at]
            staged[group ^ place_ref[0], at] = base
            staged[group ^ place_ref[0], count + at] = value
            first = first + base * base
            second = second + base * value
            third = third + value * value
        sums[0] = first
        sums[1] = second
        sums[2] = third

    for e in range(4):
        own_ref[e] = staged[2 * e]
        other_ref[e] = staged[2 * e + 1]
    cos = twist_ref[0]
    sin = twist_ref[1]
    power = jnp.zeros((8, LANES), F32)
    for start in range(0, count, CHUNK):
        spectra = forward_chunk(
            [filtered[start + f] for f in range(CHUNK)], ahead_rows_ref[...], ahead_lanes_ref[...], cos, sin
        )
        weights = weights_ref[start : start + CHUNK].reshape(CHUNK * ROWS, LANES)
        weighted = spectra * weights
        power = power + jnp.sum((weighted * spectra).reshape(CHUNK * ROWS // 8, 8, LANES), 0)
        frames = backward_chunk(weighted, back_lanes_ref[...], back_rows_ref[...], cos, sin)
        for f in range(CHUNK):
            for group in range(ROWS // 8):
                out_ref[group, start + f] = frames[
                    group * 8 : (group + 1) * 8, f * LANES : (f + 1) * LANES
                ]
    totals = pack([sums[0], sums[1], sums[2], power])
    for group in range(ROWS // 8):
        out_ref[group, count] = totals


def join_kernel(own_ref, other_ref, *outputs):
    slots = own_ref.shape[1]
    for e, output in enumerate(outputs):
        output[:slots] = own_ref[e + 1]
        output[slots:] = other_ref[e + 1]


def tail_kernel(moved_ref, _, frames_ref, sums_ref):
    count = frames_ref.shape[0]
    frames_ref[...] = moved_ref[0, :count]
    total = moved_ref[0, count]
    for part in range(1, moved_ref.shape[0]):
        total = total + moved_ref[part, count]
    sums_ref[...] = jnp.broadcast_to((total[:4] + total[4:])[None], sums_ref.shape)


def last_kernel(place_ref, keep_ref, moved_ref, after_ref, sums_ref, taps_ref, *rest):
    own_ref, other_ref, *lanes = rest[:5]
    solution_ref, residual_ref, kept, left, pairs = rest[5:]
    parts, count = moved_ref.shape[0], moved_ref.shape[1] - 1
    reach = taps_ref.shape[0] - 1
    rows = pl.ds(pl.multiple_of(place_ref[0] * 8, 8), 8)
    pairs[place_ref[0]] = own_ref[0]
    pairs[place_ref[0] ^ 1] = other_ref[0]
    for e, lane in enumerate(lanes):
        pairs[place_ref[0] ^ (2 * e + 2)] = lane[: 2 * count]
        pairs[place_ref[0] ^ (2 * e + 3)] = lane[2 * count :]
    sums = jnp.sum(sums_ref[...], 0)
    norm, curve, square, power = (
        jnp.sum(jnp.sum(jnp.where(quarters(4) == at, sums, 0.0), 1, keepdims=True), 0, keepdims=True)
        for at in range(4)
    )
    cube = power + RIDGE * square
    step = norm / curve
    next_norm = step * step * square - norm
    grown = step * square / curve
    next_step = next_norm / (step * (step * cube - grown * square))
    to_base = step + next_step * grown
    to_image = -(next_step * step)
    image_rate = -(step + next_step * grown)
    cube_rate = next_step * step
    to_base, to_image, image_rate, cube_rate = (
        jnp.broadcast_to(value, (8, LANES)) for value in (to_base, to_image, image_rate, cube_rate)
    )
    taps = [taps_ref[p, rows, :] for p in range(reach + 1)]

    def finish(part, tail):
        frames = [moved_ref[part, t] for t in range(count)] + tail
        for at in range(count):
            base = pairs[part, at]
            image = pairs[part, count + at]
            again = weighted_sum(taps, frames[at : at + reach + 1]) + RIDGE * image
            here = pl.ds(pl.multiple_of((part * count + at) * 8, 8), 8)
            kept[here, :] = to_base * base + to_image * image
            left[here, :] = base + image_rate * image + cube_rate * again

    @pl.loop(0, parts - 1)
    def _(part):
        finish(part, [moved_ref[part + 1, t] for t in range(reach)])

    finish(parts - 1, [after_ref[t] * keep_ref[0] for t in range(reach)])

    for block in range(parts * count // 8):
        for n1 in range(8):
            places = pl.ds(block * 64 + n1, 8, stride=8)
            columns = slice(n1 * LANES, (n1 + 1) * LANES)
            solution_ref[block * 8 : (block + 1) * 8, columns] = kept[places, :]
            residual_ref[block * 8 : (block + 1) * 8, columns] = left[places, :]


def shape(*dims):
    return jax.ShapeDtypeStruct(dims, F32)


def vmem(number):
    return [pl.BlockSpec(memory_space=pltpu.VMEM)] * number


SMEM = pl.BlockSpec(memory_space=pltpu.SMEM)
ANY = pl.BlockSpec(memory_space=pl.ANY)


def local(observed_real, observed_imag, weights, taps):
    ahead_rows, ahead_lanes, back_lanes, back_rows, twist = dft_tables()
    count = weights.shape[0]
    reach = taps.shape[0] - 1
    parts = lax.axis_size("chan")
    devices = lax.axis_size("tm") * parts
    blocks = shape(count, ROWS, LANES)
    groups = lax.axis_size("tm")
    position = lax.axis_index(AXES)
    keep = jnp.stack([position > 0, position < devices - 1, position % 2 == 1]).astype(F32)
    place = lax.axis_index("chan").astype(jnp.int32).reshape(1)
    keep_group = (lax.axis_index("tm") < groups - 1).astype(F32).reshape(1)
    tables = (ahead_rows, ahead_lanes, back_lanes, back_rows, twist)

    def neighbours(block):
        inside = [(i, i ^ 1) for i in range(devices)]
        across = [(i, min(max(((i + 1) ^ 1) - 1, 0), devices - 1)) for i in range(devices)]
        return lax.ppermute(block, AXES, inside), lax.ppermute(block, AXES, across)

    def exchange(value, axis):
        return lax.all_to_all(value, axis, split_axis=0, concat_axis=0, tiled=True)

    seed_inputs = (observed_real, observed_imag, weights, back_lanes, back_rows, twist)
    seed_inputs = tuple(pltpu.with_memory_space_constraint(v, pltpu.HBM) for v in seed_inputs)
    seeds = pl.pallas_call(
        seed_kernel,
        out_shape=blocks,
        in_specs=[pl.BlockSpec(memory_space=pltpu.HBM)] * 6,
        out_specs=vmem(1)[0],
        scratch_shapes=[pltpu.VMEM(value.shape, value.dtype) for value in seed_inputs]
        + [pltpu.VMEM((count * ROWS, LANES), F32), pltpu.SemaphoreType.DMA((6,))],
        compiler_params=params(),
        name="seed",
    )(*seed_inputs)
    inside, across = neighbours(seeds)
    weights, taps = pl.pallas_call(
        arrange_kernel,
        out_shape=(blocks, shape((reach + 1) * ROWS, LANES)),
        in_specs=vmem(2),
        out_specs=tuple(vmem(2)),
        scratch_shapes=[pltpu.VMEM((count * ROWS, LANES), F32)],
        compiler_params=params(),
        cost_estimate=pl.CostEstimate(flops=10**7, bytes_accessed=2 * 10**6, transcendentals=0),
        name="arrange",
    )(weights, taps)
    taps = taps.reshape(reach + 1, ROWS, LANES)

    images, side = pl.pallas_call(
        first_kernel,
        out_shape=(blocks, shape(reach + count, ROWS, LANES)),
        in_specs=[SMEM] + vmem(10),
        out_specs=tuple(vmem(2)),
        scratch_shapes=[pltpu.VMEM((count, ROWS, LANES), F32)],
        compiler_params=params(),
        name="first",
    )(keep, inside, seeds, across, taps, weights, *tables)
    inside, across = neighbours(images)

    outgoing, own, other = pl.pallas_call(
        second_kernel,
        out_shape=(shape(parts, count + 1, 8, LANES),) + (shape(4, 2 * count, 8, LANES),) * 2,
        in_specs=[SMEM, SMEM] + vmem(11),
        out_specs=tuple(vmem(3)),
        scratch_shapes=[
            pltpu.VMEM((count, ROWS, LANES), F32),
            pltpu.VMEM((3, 8, LANES), F32),
            pltpu.VMEM((parts, 2 * count, 8, LANES), F32),
        ],
        compiler_params=params(),
        name="second",
    )(place, keep, inside, images, across, side, taps, weights, *tables)

    moved = exchange(outgoing, "chan")
    other = lax.ppermute(other, AXES, [(i, i ^ 1) for i in range(devices)])
    moved, own, other = lax.optimization_barrier((moved, own, other))
    lanes = pl.pallas_call(
        join_kernel,
        out_shape=(shape(4 * count, 8, LANES),) * 3,
        in_specs=vmem(2),
        out_specs=tuple(vmem(3)),
        compiler_params=params(),
        name="join",
    )(own, other)
    lanes = [
        lax.ppermute(lane, AXES, [(i, i ^ (2 * e + 2)) for i in range(devices)])
        for e, lane in enumerate(lanes)
    ]
    after, sums = pl.pallas_call(
        tail_kernel,
        out_shape=(shape(count, 8, LANES), shape(groups, 4, LANES)),
        in_specs=vmem(1) + [ANY],
        out_specs=tuple(vmem(2)),
        compiler_params=params(),
        name="tail",
    )(moved, lanes[0])
    after = lax.ppermute(after, "tm", [(i + 1, i) for i in range(groups - 1)])
    sums = exchange(sums, "tm")
    return pl.pallas_call(
        last_kernel,
        out_shape=(shape(parts * count, 8 * LANES), shape(parts * count, 8 * LANES)),
        in_specs=[SMEM, SMEM] + vmem(9),
        out_specs=tuple(vmem(2)),
        scratch_shapes=[
            pltpu.VMEM((parts * count * 8, LANES), F32),
            pltpu.VMEM((parts * count * 8, LANES), F32),
            pltpu.VMEM((parts, 2 * count, 8, LANES), F32),
        ],
        compiler_params=params(),
        name="last",
    )(place, keep_group, moved, after, sums, taps, own, other, *lanes)


def solution(mesh):
    placed = (P(AXES, None), P(AXES, None), P(AXES, None), P())
    return jax.shard_map(
        local,
        mesh=mesh,
        in_specs=placed,
        out_specs=(P("tm", "chan"), P("tm", "chan")),
        check_vma=False,
    )
```

```python
import functools
import math

import jax
import jax.numpy as jnp
import numpy as np
from jax import lax
from jax.experimental import pallas as pl
from jax.experimental.pallas import tpu as pltpu
from jax.sharding import PartitionSpec as P

RIDGE = 0.25
ROWS = 64
LANES = 128
CHUNK = 16
F32 = jnp.float32
BF16 = jnp.bfloat16
AXES = ("tm", "chan")
VMEM_BYTES = 16 * 1024 * 1024


def params(limit=VMEM_BYTES):
    return pltpu.CompilerParams(vmem_limit_bytes=limit)


def halves(table):
    high = table.astype(np.float32).astype(jnp.bfloat16)
    low = (table - high.astype(np.float64)).astype(np.float32).astype(jnp.bfloat16)
    return high, low


def dft_tables():
    n1 = np.arange(ROWS)
    n2 = np.arange(LANES)
    k1 = np.arange(ROWS)
    k2 = (2 * np.arange(32)[None, :] + np.arange(2)[:, None]).reshape(-1)
    first = 2.0 * np.pi * (n1[:, None] * k1[None, :] % ROWS) / ROWS
    back_rows = np.concatenate([np.cos(first), -np.sin(first)], 1)
    second = 2.0 * np.pi * (k2[:, None] * n2[None, :] % LANES) / LANES
    scale = 1.0 / math.sqrt(ROWS * ROWS)
    cos = (np.cos(second) * scale).reshape(2, 32, LANES)
    sin = (np.sin(second) * scale).reshape(2, 32, LANES)
    from_real = np.concatenate([cos, sin], 2)
    from_imag = np.concatenate([-sin, cos], 2)
    back_lanes = np.stack([from_real, from_imag], 1).reshape(LANES, 2 * LANES)
    rows_high, rows_low = halves(back_rows)
    lanes_high, lanes_low = halves(back_lanes)
    twist = 2.0 * np.pi * k1[:, None] * n2[None, :] / (ROWS * LANES)
    return (
        np.concatenate([rows_high.T, rows_high.T, rows_low.T], 1),
        np.concatenate([lanes_high.T, lanes_low.T], 1),
        np.concatenate([lanes_high, lanes_high, lanes_low], 0),
        np.block([[rows_high, rows_high], [rows_low, np.zeros_like(rows_low)]]),
        np.stack([np.cos(twist), np.sin(twist)]).astype(np.float32),
    )


def split(value):
    high = value.astype(BF16)
    low = (value - high.astype(F32)).astype(BF16)
    return high, low


def dot(left, right):
    return jnp.dot(left, right, preferred_element_type=F32)


def forward_chunk(frames, ahead_rows, ahead_lanes, cos, sin):
    high, low = split(jnp.concatenate(frames, 1))
    mixed = dot(ahead_rows, jnp.concatenate([high, low, high], 0))
    turned = []
    for f in range(len(frames)):
        real = mixed[:ROWS, f * LANES : (f + 1) * LANES]
        imag = mixed[ROWS:, f * LANES : (f + 1) * LANES]
        turned.append(jnp.concatenate([real * cos + imag * sin, imag * cos - real * sin], 1))
    high, low = split(jnp.concatenate(turned, 0))
    wide = dot(high, ahead_lanes)
    return wide[:, :LANES] + wide[:, LANES:] + dot(low, ahead_lanes[:, :LANES])


def backward_chunk(spectra, back_lanes, back_rows, cos, sin):
    high, low = split(spectra)
    mixed = dot(jnp.concatenate([high, low, high], 1), back_lanes)
    turned = []
    for f in range(spectra.shape[0] // ROWS):
        real = mixed[f * ROWS : (f + 1) * ROWS, :LANES]
        imag = mixed[f * ROWS : (f + 1) * ROWS, LANES:]
        turned.append(jnp.concatenate([real * cos - imag * sin, real * sin + imag * cos], 0))
    high, low = split(jnp.concatenate(turned, 1))
    tall = dot(back_rows, jnp.concatenate([high, low], 0))
    return tall[:ROWS] + tall[ROWS:]


def turn_pair(block):
    flipped = block.T
    low_half = flipped[:ROWS]
    high_half = flipped[ROWS:]
    left = lax.broadcasted_iota(jnp.int32, (ROWS, LANES), 1) < ROWS
    return (
        jnp.where(left, low_half, pltpu.roll(high_half, ROWS, 1)),
        jnp.where(left, pltpu.roll(low_half, ROWS, 1), high_half),
    )


def seed_kernel(*refs):
    sources, out_ref, places, held, semaphore = refs[:6], refs[6], refs[7:13], refs[13], refs[14]
    copies = [
        pltpu.make_async_copy(source, place, semaphore.at[at])
        for at, (source, place) in enumerate(zip(sources, places))
    ]
    for copy in copies:
        copy.start()
    real_ref, imag_ref, weights_ref, back_lanes_ref, back_rows_ref, twist_ref = places
    count = real_ref.shape[0]
    for copy in copies:
        copy.wait()
    for j in range(32):
        columns = slice(j * LANES, (j + 1) * LANES)
        weights = weights_ref[:, columns]
        held[pl.ds(j, count, stride=ROWS), :] = weights * real_ref[:, columns]
        held[pl.ds(32 + j, count, stride=ROWS), :] = weights * imag_ref[:, columns]
    cos = twist_ref[0]
    sin = twist_ref[1]
    for start in range(0, count, CHUNK):
        spectra = []
        for f in range(start, start + CHUNK, 2):
            spectra += turn_pair(held[f * ROWS : (f + 2) * ROWS, :])
        frames = backward_chunk(
            jnp.concatenate(spectra, 0), back_lanes_ref[...], back_rows_ref[...], cos, sin
        )
        for f in range(CHUNK):
            out_ref[start + f] = frames[:, f * LANES : (f + 1) * LANES]


def arrange_kernel(weights_ref, taps_ref, weights_out, taps_out, held):
    count = weights_ref.shape[0]
    for j in range(32):
        weights = weights_ref[:, j * LANES : (j + 1) * LANES]
        held[pl.ds(j, count, stride=ROWS), :] = weights
        held[pl.ds(32 + j, count, stride=ROWS), :] = weights
    for f in range(0, count, 2):
        first, second = turn_pair(held[f * ROWS : (f + 2) * ROWS, :])
        weights_out[f] = first
        weights_out[f + 1] = second
    for n1 in range(ROWS):
        taps_out[pl.ds(n1, taps_ref.shape[0], stride=ROWS), :] = taps_ref[
            :, n1 * LANES : (n1 + 1) * LANES
        ]


def weighted_sum(taps, values):
    total = taps[0] * values[0]
    for tap, value in zip(taps[1:], values[1:]):
        total = total + tap * value
    return total


def back_filter(rows, taps, inside_ref, here_ref, across_ref, keep):
    reach = len(taps) - 1
    count = here_ref.shape[0]
    odd = jnp.full((8, LANES), keep[2]) > 0.5
    frames = [
        jnp.where(odd, inside_ref[t, rows, :], across_ref[t, rows, :]) for t in range(count - reach, count)
    ]
    frames += [here_ref[t, rows, :] for t in range(count)]
    frames += [
        jnp.where(odd, across_ref[t, rows, :], inside_ref[t, rows, :]) * keep[1] for t in range(reach)
    ]
    result = []
    for at in range(reach + count):
        total = weighted_sum(taps, frames[at : at + reach + 1])
        result.append(total * keep[0] if at < reach else total)
    return result


def ahead_filter(taps, frames):
    reach = len(taps) - 1
    return [
        weighted_sum(taps, [frames[at + reach - tap] for tap in range(reach + 1)])
        for at in range(len(frames) - reach)
    ]


def first_kernel(
    keep_ref, inside_ref, here_ref, across_ref, taps_ref, weights_ref,
    ahead_rows_ref, ahead_lanes_ref, back_lanes_ref, back_rows_ref, twist_ref,
    out_ref, side_ref, filtered,
):
    count = here_ref.shape[0]
    keep = (keep_ref[0], keep_ref[1], keep_ref[2])

    @pl.loop(0, ROWS // 8)
    def _(group):
        rows = pl.ds(pl.multiple_of(group * 8, 8), 8)
        taps = [taps_ref[p, rows, :] for p in range(taps_ref.shape[0])]
        side = back_filter(rows, taps, inside_ref, here_ref, across_ref, keep)
        for at, value in enumerate(side):
            side_ref[at, rows, :] = value
        for at, value in enumerate(ahead_filter(taps, side)):
            filtered[at, rows, :] = value

    cos = twist_ref[0]
    sin = twist_ref[1]
    for start in range(0, count, CHUNK):
        spectra = forward_chunk(
            [filtered[start + f] for f in range(CHUNK)], ahead_rows_ref[...], ahead_lanes_ref[...], cos, sin
        )
        weights = weights_ref[start : start + CHUNK].reshape(CHUNK * ROWS, LANES)
        frames = backward_chunk(spectra * weights, back_lanes_ref[...], back_rows_ref[...], cos, sin)
        for f in range(CHUNK):
            out_ref[start + f] = frames[:, f * LANES : (f + 1) * LANES]


def quarters(rows):
    return lax.broadcasted_iota(jnp.int32, (rows, LANES), 1) // 32


def pack(values):
    packed = jnp.zeros((8, LANES), F32)
    for at, value in enumerate(values):
        value = value + pltpu.roll(value, 64, 1)
        value = value + pltpu.roll(value, 32, 1)
        packed = jnp.where(quarters(8) == at, value, packed)
    return packed


def second_kernel(
    place_ref, keep_ref, inside_ref, here_ref, across_ref, side_ref, taps_ref, weights_ref,
    ahead_rows_ref, ahead_lanes_ref, back_lanes_ref, back_rows_ref, twist_ref,
    out_ref, *rest,
):
    own_ref, other_ref, filtered, sums, staged = rest
    count = here_ref.shape[0]
    keep = (keep_ref[0], keep_ref[1], keep_ref[2])
    reach = taps_ref.shape[0] - 1
    sums[...] = jnp.zeros_like(sums)

    @pl.loop(0, ROWS // 8)
    def _(group):
        rows = pl.ds(pl.multiple_of(group * 8, 8), 8)
        taps = [taps_ref[p, rows, :] for p in range(reach + 1)]
        image = back_filter(rows, taps, inside_ref, here_ref, across_ref, keep)
        side = [side_ref[at, rows, :] for at in range(reach + count)]
        image = [value + RIDGE * base for value, base in zip(image, side)]
        for at, value in enumerate(ahead_filter(taps, image)):
            filtered[at, rows, :] = value
        first, second, third = sums[0], sums[1], sums[2]
        for at in range(count):
            base = side[reach + at]
            value = image[reach + at]
            staged[group ^ place_ref[0], at] = base
            staged[group ^ place_ref[0], count + at] = value
            first = first + base * base
            second = second + base * value
            third = third + value * value
        sums[0] = first
        sums[1] = second
        sums[2] = third

    for e in range(4):
        own_ref[e] = staged[2 * e]
        other_ref[e] = staged[2 * e + 1]
    cos = twist_ref[0]
    sin = twist_ref[1]
    power = jnp.zeros((8, LANES), F32)
    for start in range(0, count, CHUNK):
        spectra = forward_chunk(
            [filtered[start + f] for f in range(CHUNK)], ahead_rows_ref[...], ahead_lanes_ref[...], cos, sin
        )
        weights = weights_ref[start : start + CHUNK].reshape(CHUNK * ROWS, LANES)
        weighted = spectra * weights
        power = power + jnp.sum((weighted * spectra).reshape(CHUNK * ROWS // 8, 8, LANES), 0)
        frames = backward_chunk(weighted, back_lanes_ref[...], back_rows_ref[...], cos, sin)
        for f in range(CHUNK):
            for group in range(ROWS // 8):
                out_ref[group, start + f] = frames[
                    group * 8 : (group + 1) * 8, f * LANES : (f + 1) * LANES
                ]
    totals = pack([sums[0], sums[1], sums[2], power])
    for group in range(ROWS // 8):
        out_ref[group, count] = totals


def join_kernel(own_ref, other_ref, *outputs):
    slots = own_ref.shape[1]
    for e, output in enumerate(outputs):
        output[:slots] = own_ref[e + 1]
        output[slots:] = other_ref[e + 1]


def tail_kernel(moved_ref, _, frames_ref, sums_ref):
    count = frames_ref.shape[0]
    frames_ref[...] = moved_ref[0, :count]
    total = moved_ref[0, count]
    for part in range(1, moved_ref.shape[0]):
        total = total + moved_ref[part, count]
    sums_ref[...] = jnp.broadcast_to((total[:4] + total[4:])[None], sums_ref.shape)


def last_kernel(place_ref, keep_ref, moved_ref, after_ref, sums_ref, taps_ref, *rest):
    own_ref, other_ref, *lanes = rest[:5]
    solution_ref, residual_ref, kept, left, pairs = rest[5:]
    parts, count = moved_ref.shape[0], moved_ref.shape[1] - 1
    reach = taps_ref.shape[0] - 1
    rows = pl.ds(pl.multiple_of(place_ref[0] * 8, 8), 8)
    pairs[place_ref[0]] = own_ref[0]
    pairs[place_ref[0] ^ 1] = other_ref[0]
    for e, lane in enumerate(lanes):
        pairs[place_ref[0] ^ (2 * e + 2)] = lane[: 2 * count]
        pairs[place_ref[0] ^ (2 * e + 3)] = lane[2 * count :]
    sums = jnp.sum(sums_ref[...], 0)
    norm, curve, square, power = (
        jnp.sum(jnp.sum(jnp.where(quarters(4) == at, sums, 0.0), 1, keepdims=True), 0, keepdims=True)
        for at in range(4)
    )
    cube = power + RIDGE * square
    step = norm / curve
    next_norm = step * step * square - norm
    grown = step * square / curve
    next_step = next_norm / (step * (step * cube - grown * square))
    to_base = step + next_step * grown
    to_image = -(next_step * step)
    image_rate = -(step + next_step * grown)
    cube_rate = next_step * step
    to_base, to_image, image_rate, cube_rate = (
        jnp.broadcast_to(value, (8, LANES)) for value in (to_base, to_image, image_rate, cube_rate)
    )
    taps = [taps_ref[p, rows, :] for p in range(reach + 1)]

    def finish(part, tail):
        frames = [moved_ref[part, t] for t in range(count)] + tail
        for at in range(count):
            base = pairs[part, at]
            image = pairs[part, count + at]
            again = weighted_sum(taps, frames[at : at + reach + 1]) + RIDGE * image
            here = pl.ds(pl.multiple_of((part * count + at) * 8, 8), 8)
            kept[here, :] = to_base * base + to_image * image
            left[here, :] = base + image_rate * image + cube_rate * again

    @pl.loop(0, parts - 1)
    def _(part):
        finish(part, [moved_ref[part + 1, t] for t in range(reach)])

    finish(parts - 1, [after_ref[t] * keep_ref[0] for t in range(reach)])

    for block in range(parts * count // 8):
        for n1 in range(8):
            places = pl.ds(block * 64 + n1, 8, stride=8)
            columns = slice(n1 * LANES, (n1 + 1) * LANES)
            solution_ref[block * 8 : (block + 1) * 8, columns] = kept[places, :]
            residual_ref[block * 8 : (block + 1) * 8, columns] = left[places, :]


def shape(*dims):
    return jax.ShapeDtypeStruct(dims, F32)


def vmem(number):
    return [pl.BlockSpec(memory_space=pltpu.VMEM)] * number


SMEM = pl.BlockSpec(memory_space=pltpu.SMEM)
ANY = pl.BlockSpec(memory_space=pl.ANY)


def local(observed_real, observed_imag, weights, taps):
    ahead_rows, ahead_lanes, back_lanes, back_rows, twist = dft_tables()
    count = weights.shape[0]
    reach = taps.shape[0] - 1
    parts = lax.axis_size("chan")
    devices = lax.axis_size("tm") * parts
    blocks = shape(count, ROWS, LANES)
    groups = lax.axis_size("tm")
    position = lax.axis_index(AXES)
    keep = jnp.stack([position > 0, position < devices - 1, position % 2 == 1]).astype(F32)
    place = lax.axis_index("chan").astype(jnp.int32).reshape(1)
    keep_group = (lax.axis_index("tm") < groups - 1).astype(F32).reshape(1)
    tables = (ahead_rows, ahead_lanes, back_lanes, back_rows, twist)

    def neighbours(block):
        inside = [(i, i ^ 1) for i in range(devices)]
        across = [(i, min(max(((i + 1) ^ 1) - 1, 0), devices - 1)) for i in range(devices)]
        return lax.ppermute(block, AXES, inside), lax.ppermute(block, AXES, across)

    def exchange(value, axis):
        return lax.all_to_all(value, axis, split_axis=0, concat_axis=0, tiled=True)

    seed_inputs = (observed_real, observed_imag, weights, back_lanes, back_rows, twist)
    seed_inputs = tuple(pltpu.with_memory_space_constraint(v, pltpu.HBM) for v in seed_inputs)
    seeds = pl.pallas_call(
        seed_kernel,
        out_shape=blocks,
        in_specs=[pl.BlockSpec(memory_space=pltpu.HBM)] * 6,
        out_specs=vmem(1)[0],
        scratch_shapes=[pltpu.VMEM(value.shape, value.dtype) for value in seed_inputs]
        + [pltpu.VMEM((count * ROWS, LANES), F32), pltpu.SemaphoreType.DMA((6,))],
        compiler_params=params(),
        name="seed",
    )(*seed_inputs)
    inside, across = neighbours(seeds)
    weights, taps = pl.pallas_call(
        arrange_kernel,
        out_shape=(blocks, shape((reach + 1) * ROWS, LANES)),
        in_specs=vmem(2),
        out_specs=tuple(vmem(2)),
        scratch_shapes=[pltpu.VMEM((count * ROWS, LANES), F32)],
        compiler_params=params(),
        cost_estimate=pl.CostEstimate(flops=10**7, bytes_accessed=2 * 10**6, transcendentals=0),
        name="arrange",
    )(weights, taps)
    taps = taps.reshape(reach + 1, ROWS, LANES)

    images, side = pl.pallas_call(
        first_kernel,
        out_shape=(blocks, shape(reach + count, ROWS, LANES)),
        in_specs=[SMEM] + vmem(10),
        out_specs=tuple(vmem(2)),
        scratch_shapes=[pltpu.VMEM((count, ROWS, LANES), F32)],
        compiler_params=params(),
        name="first",
    )(keep, inside, seeds, across, taps, weights, *tables)
    inside, across = neighbours(images)

    outgoing, own, other = pl.pallas_call(
        second_kernel,
        out_shape=(shape(parts, count + 1, 8, LANES),) + (shape(4, 2 * count, 8, LANES),) * 2,
        in_specs=[SMEM, SMEM] + vmem(11),
        out_specs=tuple(vmem(3)),
        scratch_shapes=[
            pltpu.VMEM((count, ROWS, LANES), F32),
            pltpu.VMEM((3, 8, LANES), F32),
            pltpu.VMEM((parts, 2 * count, 8, LANES), F32),
        ],
        compiler_params=params(),
        name="second",
    )(place, keep, inside, images, across, side, taps, weights, *tables)

    moved = exchange(outgoing, "chan")
    other = lax.ppermute(other, AXES, [(i, i ^ 1) for i in range(devices)])
    moved, own, other = lax.optimization_barrier((moved, own, other))
    lanes = pl.pallas_call(
        join_kernel,
        out_shape=(shape(4 * count, 8, LANES),) * 3,
        in_specs=vmem(2),
        out_specs=tuple(vmem(3)),
        compiler_params=params(),
        name="join",
    )(own, other)
    joined = lanes[0]
    lanes = [
        lax.ppermute(lane, AXES, [(i, i ^ (2 * e + 2)) for i in range(devices)])
        for e, lane in enumerate(lanes)
    ]
    after, sums = pl.pallas_call(
        tail_kernel,
        out_shape=(shape(count, 8, LANES), shape(groups, 4, LANES)),
        in_specs=vmem(1) + [ANY],
        out_specs=tuple(vmem(2)),
        compiler_params=params(),
        name="tail",
    )(moved, joined)
    after = lax.ppermute(after, "tm", [(i + 1, i) for i in range(groups - 1)])
    sums = exchange(sums, "tm")
    return pl.pallas_call(
        last_kernel,
        out_shape=(shape(parts * count, 8 * LANES), shape(parts * count, 8 * LANES)),
        in_specs=[SMEM, SMEM] + vmem(9),
        out_specs=tuple(vmem(2)),
        scratch_shapes=[
            pltpu.VMEM((parts * count * 8, LANES), F32),
            pltpu.VMEM((parts * count * 8, LANES), F32),
            pltpu.VMEM((parts, 2 * count, 8, LANES), F32),
        ],
        compiler_params=params(),
        name="last",
    )(place, keep_group, moved, after, sums, taps, own, other, *lanes)


def solution(mesh):
    placed = (P(AXES, None), P(AXES, None), P(AXES, None), P())
    return jax.shard_map(
        local,
        mesh=mesh,
        in_specs=placed,
        out_specs=(P("tm", "chan"), P("tm", "chan")),
        check_vma=False,
    )
```

```python
import functools
import math

import jax
import jax.numpy as jnp
import numpy as np
from jax import lax
from jax.experimental import pallas as pl
from jax.experimental.pallas import tpu as pltpu
from jax.sharding import PartitionSpec as P

RIDGE = 0.25
ROWS = 64
LANES = 128
CHUNK = 16
F32 = jnp.float32
BF16 = jnp.bfloat16
AXES = ("tm", "chan")
VMEM_BYTES = 16 * 1024 * 1024


def params(limit=VMEM_BYTES):
    return pltpu.CompilerParams(vmem_limit_bytes=limit)


def halves(table):
    high = table.astype(np.float32).astype(jnp.bfloat16)
    low = (table - high.astype(np.float64)).astype(np.float32).astype(jnp.bfloat16)
    return high, low


def dft_tables():
    n1 = np.arange(ROWS)
    n2 = np.arange(LANES)
    k1 = np.arange(ROWS)
    k2 = (2 * np.arange(32)[None, :] + np.arange(2)[:, None]).reshape(-1)
    first = 2.0 * np.pi * (n1[:, None] * k1[None, :] % ROWS) / ROWS
    back_rows = np.concatenate([np.cos(first), -np.sin(first)], 1)
    second = 2.0 * np.pi * (k2[:, None] * n2[None, :] % LANES) / LANES
    scale = 1.0 / math.sqrt(ROWS * ROWS)
    cos = (np.cos(second) * scale).reshape(2, 32, LANES)
    sin = (np.sin(second) * scale).reshape(2, 32, LANES)
    from_real = np.concatenate([cos, sin], 2)
    from_imag = np.concatenate([-sin, cos], 2)
    back_lanes = np.stack([from_real, from_imag], 1).reshape(LANES, 2 * LANES)
    rows_high, rows_low = halves(back_rows)
    lanes_high, lanes_low = halves(back_lanes)
    twist = 2.0 * np.pi * k1[:, None] * n2[None, :] / (ROWS * LANES)
    return (
        np.concatenate([rows_high.T, rows_high.T, rows_low.T], 1),
        np.concatenate([lanes_high.T, lanes_low.T], 1),
        np.concatenate([lanes_high, lanes_high, lanes_low], 0),
        np.block([[rows_high, rows_high], [rows_low, np.zeros_like(rows_low)]]),
        np.stack([np.cos(twist), np.sin(twist)]).astype(np.float32),
    )


def split(value):
    high = value.astype(BF16)
    low = (value - high.astype(F32)).astype(BF16)
    return high, low


def dot(left, right):
    return jnp.dot(left, right, preferred_element_type=F32)


def forward_chunk(frames, ahead_rows, ahead_lanes, cos, sin):
    high, low = split(jnp.concatenate(frames, 1))
    mixed = dot(ahead_rows, jnp.concatenate([high, low, high], 0))
    turned = []
    for f in range(len(frames)):
        real = mixed[:ROWS, f * LANES : (f + 1) * LANES]
        imag = mixed[ROWS:, f * LANES : (f + 1) * LANES]
        turned.append(jnp.concatenate([real * cos + imag * sin, imag * cos - real * sin], 1))
    high, low = split(jnp.concatenate(turned, 0))
    wide = dot(high, ahead_lanes)
    return wide[:, :LANES] + wide[:, LANES:] + dot(low, ahead_lanes[:, :LANES])


def backward_chunk(spectra, back_lanes, back_rows, cos, sin):
    high, low = split(spectra)
    mixed = dot(jnp.concatenate([high, low, high], 1), back_lanes)
    turned = []
    for f in range(spectra.shape[0] // ROWS):
        real = mixed[f * ROWS : (f + 1) * ROWS, :LANES]
        imag = mixed[f * ROWS : (f + 1) * ROWS, LANES:]
        turned.append(jnp.concatenate([real * cos - imag * sin, real * sin + imag * cos], 0))
    high, low = split(jnp.concatenate(turned, 1))
    tall = dot(back_rows, jnp.concatenate([high, low], 0))
    return tall[:ROWS] + tall[ROWS:]


def turn_pair(block):
    flipped = block.T
    low_half = flipped[:ROWS]
    high_half = flipped[ROWS:]
    left = lax.broadcasted_iota(jnp.int32, (ROWS, LANES), 1) < ROWS
    return (
        jnp.where(left, low_half, pltpu.roll(high_half, ROWS, 1)),
        jnp.where(left, pltpu.roll(low_half, ROWS, 1), high_half),
    )


def seed_kernel(*refs):
    sources, out_ref, places, held, semaphore = refs[:6], refs[6], refs[7:13], refs[13], refs[14]
    copies = [
        pltpu.make_async_copy(source, place, semaphore.at[at])
        for at, (source, place) in enumerate(zip(sources, places))
    ]
    for copy in copies:
        copy.start()
    real_ref, imag_ref, weights_ref, back_lanes_ref, back_rows_ref, twist_ref = places
    count = real_ref.shape[0]
    for copy in copies:
        copy.wait()
    for j in range(32):
        columns = slice(j * LANES, (j + 1) * LANES)
        weights = weights_ref[:, columns]
        held[pl.ds(j, count, stride=ROWS), :] = weights * real_ref[:, columns]
        held[pl.ds(32 + j, count, stride=ROWS), :] = weights * imag_ref[:, columns]
    cos = twist_ref[0]
    sin = twist_ref[1]
    for start in range(0, count, CHUNK):
        spectra = []
        for f in range(start, start + CHUNK, 2):
            spectra += turn_pair(held[f * ROWS : (f + 2) * ROWS, :])
        frames = backward_chunk(
            jnp.concatenate(spectra, 0), back_lanes_ref[...], back_rows_ref[...], cos, sin
        )
        for f in range(CHUNK):
            out_ref[start + f] = frames[:, f * LANES : (f + 1) * LANES]


def arrange_kernel(weights_ref, taps_ref, weights_out, taps_out, held):
    count = weights_ref.shape[0]
    for j in range(32):
        weights = weights_ref[:, j * LANES : (j + 1) * LANES]
        held[pl.ds(j, count, stride=ROWS), :] = weights
        held[pl.ds(32 + j, count, stride=ROWS), :] = weights
    for f in range(0, count, 2):
        first, second = turn_pair(held[f * ROWS : (f + 2) * ROWS, :])
        weights_out[f] = first
        weights_out[f + 1] = second
    for n1 in range(ROWS):
        taps_out[pl.ds(n1, taps_ref.shape[0], stride=ROWS), :] = taps_ref[
            :, n1 * LANES : (n1 + 1) * LANES
        ]


def weighted_sum(taps, values):
    total = taps[0] * values[0]
    for tap, value in zip(taps[1:], values[1:]):
        total = total + tap * value
    return total


def back_filter(rows, taps, inside_ref, here_ref, across_ref, keep):
    reach = len(taps) - 1
    count = here_ref.shape[0]
    odd = jnp.full((8, LANES), keep[2]) > 0.5
    frames = [
        jnp.where(odd, inside_ref[t, rows, :], across_ref[t, rows, :]) for t in range(count - reach, count)
    ]
    frames += [here_ref[t, rows, :] for t in range(count)]
    frames += [
        jnp.where(odd, across_ref[t, rows, :], inside_ref[t, rows, :]) * keep[1] for t in range(reach)
    ]
    result = []
    for at in range(reach + count):
        total = weighted_sum(taps, frames[at : at + reach + 1])
        result.append(total * keep[0] if at < reach else total)
    return result


def ahead_filter(taps, frames):
    reach = len(taps) - 1
    return [
        weighted_sum(taps, [frames[at + reach - tap] for tap in range(reach + 1)])
        for at in range(len(frames) - reach)
    ]


def first_kernel(
    keep_ref, inside_ref, here_ref, across_ref, taps_ref, weights_ref,
    ahead_rows_ref, ahead_lanes_ref, back_lanes_ref, back_rows_ref, twist_ref,
    out_ref, side_ref, filtered,
):
    count = here_ref.shape[0]
    keep = (keep_ref[0], keep_ref[1], keep_ref[2])

    @pl.loop(0, ROWS // 8)
    def _(group):
        rows = pl.ds(pl.multiple_of(group * 8, 8), 8)
        taps = [taps_ref[p, rows, :] for p in range(taps_ref.shape[0])]
        side = back_filter(rows, taps, inside_ref, here_ref, across_ref, keep)
        for at, value in enumerate(side):
            side_ref[at, rows, :] = value
        for at, value in enumerate(ahead_filter(taps, side)):
            filtered[at, rows, :] = value

    cos = twist_ref[0]
    sin = twist_ref[1]
    for start in range(0, count, CHUNK):
        spectra = forward_chunk(
            [filtered[start + f] for f in range(CHUNK)], ahead_rows_ref[...], ahead_lanes_ref[...], cos, sin
        )
        weights = weights_ref[start : start + CHUNK].reshape(CHUNK * ROWS, LANES)
        frames = backward_chunk(spectra * weights, back_lanes_ref[...], back_rows_ref[...], cos, sin)
        for f in range(CHUNK):
            out_ref[start + f] = frames[:, f * LANES : (f + 1) * LANES]


def quarters(rows):
    return lax.broadcasted_iota(jnp.int32, (rows, LANES), 1) // 32


def pack(values):
    packed = jnp.zeros((8, LANES), F32)
    for at, value in enumerate(values):
        value = value + pltpu.roll(value, 64, 1)
        value = value + pltpu.roll(value, 32, 1)
        packed = jnp.where(quarters(8) == at, value, packed)
    return packed


def second_kernel(
    place_ref, keep_ref, inside_ref, here_ref, across_ref, side_ref, taps_ref, weights_ref,
    ahead_rows_ref, ahead_lanes_ref, back_lanes_ref, back_rows_ref, twist_ref,
    out_ref, *rest,
):
    own_ref, other_ref, filtered, sums, staged = rest
    count = here_ref.shape[0]
    keep = (keep_ref[0], keep_ref[1], keep_ref[2])
    reach = taps_ref.shape[0] - 1
    sums[...] = jnp.zeros_like(sums)

    @pl.loop(0, ROWS // 8)
    def _(group):
        rows = pl.ds(pl.multiple_of(group * 8, 8), 8)
        taps = [taps_ref[p, rows, :] for p in range(reach + 1)]
        image = back_filter(rows, taps, inside_ref, here_ref, across_ref, keep)
        side = [side_ref[at, rows, :] for at in range(reach + count)]
        image = [value + RIDGE * base for value, base in zip(image, side)]
        for at, value in enumerate(ahead_filter(taps, image)):
            filtered[at, rows, :] = value
        first, second, third = sums[0], sums[1], sums[2]
        for at in range(count):
            base = side[reach + at]
            value = image[reach + at]
            staged[group ^ place_ref[0], at] = base
            staged[group ^ place_ref[0], count + at] = value
            first = first + base * base
            second = second + base * value
            third = third + value * value
        sums[0] = first
        sums[1] = second
        sums[2] = third

    for e in range(4):
        own_ref[e] = staged[2 * e]
        other_ref[e] = staged[2 * e + 1]
    cos = twist_ref[0]
    sin = twist_ref[1]
    power = jnp.zeros((8, LANES), F32)
    for start in range(0, count, CHUNK):
        spectra = forward_chunk(
            [filtered[start + f] for f in range(CHUNK)], ahead_rows_ref[...], ahead_lanes_ref[...], cos, sin
        )
        weights = weights_ref[start : start + CHUNK].reshape(CHUNK * ROWS, LANES)
        weighted = spectra * weights
        power = power + jnp.sum((weighted * spectra).reshape(CHUNK * ROWS // 8, 8, LANES), 0)
        frames = backward_chunk(weighted, back_lanes_ref[...], back_rows_ref[...], cos, sin)
        for f in range(CHUNK):
            for group in range(ROWS // 8):
                out_ref[group, start + f] = frames[
                    group * 8 : (group + 1) * 8, f * LANES : (f + 1) * LANES
                ]
    totals = pack([sums[0], sums[1], sums[2], power])
    for group in range(ROWS // 8):
        out_ref[group, count] = totals


def join_kernel(own_ref, other_ref, *outputs):
    slots = own_ref.shape[1]
    for e, output in enumerate(outputs):
        output[:slots] = own_ref[e + 1]
        output[slots:] = other_ref[e + 1]


def tail_kernel(moved_ref, _, frames_ref, sums_ref):
    count = frames_ref.shape[0]
    frames_ref[...] = moved_ref[0, :count]
    total = moved_ref[0, count]
    for part in range(1, moved_ref.shape[0]):
        total = total + moved_ref[part, count]
    sums_ref[...] = jnp.broadcast_to((total[:4] + total[4:])[None], sums_ref.shape)


def last_kernel(place_ref, keep_ref, moved_ref, after_ref, sums_ref, taps_ref, *rest):
    own_ref, other_ref, *lanes = rest[:5]
    *outputs, kept, left, pairs, kept_rows, left_rows, semaphore = rest[5:]
    parts, count = moved_ref.shape[0], moved_ref.shape[1] - 1
    reach = taps_ref.shape[0] - 1
    rows = pl.ds(pl.multiple_of(place_ref[0] * 8, 8), 8)
    pairs[place_ref[0]] = own_ref[0]
    pairs[place_ref[0] ^ 1] = other_ref[0]
    for e, lane in enumerate(lanes):
        pairs[place_ref[0] ^ (2 * e + 2)] = lane[: 2 * count]
        pairs[place_ref[0] ^ (2 * e + 3)] = lane[2 * count :]
    sums = jnp.sum(sums_ref[...], 0)
    norm, curve, square, power = (
        jnp.sum(jnp.sum(jnp.where(quarters(4) == at, sums, 0.0), 1, keepdims=True), 0, keepdims=True)
        for at in range(4)
    )
    cube = power + RIDGE * square
    step = norm / curve
    next_norm = step * step * square - norm
    grown = step * square / curve
    next_step = next_norm / (step * (step * cube - grown * square))
    to_base = step + next_step * grown
    to_image = -(next_step * step)
    image_rate = -(step + next_step * grown)
    cube_rate = next_step * step
    to_base, to_image, image_rate, cube_rate = (
        jnp.broadcast_to(value, (8, LANES)) for value in (to_base, to_image, image_rate, cube_rate)
    )
    taps = [taps_ref[p, rows, :] for p in range(reach + 1)]

    def finish(part, tail):
        frames = [moved_ref[part, t] for t in range(count)] + tail
        for at in range(count):
            base = pairs[part, at]
            image = pairs[part, count + at]
            again = weighted_sum(taps, frames[at : at + reach + 1]) + RIDGE * image
            here = slice(at * 8, (at + 1) * 8)
            kept[here, :] = to_base * base + to_image * image
            left[here, :] = base + image_rate * image + cube_rate * again
        for block in range(count // 8):
            ready = pl.ds(pl.multiple_of(part * count + block * 8, 8), 8)
            for n1 in range(8):
                places = pl.ds(block * 64 + n1, 8, stride=8)
                columns = slice(n1 * LANES, (n1 + 1) * LANES)
                kept_rows[ready, columns] = kept[places, :]
                left_rows[ready, columns] = left[places, :]
        for copy in copies(part):
            copy.start()

    def copies(part):
        ready = pl.ds(pl.multiple_of(part * count, 8), count)
        return [
            pltpu.make_async_copy(held.at[ready], output.at[ready], semaphore.at[which, part])
            for which, (held, output) in enumerate(zip((kept_rows, left_rows), outputs))
        ]

    @pl.loop(0, parts - 1)
    def _(part):
        finish(part, [moved_ref[part + 1, t] for t in range(reach)])

    finish(parts - 1, [after_ref[t] * keep_ref[0] for t in range(reach)])
    for part in range(parts):
        for copy in copies(part):
            copy.wait()


def shape(*dims):
    return jax.ShapeDtypeStruct(dims, F32)


def vmem(number):
    return [pl.BlockSpec(memory_space=pltpu.VMEM)] * number


SMEM = pl.BlockSpec(memory_space=pltpu.SMEM)
ANY = pl.BlockSpec(memory_space=pl.ANY)


def local(observed_real, observed_imag, weights, taps):
    ahead_rows, ahead_lanes, back_lanes, back_rows, twist = dft_tables()
    count = weights.shape[0]
    reach = taps.shape[0] - 1
    parts = lax.axis_size("chan")
    devices = lax.axis_size("tm") * parts
    blocks = shape(count, ROWS, LANES)
    groups = lax.axis_size("tm")
    position = lax.axis_index(AXES)
    keep = jnp.stack([position > 0, position < devices - 1, position % 2 == 1]).astype(F32)
    place = lax.axis_index("chan").astype(jnp.int32).reshape(1)
    keep_group = (lax.axis_index("tm") < groups - 1).astype(F32).reshape(1)
    tables = (ahead_rows, ahead_lanes, back_lanes, back_rows, twist)

    def neighbours(block):
        inside = [(i, i ^ 1) for i in range(devices)]
        across = [(i, min(max(((i + 1) ^ 1) - 1, 0), devices - 1)) for i in range(devices)]
        return lax.ppermute(block, AXES, inside), lax.ppermute(block, AXES, across)

    def exchange(value, axis):
        return lax.all_to_all(value, axis, split_axis=0, concat_axis=0, tiled=True)

    seed_inputs = (observed_real, observed_imag, weights, back_lanes, back_rows, twist)
    seed_inputs = tuple(pltpu.with_memory_space_constraint(v, pltpu.HBM) for v in seed_inputs)
    seeds = pl.pallas_call(
        seed_kernel,
        out_shape=blocks,
        in_specs=[pl.BlockSpec(memory_space=pltpu.HBM)] * 6,
        out_specs=vmem(1)[0],
        scratch_shapes=[pltpu.VMEM(value.shape, value.dtype) for value in seed_inputs]
        + [pltpu.VMEM((count * ROWS, LANES), F32), pltpu.SemaphoreType.DMA((6,))],
        compiler_params=params(),
        name="seed",
    )(*seed_inputs)
    inside, across = neighbours(seeds)
    weights, taps = pl.pallas_call(
        arrange_kernel,
        out_shape=(blocks, shape((reach + 1) * ROWS, LANES)),
        in_specs=vmem(2),
        out_specs=tuple(vmem(2)),
        scratch_shapes=[pltpu.VMEM((count * ROWS, LANES), F32)],
        compiler_params=params(),
        cost_estimate=pl.CostEstimate(flops=10**7, bytes_accessed=2 * 10**6, transcendentals=0),
        name="arrange",
    )(weights, taps)
    taps = taps.reshape(reach + 1, ROWS, LANES)

    images, side = pl.pallas_call(
        first_kernel,
        out_shape=(blocks, shape(reach + count, ROWS, LANES)),
        in_specs=[SMEM] + vmem(10),
        out_specs=tuple(vmem(2)),
        scratch_shapes=[pltpu.VMEM((count, ROWS, LANES), F32)],
        compiler_params=params(),
        name="first",
    )(keep, inside, seeds, across, taps, weights, *tables)
    inside, across = neighbours(images)

    outgoing, own, other = pl.pallas_call(
        second_kernel,
        out_shape=(shape(parts, count + 1, 8, LANES),) + (shape(4, 2 * count, 8, LANES),) * 2,
        in_specs=[SMEM, SMEM] + vmem(11),
        out_specs=tuple(vmem(3)),
        scratch_shapes=[
            pltpu.VMEM((count, ROWS, LANES), F32),
            pltpu.VMEM((3, 8, LANES), F32),
            pltpu.VMEM((parts, 2 * count, 8, LANES), F32),
        ],
        compiler_params=params(),
        name="second",
    )(place, keep, inside, images, across, side, taps, weights, *tables)

    moved = exchange(outgoing, "chan")
    other = lax.ppermute(other, AXES, [(i, i ^ 1) for i in range(devices)])
    moved, own, other = lax.optimization_barrier((moved, own, other))
    lanes = pl.pallas_call(
        join_kernel,
        out_shape=(shape(4 * count, 8, LANES),) * 3,
        in_specs=vmem(2),
        out_specs=tuple(vmem(3)),
        compiler_params=params(),
        name="join",
    )(own, other)
    joined = lanes[0]
    lanes = [
        lax.ppermute(lane, AXES, [(i, i ^ (2 * e + 2)) for i in range(devices)])
        for e, lane in enumerate(lanes)
    ]
    after, sums = pl.pallas_call(
        tail_kernel,
        out_shape=(shape(count, 8, LANES), shape(groups, 4, LANES)),
        in_specs=vmem(1) + [ANY],
        out_specs=tuple(vmem(2)),
        compiler_params=params(),
        name="tail",
    )(moved, joined)
    after = lax.ppermute(after, "tm", [(i + 1, i) for i in range(groups - 1)])
    sums = exchange(sums, "tm")
    return pl.pallas_call(
        last_kernel,
        out_shape=(shape(parts * count, 8 * LANES), shape(parts * count, 8 * LANES)),
        in_specs=[SMEM, SMEM] + vmem(9),
        out_specs=(pl.BlockSpec(memory_space=pltpu.HBM),) * 2,
        scratch_shapes=[
            pltpu.VMEM((count * 8, LANES), F32),
            pltpu.VMEM((count * 8, LANES), F32),
            pltpu.VMEM((parts, 2 * count, 8, LANES), F32),
            pltpu.VMEM((parts * count, 8 * LANES), F32),
            pltpu.VMEM((parts * count, 8 * LANES), F32),
            pltpu.SemaphoreType.DMA((2, parts)),
        ],
        compiler_params=params(),
        name="last",
    )(place, keep_group, moved, after, sums, taps, own, other, *lanes)


def solution(mesh):
    placed = (P(AXES, None), P(AXES, None), P(AXES, None), P())
    return jax.shard_map(
        local,
        mesh=mesh,
        in_specs=placed,
        out_specs=(P("tm", "chan"), P("tm", "chan")),
        check_vma=False,
    )
```
